32 devices in a mesh: ctx: 8 (over z, y), fsdp: 4 (over x, core).
Axes of the slice: x: 2, y: 2, z: 4, core: 2. Of those that a mesh axis runs over, the one named last changes fastest.
Arguments:
- tokens: bfloat16 [4, 2048, 768], P('fsdp', 'ctx'), may hold values from -6 to 6
- cotangent: bfloat16 [4, 2048, 768], P('fsdp', 'ctx'), may hold values from -6 to 6
- lengths: int32 [4, 4], P('fsdp'), may hold values from 1 to 1840, as said below
- piece_order: int32 [4, 16], P('fsdp'), may hold values from 0 to 15, each once within a row
- routes: int32 [4, 2048, 2], P('fsdp', 'ctx'), may hold values from 0 to 15, all different within a row; in each aligned block of 256 rows (0 to 255, 256 to 511, ..., all dimensions but the last counted through in order) at most 64 rows name the same one
- attn_in: bfloat16 [2, 768, 2304], P(None, 'fsdp'), may hold values from -0.21875 to 0.21875
- attn_out: bfloat16 [2, 768, 768], P(None, 'fsdp'), may hold values from -3.5 to 3.5
- norm_gain: bfloat16 [2, 2, 768], P(None, None, 'fsdp'), may hold values from 0.5 to 1.5
- mlp_in: bfloat16 [2, 768, 4096], P(None, 'fsdp'), may hold values from -0.21875 to 0.21875
- mlp_out: bfloat16 [2, 2048, 768], P(None, 'fsdp'), may hold values from -0.125 to 0.125
- router: bfloat16 [768, 16], P('fsdp'), may hold values from -0.14941406 to 0.14941406
- expert_in: bfloat16 [2, 32768, 768], P(None, 'ctx', 'fsdp'), may hold values from -0.21875 to 0.21875
- expert_out: bfloat16 [32768, 768], P('ctx', 'fsdp'), may hold values from -0.5 to 0.5
Outputs:
- output: float32 [4, 2048, 768], P('fsdp', 'ctx')
- tokens_grad: float32 [4, 2048, 768], P('fsdp', 'ctx')
- attn_in_grad: float32 [2, 768, 2304], P(None, 'fsdp')
- attn_out_grad: float32 [2, 768, 768], P(None, 'fsdp')
- norm_gain_grad: float32 [2, 2, 768], P(None, None, 'fsdp')
- mlp_in_grad: float32 [2, 768, 4096], P(None, 'fsdp')
- mlp_out_grad: float32 [2, 2048, 768], P(None, 'fsdp')
- router_grad: float32 [768, 16], P('fsdp')
- expert_in_grad: float32 [2, 32768, 768], P(None, 'ctx', 'fsdp')
- expert_out_grad: float32 [32768, 768], P('ctx', 'fsdp')
The draws below stay inside these ranges and needn't reach their ends.
Inputs may be any that keep to these rules, and one draw needn't show every extreme that they name: `lengths`: each row sums to 1843; its largest length is 1840 and its smallest 1. `piece_order`: each row names every piece once. `routes`: a token's two experts differ; among the 256 slots of one device no expert is named more than 64 times, and that bound is reached.
All inputs are finite; a program needn't handle non-finite values.
Results may differ from the reference program's by a relative error of at most 0.028.
Values may be sent and summed in bfloat16 or wider, within the bound.
No kernel may reach another device: no remote copies, remote signals or barrier semaphores. Data moves between devices by JAX's collectives and lax.ppermute only.
A program may use at most 320 MiB of HBM per device.

```python
import math
import jax
import jax.numpy as jnp
import numpy as np
from jax import lax

D = 768
HEADS = 12
HD = 64
FF = 2048
EXPERTS = 16
TOP = 2
NSEQ = 4
TOK_DEV = 256
NPIECE = 16
SLOTS = 2048
GROUPS = 4
FILLED = 1843
MOST = 1840
LEAST = 1
CAP = 64
N_CTX = 8


def draw_lengths(key, part):
    extra = FILLED - MOST - (NSEQ - 1) * LEAST

    def one_row(row_key):
        cut_key, perm_key = jax.random.split(row_key)
        cuts = jnp.sort(jax.random.randint(cut_key, (NSEQ - 3,), 0, extra + 1))
        bounds = jnp.concatenate([jnp.zeros((1,), jnp.int32), cuts.astype(jnp.int32), jnp.full((1,), extra, jnp.int32)])
        pieces = bounds[1:] - bounds[:-1]
        values = jnp.concatenate([jnp.full((1,), MOST, jnp.int32), jnp.full((1,), LEAST, jnp.int32), LEAST + pieces])
        return values[jax.random.permutation(perm_key, NSEQ)]
    return jax.vmap(one_row)(jax.random.split(key, GROUPS)).astype(jnp.int32)


def shard_levels(key, extent, shards, smallest, largest):
    def one(dim, blocks):
        heights = jax.random.uniform(jax.random.fold_in(jax.random.fold_in(key, 6), dim), (blocks,), jnp.float32, smallest / len(shards), largest / len(shards))
        return jnp.repeat(jnp.exp(heights), extent[dim] // blocks).reshape((-1,) + (1,) * (len(extent) - dim - 1))

    loudness = one(*shards[0])
    for cut in shards[1:]:
        loudness = loudness * one(*cut)
    return loudness


def routed_block(key, own, number, rows, count, top, limit, skew):
    order = jax.random.permutation(key, count)
    heavy_load, common = load_shares(count, rows * top, limit, skew, True), load_shares(count, rows * top, limit, skew, False)
    places = jnp.arange(count)

    def named(sizes, offset_by):
        used = int((sizes > 0).sum())
        fixed = max(1, used // 4)
        shifted = fixed + (places - fixed + offset_by * (used - fixed)) % max(1, count - fixed)
        return jnp.zeros((count,), jnp.int32).at[order[jnp.where(places < fixed, places, shifted)]].set(jnp.asarray(sizes, jnp.int32))

    sizes = jnp.where(number % 4 == 0, named(heavy_load, number // 4), named(common, number - number // 4 - 1))
    mixed = jax.random.permutation(jax.random.fold_in(own, 3), count)
    donor, sink = mixed[0:count // 2 * 2:2], mixed[1:count // 2 * 2:2]
    room = jnp.minimum(sizes[donor] - 1, limit - sizes[sink]) // 2
    room = jnp.where((donor == order[0]) | (sink == order[0]) | (sizes[sink] == 0), 0, jnp.maximum(room, 0))
    shifted = jax.random.randint(jax.random.fold_in(own, 4), (count // 2,), 0, 1 << 20) % (room + 1)
    sizes = sizes.at[donor].add(-shifted).at[sink].add(shifted)
    items = jnp.searchsorted(jnp.cumsum(sizes), jnp.arange(rows * top), side="right").astype(jnp.int32)
    listing = items.reshape(top, rows).T
    listing = listing[jax.random.permutation(jax.random.fold_in(own, 1), rows)]
    offset_by = jax.random.randint(jax.random.fold_in(own, 2), (rows, 1), 0, top)
    return jnp.take_along_axis(listing, (jnp.arange(top)[None, :] + offset_by) % top, axis=1)


def load_shares(number_of, total, limit, lean, full):
    weights = [(1 << 20) // math.isqrt(standing ** lean) + 1 for standing in range(1, number_of + 1)]
    largest = limit if full else min(limit, max(-(-total // number_of), total * weights[0] // sum(weights)))
    least = 1 if total - largest >= number_of - 1 else 0
    counts, rest = [largest] + [least] * (number_of - 1), total - largest - least * (number_of - 1)
    while rest > 0:
        free = [i for i in range(1, number_of) if counts[i] < largest] or [i for i in range(1, number_of) if counts[i] < limit]
        whole, left = sum([weights[i] for i in free]), rest
        for i in free:
            more = min(limit - counts[i], max(1, left * weights[i] // whole), rest)
            counts[i] = counts[i] + more
            rest = rest - more
    return np.array(counts)


def centred(key, dims, width, most, cuts=(), kind=jnp.bfloat16):
    drawn = width * jax.random.normal(key, dims, jnp.float32)
    if cuts:
        drawn = drawn * shard_levels(key, dims, cuts, -0.22, 0.18)
    return jnp.clip(drawn, -most, most).astype(kind)


def setup_inputs(seed: int = 0) -> dict:
    seeds = jax.random.split(jax.random.key(seed), 14)
    tokens = centred(seeds[0], (GROUPS, SLOTS, D), 1.0, 6.0, ((0, 4), (1, 8)))
    cotangent = centred(seeds[1], (GROUPS, SLOTS, D), 1.0, 6.0, ((0, 4), (1, 8)))
    lengths = draw_lengths(jax.random.fold_in(seeds[13], 71), 0)
    piece_order = jax.vmap(lambda own: jax.random.permutation(own, NPIECE))(jax.random.split(seeds[3], GROUPS)).reshape((GROUPS, NPIECE)).astype(jnp.int32)
    routes_keys = jax.random.split(jax.random.fold_in(seeds[4], 1), GROUPS * SLOTS // TOK_DEV)
    routes_turns = jax.random.permutation(jax.random.fold_in(seeds[4], 3), GROUPS * SLOTS // TOK_DEV)
    routes = jax.vmap(lambda own, number: routed_block(jax.random.fold_in(seeds[4], 2), own, number, TOK_DEV, EXPERTS, TOP, CAP, 1))(routes_keys, routes_turns).reshape((GROUPS, SLOTS, TOP))
    attn_in = centred(seeds[5], (2, D, 3 * D), D ** -0.5, 0.21875, ((1, 4),))
    attn_out = centred(seeds[6], (2, D, D), (max(D // 256, 1)) ** -0.5, 3.5, ((1, 4),))
    norm_gain = jnp.clip(1.0 + 0.1 * jax.random.normal(seeds[7], (2, 2, D), jnp.float32), 0.5, 1.5).astype(jnp.bfloat16)
    mlp_in = centred(seeds[8], (2, D, 2 * FF), D ** -0.5, 0.21875, ((1, 4),))
    mlp_out = centred(seeds[9], (2, FF, D), FF ** -0.5, 0.125, ((1, 4),))
    router = centred(seeds[10], (D, EXPERTS), 0.025, 0.14941406, ((0, 4),))
    expert_in = centred(seeds[11], (2, EXPERTS * FF, D), D ** -0.5, 0.21875, ((1, 8), (2, 4)))
    expert_out = centred(seeds[12], (EXPERTS * FF, D), (FF // 16) ** -0.5, 0.5, ((0, 8), (1, 4)))
    return {"tokens": tokens, "cotangent": cotangent, "lengths": lengths, "piece_order": piece_order, "routes": routes, "attn_in": attn_in, "attn_out": attn_out, "norm_gain": norm_gain, "mlp_in": mlp_in, "mlp_out": mlp_out, "router": router, "expert_in": expert_in, "expert_out": expert_out}


@jax.custom_vjp
def low(v):
    return lax.optimization_barrier(v.astype(jnp.bfloat16)).astype(jnp.float32)

@jax.custom_vjp
def low_back(v):
    return v

def low_keep(v):
    return (low(v), None)

def low_pass(kept, grad):
    return (grad,)

def back_keep(v):
    return (v, None)

def back_low(kept, grad):
    return (low(grad),)
low.defvjp(low_keep, low_pass)
low_back.defvjp(back_keep, back_low)
HIGHEST = lax.Precision.HIGHEST
EPSILON = 1e-06
NEGATIVE = -1e+30

def round_both(values):
    return low(low_back(values))

def layout(lengths_row, order_row, piece_len):
    all_slots = order_row.shape[0] * piece_len
    position = (order_row[:, None] * piece_len + jnp.arange(piece_len, dtype=jnp.int32)[None, :]).reshape(all_slots)
    seq_ends = jnp.cumsum(lengths_row, dtype=jnp.int32)
    segment = lax.optimization_barrier(jnp.sum((position[:, None] >= seq_ends[None, :]).astype(jnp.int32), axis=1, dtype=jnp.int32))
    seq_index = jnp.arange(lengths_row.shape[0], dtype=jnp.int32)
    seq_start = lax.optimization_barrier(jnp.sum(jnp.where(segment[:, None] > seq_index[None, :], lengths_row[None, :], 0), axis=1, dtype=jnp.int32))
    return (position, segment, position - seq_start)

def visible(query_pos, query_seg, key_pos, key_seg, seq_count):
    same_seq = (query_seg[:, None] == key_seg[None, :]) & (query_seg[:, None] < seq_count)
    causal = key_pos[None, :] <= query_pos[:, None]
    return same_seq & causal | (key_pos[None, :] == query_pos[:, None])

def angles(offset, head_dim):
    freq_table = jnp.exp(jnp.arange(head_dim // 2, dtype=jnp.float32) * (-2.0 * math.log(10000.0) / head_dim))
    theta = offset.astype(jnp.float32)[..., None] * freq_table
    return (jnp.cos(theta), jnp.sin(theta))

def rotate(values, cosine, sine_table):
    half_dim = values.shape[-1] // 2
    lead_half = values[..., :half_dim]
    tail_half = values[..., half_dim:]
    return jnp.concatenate([lead_half * cosine - tail_half * sine_table, tail_half * cosine + lead_half * sine_table], axis=-1)

def rms_norm(resid, gain_row):
    return resid * lax.rsqrt(lax.optimization_barrier(jnp.mean(resid * resid, axis=-1, keepdims=True)) + EPSILON) * gain_row

def feed_branch(normed, w_in, w_out):
    mixed_proj = jnp.einsum('...d,df->...f', normed, w_in, precision=HIGHEST)
    gate_pre = low_back(mixed_proj[..., :FF])
    up_pre = low_back(mixed_proj[..., FF:])
    hidden = round_both(jax.nn.silu(gate_pre) * up_pre)
    return jnp.einsum('...f,fd->...d', hidden, w_out, precision=HIGHEST)

def reference(tokens, cotangent, lengths, piece_order, routes, attn_in, attn_out, norm_gain, mlp_in, mlp_out, router, expert_in, expert_out):
    position, segment, offset = jax.vmap(lambda lengths_row, order_row: layout(lengths_row, order_row, TOK_DEV // 2))(lengths, piece_order)
    cosine, sine_table = angles(offset, HD)
    cosine = cosine[:, :, None, :]
    sine_table = sine_table[:, :, None, :]
    query_span = min(512, SLOTS)
    item_routes = routes.reshape(GROUPS, N_CTX, TOK_DEV * TOP)
    chosen = (item_routes[..., None] == jnp.arange(EXPERTS, dtype=jnp.int32)).astype(jnp.int32)
    ranked = jnp.cumsum(chosen, axis=2, dtype=jnp.int32) - chosen
    slot_in = lax.optimization_barrier(jnp.sum(ranked * chosen, axis=-1, dtype=jnp.int32))
    source_block = jnp.arange(GROUPS * N_CTX, dtype=jnp.int32).reshape(GROUPS, N_CTX, 1)
    row_id = (source_block * CAP + slot_in).reshape(GROUPS, SLOTS, TOP).astype(jnp.int32)

    def attend_group(group_items):
        queries, keys_rot, values_rot, group_pos, group_seg = group_items
        query_blocks = queries.reshape(SLOTS // query_span, query_span, HEADS, HD)
        pos_blocks = group_pos.reshape(SLOTS // query_span, query_span)
        seg_blocks = group_seg.reshape(SLOTS // query_span, query_span)

        def one_block(block_items):
            block_query, block_pos, block_seg = block_items
            scores = low_back(jnp.einsum('qhd,khd->hqk', block_query, keys_rot, precision=HIGHEST))
            allowed = visible(block_pos, block_seg, group_pos, group_seg, NSEQ)
            scores = jnp.where(allowed[None], scores, NEGATIVE)
            weights = low(jax.nn.softmax(scores, axis=-1))
            return jnp.einsum('hqk,khd->qhd', weights, values_rot, precision=HIGHEST)
        return lax.map(jax.checkpoint(one_block), (query_blocks, pos_blocks, seg_blocks)).reshape(SLOTS, HEADS, HD)

    def attention(normed, w_in, w_out):
        mixed_proj = low_back(jnp.einsum('gsd,de->gse', normed, w_in, precision=HIGHEST))
        queries = mixed_proj[..., :D].reshape(GROUPS, SLOTS, HEADS, HD)
        keys_raw = mixed_proj[..., D:2 * D].reshape(GROUPS, SLOTS, HEADS, HD)
        values_raw = mixed_proj[..., 2 * D:].reshape(GROUPS, SLOTS, HEADS, HD)
        queries = round_both(rotate(queries, cosine, sine_table) * 0.125)
        keys_rot = round_both(rotate(keys_raw, cosine, sine_table))
        values_rot = round_both(values_raw)
        context = lax.map(attend_group, (queries, keys_rot, values_rot, position, segment))
        attended = round_both(context.reshape(GROUPS, SLOTS, D))
        return low_back(jnp.einsum('gsd,de->gse', attended, w_out, precision=HIGHEST))

    def experts_mix(normed, router_full, experts_in, experts_out):
        logits = jnp.einsum('gsd,de->gse', normed, router_full, precision=HIGHEST)
        gate_probs = jax.nn.softmax(jnp.take_along_axis(logits, routes, axis=-1), axis=-1)
        copies = jnp.stack([low_back(normed) for copy_idx in range(TOP)], axis=2)
        table = jnp.zeros((EXPERTS, GROUPS * N_CTX * CAP, D), jnp.float32).at[routes, row_id].set(copies)
        gate_all = experts_in[0].reshape(EXPERTS, FF, D)
        up_all = experts_in[1].reshape(EXPERTS, FF, D)
        down_all = experts_out.reshape(EXPERTS, FF, D)

        def one_expert(expert_items):
            expert_rows, gate_rows, up_rows, down_rows = expert_items
            w_in = jnp.concatenate([jnp.transpose(gate_rows), jnp.transpose(up_rows)], axis=1)
            return round_both(feed_branch(expert_rows, w_in, down_rows))
        results = lax.map(jax.checkpoint(one_expert), (table, gate_all, up_all, down_all))
        return lax.optimization_barrier(jnp.sum(gate_probs[..., None] * results[routes, row_id], axis=2))

    def forward(resid, attn_in_full, attn_out_full, gains_full, mlp_in_full, mlp_out_full, router_full, expert_in_full, expert_out_full):
        for layer in range(2):
            normed = low(rms_norm(resid, gains_full[layer, 0]))
            resid = resid + attention(normed, attn_in_full[layer], attn_out_full[layer])
            normed = low(rms_norm(resid, gains_full[layer, 1]))
            resid = resid + low_back(feed_branch(normed, mlp_in_full[layer], mlp_out_full[layer]))
            if layer == 1:
                resid = resid + experts_mix(normed, router_full, expert_in_full, expert_out_full)
        return resid
    output, pullback = jax.vjp(forward, tokens.astype(jnp.float32), attn_in.astype(jnp.float32), attn_out.astype(jnp.float32), norm_gain.astype(jnp.float32), mlp_in.astype(jnp.float32), mlp_out.astype(jnp.float32), router.astype(jnp.float32), expert_in.astype(jnp.float32), expert_out.astype(jnp.float32))
    grads = pullback(cotangent.astype(jnp.float32))
    return (output, grads[0], grads[1], grads[2], grads[3], grads[4], grads[5], grads[6], grads[7], grads[8])
```

```python
import math

import jax
import jax.numpy as jnp
from jax import lax
from jax.sharding import PartitionSpec as P

HEADS = 12
HD = 64
FF = 2048
TOP = 2


HIGHEST = lax.Precision.HIGHEST
EPSILON = 1e-06
NEGATIVE = -1e30


def layout(lengths_row, order_row, piece_len):
    all_slots = order_row.shape[0] * piece_len
    position = (
        order_row[:, None] * piece_len + jnp.arange(piece_len, dtype=jnp.int32)[None, :]
    ).reshape(all_slots)
    count = jnp.arange(lengths_row.shape[0], dtype=jnp.int32)
    seq_ends = jnp.sum(
        jnp.where(count[:, None] <= count[None, :], lengths_row[:, None], 0), axis=0, dtype=jnp.int32
    )
    segment = jnp.sum(
        (position[:, None] >= seq_ends[None, :]).astype(jnp.int32), axis=1, dtype=jnp.int32
    )
    seq_index = jnp.arange(lengths_row.shape[0], dtype=jnp.int32)
    seq_start = jnp.sum(
        jnp.where(segment[:, None] > seq_index[None, :], lengths_row[None, :], 0),
        axis=1,
        dtype=jnp.int32,
    )
    return (position, segment, position - seq_start)


def visible(query_pos, query_seg, key_pos, key_seg, seq_count):
    same_seq = (query_seg[:, None] == key_seg[None, :]) & (query_seg[:, None] < seq_count)
    causal = key_pos[None, :] <= query_pos[:, None]
    return same_seq & causal | (key_pos[None, :] == query_pos[:, None])


def angles(offset, head_dim):
    freq_table = jnp.exp(
        jnp.arange(head_dim // 2, dtype=jnp.float32) * (-2.0 * math.log(10000.0) / head_dim)
    )
    theta = offset.astype(jnp.float32)[..., None] * freq_table
    return (jnp.cos(theta), jnp.sin(theta))


def rotate(values, cosine, sine_table):
    half_dim = values.shape[-1] // 2
    lead_half = values[..., :half_dim]
    tail_half = values[..., half_dim:]
    return jnp.concatenate(
        [lead_half * cosine - tail_half * sine_table, tail_half * cosine + lead_half * sine_table],
        axis=-1,
    )


def unrotate(grads, cosine, sine_table):
    half_dim = grads.shape[-1] // 2
    lead_half = grads[..., :half_dim]
    tail_half = grads[..., half_dim:]
    return jnp.concatenate(
        [lead_half * cosine + tail_half * sine_table, tail_half * cosine - lead_half * sine_table],
        axis=-1,
    )


def rounded(values):
    return lax.optimization_barrier(values.astype(jnp.bfloat16)).astype(jnp.float32)


def rms_apply(resid, gain_row):
    inv_rms = lax.rsqrt(jnp.mean(resid * resid, axis=-1, keepdims=True) + EPSILON)
    return (resid * inv_rms * gain_row, inv_rms)


def rms_back(resid, inv_rms, gain_row, grad_normed):
    weighted = grad_normed * gain_row
    grad_resid = inv_rms * weighted - resid * inv_rms**3 * jnp.mean(
        weighted * resid, axis=-1, keepdims=True
    )
    return (grad_resid, jnp.sum(grad_normed * resid * inv_rms, axis=0))


def feed_forward(normed, w_in, w_out):
    mixed_proj = jnp.dot(normed, w_in, preferred_element_type=jnp.float32)
    hidden_width = w_out.shape[0]
    hidden = (jax.nn.silu(mixed_proj[:, :hidden_width]) * mixed_proj[:, hidden_width:]).astype(
        jnp.bfloat16
    )
    return (jnp.dot(hidden, w_out, preferred_element_type=jnp.float32), mixed_proj, hidden)


def feed_back(normed, mixed_proj, hidden, grad_result, w_in, w_out):
    hidden_width = w_out.shape[0]
    grad_wout = jnp.einsum("tf,td->fd", hidden, grad_result, preferred_element_type=jnp.float32)
    grad_hidden = rounded(
        jnp.einsum("td,fd->tf", grad_result, w_out, preferred_element_type=jnp.float32)
    )
    gate_pre = mixed_proj[:, :hidden_width]
    up_pre = mixed_proj[:, hidden_width:]
    sigmoid_gate = jax.nn.sigmoid(gate_pre)
    grad_gate = grad_hidden * up_pre * sigmoid_gate * (1.0 + gate_pre * (1.0 - sigmoid_gate))
    grad_up = grad_hidden * gate_pre * sigmoid_gate
    grad_mixed = jnp.concatenate([grad_gate, grad_up], axis=1).astype(jnp.bfloat16)
    grad_win = jnp.einsum("td,tf->df", normed, grad_mixed, preferred_element_type=jnp.float32)
    grad_normed = jnp.einsum("tf,df->td", grad_mixed, w_in, preferred_element_type=jnp.float32)
    return (grad_normed, grad_win, grad_wout)


def attend_keys(queries, all_keys, all_values, geometry):
    local_pos, local_seg, cosine, sine_table, all_pos, all_seg, seq_count = geometry
    tok_rows = queries.shape[0]
    all_slots = all_keys.shape[0]
    key_span = min(512, all_slots)
    query_heads = queries.reshape(tok_rows, HEADS, HD)

    def advance(carried, block_idx):
        run_max, run_sum, accumulated = carried
        begin_at = block_idx * key_span
        key_block = lax.dynamic_slice_in_dim(all_keys, begin_at, key_span, 0).reshape(
            key_span, HEADS, HD
        )
        value_block = lax.dynamic_slice_in_dim(all_values, begin_at, key_span, 0).reshape(
            key_span, HEADS, HD
        )
        allowed = visible(
            local_pos,
            local_seg,
            lax.dynamic_slice_in_dim(all_pos, begin_at, key_span, 0),
            lax.dynamic_slice_in_dim(all_seg, begin_at, key_span, 0),
            seq_count,
        )[None]
        scores = jnp.where(
            allowed,
            jnp.einsum("thd,khd->htk", query_heads, key_block, preferred_element_type=jnp.float32),
            NEGATIVE,
        )
        new_max = jnp.maximum(run_max, jnp.max(scores, axis=-1))
        weights = jnp.where(allowed, jnp.exp(scores - new_max[..., None]), 0.0)
        factor = jnp.exp(run_max - new_max)
        run_sum = run_sum * factor + jnp.sum(weights, axis=-1)
        accumulated = accumulated * factor[..., None] + jnp.einsum(
            "htk,khd->htd",
            weights.astype(jnp.bfloat16),
            value_block,
            preferred_element_type=jnp.float32,
        )
        return ((new_max, run_sum, accumulated), None)

    start_state = (
        jnp.full((HEADS, tok_rows), NEGATIVE, jnp.float32),
        jnp.zeros((HEADS, tok_rows), jnp.float32),
        jnp.zeros((HEADS, tok_rows, HD), jnp.float32),
    )
    (run_max, run_sum, accumulated), ignored = lax.scan(
        advance, start_state, jnp.arange(all_slots // key_span)
    )
    context = jnp.transpose(accumulated / run_sum[..., None], (1, 0, 2))
    return (context, run_max + jnp.log(run_sum))


def attend_forward(resid, gain_row, w_in, w_out, geometry):
    local_pos, local_seg, cosine, sine_table, all_pos, all_seg, seq_count = geometry
    tok_rows, model_width = resid.shape
    normed, inv_rms = rms_apply(resid, gain_row)
    normed = normed.astype(jnp.bfloat16)
    mixed_proj = jnp.dot(normed, w_in, preferred_element_type=jnp.float32)
    queries = (
        (
            rotate(mixed_proj[:, :model_width].reshape(tok_rows, HEADS, HD), cosine, sine_table)
            * 0.125
        )
        .astype(jnp.bfloat16)
        .reshape(tok_rows, model_width)
    )
    keys_rot = (
        rotate(
            mixed_proj[:, model_width : 2 * model_width].reshape(tok_rows, HEADS, HD),
            cosine,
            sine_table,
        )
        .astype(jnp.bfloat16)
        .reshape(tok_rows, model_width)
    )
    values_rot = mixed_proj[:, 2 * model_width :].astype(jnp.bfloat16)
    all_keys, all_values = (
        lax.all_gather(keys_rot, "ctx", axis=0, tiled=True),
        lax.all_gather(values_rot, "ctx", axis=0, tiled=True),
    )
    context, log_sum = attend_keys(queries, all_keys, all_values, geometry)
    attended = context.reshape(tok_rows, model_width).astype(jnp.bfloat16)
    branch = jnp.dot(attended, w_out, preferred_element_type=jnp.float32)
    kept = (
        resid,
        inv_rms,
        normed,
        queries,
        keys_rot,
        values_rot,
        all_keys,
        all_values,
        context,
        log_sum,
        attended,
    )
    return (resid + branch, kept)


def attend_backward(grad_resid, kept, gain_row, w_in, w_out, geometry):
    (
        resid,
        inv_rms,
        normed,
        queries,
        keys_rot,
        values_rot,
        all_keys,
        all_values,
        context,
        log_sum,
        attended,
    ) = kept
    local_pos, local_seg, cosine, sine_table, all_pos, all_seg, seq_count = geometry
    tok_rows, model_width = resid.shape
    all_slots = all_keys.shape[0]
    key_span = min(512, all_slots)
    block_ids = jnp.arange(all_slots // key_span)
    grad_branch = grad_resid.astype(jnp.bfloat16)
    grad_wout = jnp.einsum("td,te->de", attended, grad_branch, preferred_element_type=jnp.float32)
    grad_attended = jnp.einsum(
        "te,de->td", grad_branch, w_out, preferred_element_type=jnp.float32
    ).astype(jnp.bfloat16)
    grad_heads = grad_attended.reshape(tok_rows, HEADS, HD)
    row_delta = jnp.transpose(jnp.sum(grad_heads.astype(jnp.float32) * context, axis=-1))
    query_heads = queries.reshape(tok_rows, HEADS, HD)
    zero_query = jnp.zeros((HEADS, tok_rows, HD), jnp.float32)

    def key_block_grads(block_idx):
        begin_at = block_idx * key_span
        key_block = lax.dynamic_slice_in_dim(all_keys, begin_at, key_span, 0).reshape(
            key_span, HEADS, HD
        )
        value_block = lax.dynamic_slice_in_dim(all_values, begin_at, key_span, 0).reshape(
            key_span, HEADS, HD
        )
        allowed = visible(
            local_pos,
            local_seg,
            lax.dynamic_slice_in_dim(all_pos, begin_at, key_span, 0),
            lax.dynamic_slice_in_dim(all_seg, begin_at, key_span, 0),
            seq_count,
        )[None]
        scores = jnp.einsum(
            "thd,khd->htk", query_heads, key_block, preferred_element_type=jnp.float32
        )
        prob_block = jnp.where(allowed, jnp.exp(scores - log_sum[..., None]), 0.0)
        grad_probs = jnp.einsum(
            "thd,khd->htk", grad_heads, value_block, preferred_element_type=jnp.float32
        )
        grad_scores = (prob_block * (grad_probs - row_delta[..., None])).astype(jnp.bfloat16)
        return (key_block, prob_block, grad_scores)

    def retreat(grad_query, block_idx):
        key_block, prob_block, grad_scores = key_block_grads(block_idx)
        grad_query = grad_query + jnp.einsum(
            "htk,khd->htd", grad_scores, key_block, preferred_element_type=jnp.float32
        )
        key_part = jnp.einsum(
            "htk,thd->khd", grad_scores, query_heads, preferred_element_type=jnp.float32
        ).reshape(key_span, model_width)
        value_part = jnp.einsum(
            "htk,thd->khd",
            prob_block.astype(jnp.bfloat16),
            grad_heads,
            preferred_element_type=jnp.float32,
        ).reshape(key_span, model_width)
        return (grad_query, (key_part, value_part))

    grad_query, (key_parts, value_parts) = lax.scan(retreat, zero_query, block_ids)
    grad_keys, grad_values = (
        lax.psum_scatter(
            key_parts.reshape(all_slots, model_width), "ctx", scatter_dimension=0, tiled=True
        ),
        lax.psum_scatter(
            value_parts.reshape(all_slots, model_width), "ctx", scatter_dimension=0, tiled=True
        ),
    )
    grad_query = unrotate(rounded(jnp.transpose(grad_query, (1, 0, 2))) * 0.125, cosine, sine_table)
    grad_key_rot = unrotate(rounded(grad_keys.reshape(tok_rows, HEADS, HD)), cosine, sine_table)
    grad_mixed = jnp.concatenate(
        [
            grad_query.reshape(tok_rows, model_width),
            grad_key_rot.reshape(tok_rows, model_width),
            grad_values,
        ],
        axis=1,
    ).astype(jnp.bfloat16)
    grad_win = jnp.einsum("td,te->de", normed, grad_mixed, preferred_element_type=jnp.float32)
    grad_normed = jnp.einsum("te,de->td", grad_mixed, w_in, preferred_element_type=jnp.float32)
    grad_in, grad_gain = rms_back(resid, inv_rms, gain_row, grad_normed)
    return (grad_resid + grad_in, grad_win, grad_wout, grad_gain)


def per_device(
    tokens,
    cotangent,
    lengths,
    piece_order,
    routes,
    attn_in,
    attn_out,
    norm_gain,
    mlp_in,
    mlp_out,
    router,
    expert_in,
    expert_out,
):
    tok_rows = tokens.shape[1]
    model_width = tokens.shape[2]
    seq_count = lengths.shape[1]
    position, segment, offset = layout(lengths[0], piece_order[0], tok_rows // 2)
    first_slot = lax.axis_index("ctx") * tok_rows
    local_pos = lax.dynamic_slice_in_dim(position, first_slot, tok_rows, 0)
    local_seg = lax.dynamic_slice_in_dim(segment, first_slot, tok_rows, 0)
    cosine, sine_table = angles(lax.dynamic_slice_in_dim(offset, first_slot, tok_rows, 0), HD)
    geometry = (
        local_pos,
        local_seg,
        cosine[:, None, :],
        sine_table[:, None, :],
        position,
        segment,
        seq_count,
    )
    dense_set = (
        lax.all_gather(attn_in[0], "fsdp", axis=0, tiled=True),
        lax.all_gather(attn_out[0], "fsdp", axis=0, tiled=True),
        lax.all_gather(mlp_in[0], "fsdp", axis=0, tiled=True),
        lax.all_gather(mlp_out[0], "fsdp", axis=0, tiled=True),
        lax.all_gather(norm_gain[0], "fsdp", axis=1, tiled=True),
    )
    moe_set = (
        lax.all_gather(attn_in[1], "fsdp", axis=0, tiled=True),
        lax.all_gather(attn_out[1], "fsdp", axis=0, tiled=True),
        lax.all_gather(mlp_in[1], "fsdp", axis=0, tiled=True),
        lax.all_gather(mlp_out[1], "fsdp", axis=0, tiled=True),
        lax.all_gather(norm_gain[1], "fsdp", axis=1, tiled=True),
        lax.all_gather(router, "fsdp", axis=0, tiled=True),
        lax.all_gather(expert_in, "fsdp", axis=2, tiled=True),
        lax.all_gather(expert_out, "fsdp", axis=1, tiled=True),
    )
    resid_in = tokens[0].astype(jnp.float32)
    after_one, kept_one = attend_forward(
        resid_in, dense_set[4][0], dense_set[0], dense_set[1], geometry
    )
    normed_two, inv_two = rms_apply(after_one, dense_set[4][1])
    normed_two = normed_two.astype(jnp.bfloat16)
    dense_branch, mixed_two, hidden_two = feed_forward(normed_two, dense_set[2], dense_set[3])
    middle = after_one + dense_branch
    after_two, kept_two = attend_forward(middle, moe_set[4][0], moe_set[0], moe_set[1], geometry)
    normed_three, inv_three = rms_apply(after_two, moe_set[4][1])
    normed_three = normed_three.astype(jnp.bfloat16)
    shared, mixed_three, hidden_three = feed_forward(normed_three, moe_set[2], moe_set[3])
    num_experts = router.shape[1]
    capacity = 2 * tok_rows * TOP // num_experts
    item_count = tok_rows * TOP
    hid_dev = expert_out.shape[0]
    per_slot = min(FF, hid_dev)
    local_count = hid_dev // per_slot
    split_count = FF // per_slot
    ctx_count = lax.axis_size("ctx")
    gate_rows = moe_set[6][0].reshape(local_count, per_slot, model_width)
    up_rows = moe_set[6][1].reshape(local_count, per_slot, model_width)
    down_rows = moe_set[7].reshape(local_count, per_slot, model_width)

    def spread(per_expert):
        return jnp.broadcast_to(
            per_expert[:, None], (num_experts, split_count, capacity, model_width)
        ).reshape(ctx_count, local_count, capacity, model_width)

    def collect(returned_parts):
        return jnp.sum(
            returned_parts.reshape(num_experts, split_count, capacity, model_width), axis=1
        ).reshape(num_experts * capacity, model_width)

    logits = jnp.dot(normed_three, moe_set[5], preferred_element_type=jnp.float32)
    chosen = routes[0][:, :, None] == jnp.arange(num_experts, dtype=jnp.int32)[None, None, :]
    picked = jnp.sum(jnp.where(chosen, logits[:, None, :], 0.0), axis=-1)
    gate_probs = jax.nn.softmax(picked, axis=-1)
    flat_chosen = chosen.reshape(item_count, num_experts).astype(jnp.int32)
    items = jnp.arange(item_count, dtype=jnp.int32)
    earlier = jnp.dot(
        (items[None, :] < items[:, None]).astype(jnp.bfloat16),
        flat_chosen.astype(jnp.bfloat16),
        preferred_element_type=jnp.float32,
    ).astype(jnp.int32)
    slot_rank = jnp.sum(earlier * flat_chosen, axis=1)
    slot_target = routes[0].reshape(item_count) * capacity + slot_rank
    slot_owner = (
        jnp.full((num_experts * capacity,), item_count, jnp.int32)
        .at[slot_target]
        .set(jnp.arange(item_count, dtype=jnp.int32))
    )
    filled = slot_owner < item_count
    padded = jnp.concatenate([normed_three, jnp.zeros((1, model_width), jnp.bfloat16)], axis=0)
    outgoing = spread(
        padded[jnp.where(filled, slot_owner // TOP, tok_rows)].reshape(
            num_experts, capacity, model_width
        )
    )
    arrived_rows = lax.all_to_all(outgoing, "ctx", split_axis=0, concat_axis=0, tiled=True)
    gate_pre = jnp.einsum(
        "sjkd,jfd->sjkf", arrived_rows, gate_rows, preferred_element_type=jnp.float32
    )
    up_pre = jnp.einsum("sjkd,jfd->sjkf", arrived_rows, up_rows, preferred_element_type=jnp.float32)
    hidden_rows = (jax.nn.silu(gate_pre) * up_pre).astype(jnp.bfloat16)
    partial_rows = jnp.einsum(
        "sjkf,jfd->sjkd", hidden_rows, down_rows, preferred_element_type=jnp.float32
    )
    returned = lax.all_to_all(partial_rows, "ctx", split_axis=0, concat_axis=0, tiled=True)
    expert_rows = collect(returned).astype(jnp.bfloat16)
    back_rows = expert_rows[slot_target].reshape(tok_rows, TOP, model_width).astype(jnp.float32)
    mixture = jnp.sum(gate_probs[..., None] * back_rows, axis=1)
    output = after_two + shared + mixture
    grad_out = cotangent[0].astype(jnp.float32)
    grad_gates = jnp.sum(back_rows * grad_out[:, None, :], axis=-1)
    grad_items = (
        (gate_probs[..., None] * grad_out[:, None, :])
        .astype(jnp.bfloat16)
        .reshape(item_count, model_width)
    )
    grad_padded = jnp.concatenate([grad_items, jnp.zeros((1, model_width), jnp.bfloat16)], axis=0)
    grad_outgoing = spread(
        grad_padded[jnp.where(filled, slot_owner, item_count)].reshape(
            num_experts, capacity, model_width
        )
    )
    grad_arrived = lax.all_to_all(grad_outgoing, "ctx", split_axis=0, concat_axis=0, tiled=True)
    hidden_again = (jax.nn.silu(gate_pre) * up_pre).astype(jnp.bfloat16)
    grad_ewout = jnp.einsum(
        "sjkf,sjkd->jfd", hidden_again, grad_arrived, preferred_element_type=jnp.float32
    ).reshape(hid_dev, model_width)
    grad_hidden = rounded(
        jnp.einsum("sjkd,jfd->sjkf", grad_arrived, down_rows, preferred_element_type=jnp.float32)
    )
    sigmoid_gate = jax.nn.sigmoid(gate_pre)
    grad_gate = (
        grad_hidden * up_pre * sigmoid_gate * (1.0 + gate_pre * (1.0 - sigmoid_gate))
    ).astype(jnp.bfloat16)
    grad_up = (grad_hidden * gate_pre * sigmoid_gate).astype(jnp.bfloat16)
    grad_wgate = jnp.einsum(
        "sjkf,sjkd->jfd", grad_gate, arrived_rows, preferred_element_type=jnp.float32
    ).reshape(hid_dev, model_width)
    grad_wup = jnp.einsum(
        "sjkf,sjkd->jfd", grad_up, arrived_rows, preferred_element_type=jnp.float32
    ).reshape(hid_dev, model_width)
    grad_ewin = jnp.stack([grad_wgate, grad_wup])
    grad_rows = jnp.einsum(
        "sjkf,jfd->sjkd", grad_gate, gate_rows, preferred_element_type=jnp.float32
    ) + jnp.einsum("sjkf,jfd->sjkd", grad_up, up_rows, preferred_element_type=jnp.float32)
    grad_back = lax.all_to_all(grad_rows, "ctx", split_axis=0, concat_axis=0, tiled=True)
    grad_copies = rounded(collect(grad_back))[slot_target].reshape(tok_rows, TOP, model_width)
    grad_picked = gate_probs * (
        grad_gates - jnp.sum(gate_probs * grad_gates, axis=-1, keepdims=True)
    )
    grad_logits = jnp.sum(jnp.where(chosen, grad_picked[..., None], 0.0), axis=1)
    router_full = moe_set[5].astype(jnp.float32)
    grad_router = jnp.einsum(
        "td,te->de", normed_three.astype(jnp.float32), grad_logits, precision=HIGHEST
    )
    grad_shared_in, grad_swin, grad_swout = feed_back(
        normed_three,
        mixed_three,
        hidden_three,
        grad_out.astype(jnp.bfloat16),
        moe_set[2],
        moe_set[3],
    )
    grad_normed = (
        grad_shared_in
        + jnp.sum(grad_copies, axis=1)
        + jnp.einsum("te,de->td", grad_logits, router_full, precision=HIGHEST)
    )
    grad_in, grad_gain_three = rms_back(after_two, inv_three, moe_set[4][1], grad_normed)
    grad_resid, grad_win_two, grad_wout_two, grad_gain_two = attend_backward(
        grad_out + grad_in, kept_two, moe_set[4][0], moe_set[0], moe_set[1], geometry
    )
    moe_grads = (
        lax.psum_scatter(grad_win_two, "fsdp", scatter_dimension=0, tiled=True),
        lax.psum_scatter(grad_wout_two, "fsdp", scatter_dimension=0, tiled=True),
        lax.psum_scatter(grad_swin, "fsdp", scatter_dimension=0, tiled=True),
        lax.psum_scatter(grad_swout, "fsdp", scatter_dimension=0, tiled=True),
        lax.psum_scatter(
            jnp.stack([grad_gain_two, grad_gain_three]), "fsdp", scatter_dimension=1, tiled=True
        ),
        lax.psum_scatter(grad_router, "fsdp", scatter_dimension=0, tiled=True),
        lax.psum_scatter(grad_ewin, "fsdp", scatter_dimension=2, tiled=True),
        lax.psum_scatter(grad_ewout, "fsdp", scatter_dimension=1, tiled=True),
    )
    grad_dense_in, grad_dwin, grad_dwout = feed_back(
        normed_two,
        mixed_two,
        hidden_two,
        grad_resid.astype(jnp.bfloat16),
        dense_set[2],
        dense_set[3],
    )
    grad_in_two, grad_gain_dense = rms_back(after_one, inv_two, dense_set[4][1], grad_dense_in)
    grad_resid, grad_win_one, grad_wout_one, grad_gain_one = attend_backward(
        grad_resid + grad_in_two, kept_one, dense_set[4][0], dense_set[0], dense_set[1], geometry
    )
    dense_grads = (
        lax.psum_scatter(grad_win_one, "fsdp", scatter_dimension=0, tiled=True),
        lax.psum_scatter(grad_wout_one, "fsdp", scatter_dimension=0, tiled=True),
        lax.psum_scatter(grad_dwin, "fsdp", scatter_dimension=0, tiled=True),
        lax.psum_scatter(grad_dwout, "fsdp", scatter_dimension=0, tiled=True),
        lax.psum_scatter(
            jnp.stack([grad_gain_one, grad_gain_dense]), "fsdp", scatter_dimension=1, tiled=True
        ),
    )
    summed = lax.psum(
        (
            dense_grads[0],
            dense_grads[1],
            dense_grads[2],
            dense_grads[3],
            dense_grads[4],
            moe_grads[0],
            moe_grads[1],
            moe_grads[2],
            moe_grads[3],
            moe_grads[4],
            moe_grads[5],
        ),
        "ctx",
    )
    return (
        output[None],
        grad_resid[None],
        jnp.stack([summed[0], summed[5]]),
        jnp.stack([summed[1], summed[6]]),
        jnp.stack([summed[4], summed[9]]),
        jnp.stack([summed[2], summed[7]]),
        jnp.stack([summed[3], summed[8]]),
        summed[10],
        moe_grads[6],
        moe_grads[7],
    )


def solution(mesh):
    placed = (
        P("fsdp", "ctx", None),
        P("fsdp", "ctx", None),
        P("fsdp", None),
        P("fsdp", None),
        P("fsdp", "ctx", None),
        P(None, "fsdp", None),
        P(None, "fsdp", None),
        P(None, None, "fsdp"),
        P(None, "fsdp", None),
        P(None, "fsdp", None),
        P("fsdp", None),
        P(None, "ctx", "fsdp"),
        P("ctx", "fsdp"),
    )
    return jax.shard_map(
        per_device,
        mesh=mesh,
        in_specs=placed,
        out_specs=(
            P("fsdp", "ctx", None),
            P("fsdp", "ctx", None),
            P(None, "fsdp", None),
            P(None, "fsdp", None),
            P(None, None, "fsdp"),
            P(None, "fsdp", None),
            P(None, "fsdp", None),
            P("fsdp", None),
            P(None, "ctx", "fsdp"),
            P("ctx", "fsdp"),
        ),
        check_vma=False,
    )
```

```python
import functools
import math

import jax
import jax.numpy as jnp
from jax import lax
from jax.experimental import pallas as pl
from jax.experimental.pallas import tpu as pltpu
from jax.sharding import PartitionSpec as P

HEADS = 12
HD = 64
FF = 2048
TOP = 2
HEAD_GROUPS = 4
KEY_SPAN = 512
VMEM_LIMIT = 60 * 1024 * 1024


HIGHEST = lax.Precision.HIGHEST
EPSILON = 1e-06
NEGATIVE = -1e30


def _mask(first_key, keys, query_pos, query_start, copies):
    key_pos = first_key + lax.broadcasted_iota(jnp.int32, (keys, query_pos.shape[1]), 0)
    allowed = (key_pos <= query_pos) & (key_pos >= query_start)
    return jnp.concatenate([allowed] * copies, axis=1)


def _starts(pos, ends_ref, count):
    start = jnp.zeros_like(pos)
    for k in range(count):
        start = jnp.where(pos >= ends_ref[k], ends_ref[k] if k < count - 1 else pos, start)
    return start


def _query_geometry(place, ends_ref, count, piece, key_span):
    query_pos = place * piece + lax.broadcasted_iota(jnp.int32, (1, piece), 1)
    query_start = _starts(query_pos, ends_ref, count)
    first = place * piece
    least = jnp.int32(0)
    for k in range(count):
        least = jnp.where(first >= ends_ref[k], ends_ref[k] if k < count - 1 else first, least)
    return (
        query_pos,
        query_start,
        least // key_span,
        (first + piece - 1) // key_span + 1,
    )


def _stack_heads(rows, heads):
    head_dim = rows.shape[1] // heads
    lane = lax.broadcasted_iota(jnp.int32, rows.shape, 1) // head_dim
    zero = jnp.zeros_like(rows)
    return jnp.concatenate([jnp.where(lane == h, rows, zero) for h in range(heads)], axis=0)


def _own_heads(acc, heads, piece):
    head_dim = acc.shape[0] // heads
    return jnp.concatenate(
        [
            acc[h * head_dim : (h + 1) * head_dim, h * piece : (h + 1) * piece]
            for h in range(heads)
        ],
        axis=0,
    )


NT = (((1,), (1,)), ((), ()))


def _dot(a, b):
    return jnp.dot(a, b, preferred_element_type=jnp.float32)


def _dot_nt(a, b):
    return lax.dot_general(a, b, NT, preferred_element_type=jnp.float32)


def _forward_kernel(
    heads,
    count,
    key_span,
    place_ref,
    ends_ref,
    own_ref,
    other_ref,
    out_ref,
    keep_ref,
    lse_ref,
    keys,
    values_t,
):
    step = pl.program_id(0)
    members, _, tok, width = own_ref.shape
    piece = tok // 2
    own_pieces = members * 2
    all_pieces = own_pieces * (1 + other_ref.shape[0])

    @pl.when(step == 0)
    def _():
        for s in range(all_pieces):
            part, rest = divmod(s, own_pieces)
            member, half = divmod(rest, 2)
            rows = pl.ds(half * piece, piece)
            if part == 0:
                k_rows, v_rows = own_ref[member, 1, rows, :], own_ref[member, 2, rows, :]
            else:
                k_rows = other_ref[part - 1, member, 0, rows, :]
                v_rows = other_ref[part - 1, member, 1, rows, :]
            at = pl.ds(pl.multiple_of(place_ref[s] * piece, piece), piece)
            keys[at, :] = k_rows
            values_t[:, at] = v_rows.astype(jnp.float32).T.astype(jnp.bfloat16)

    place = place_ref[step]
    query_pos, query_start, begin, end = _query_geometry(place, ends_ref, count, piece, key_span)
    rows = pl.ds(pl.multiple_of((step % 2) * piece, piece), piece)
    stacked = _stack_heads(own_ref[step // 2, 0, rows, :], heads)
    cols = heads * piece

    def advance(block, carried):
        run_max, run_sum, acc = carried
        first = pl.multiple_of(block * key_span, key_span)
        scores = _dot_nt(keys[pl.ds(first, key_span), :], stacked)
        allowed = _mask(first, key_span, query_pos, query_start, heads)
        scores = jnp.where(allowed, scores, NEGATIVE)
        new_max = jnp.maximum(run_max, jnp.max(scores, axis=0, keepdims=True))
        weights = jnp.exp(scores - new_max)
        factor = jnp.exp(run_max - new_max)
        run_sum = run_sum * factor + jnp.sum(weights, axis=0, keepdims=True)
        acc = acc * factor + _dot(values_t[:, pl.ds(first, key_span)], weights.astype(jnp.bfloat16))
        return (new_max, run_sum, acc)

    run_max, run_sum, acc = lax.fori_loop(
        begin,
        end,
        advance,
        (
            jnp.full((1, cols), NEGATIVE, jnp.float32),
            jnp.zeros((1, cols), jnp.float32),
            jnp.zeros((width, cols), jnp.float32),
        ),
    )
    kept = _own_heads(acc / run_sum, heads, piece)
    keep_ref[0] = kept
    out_ref[0] = kept.T.astype(jnp.bfloat16)
    lse_ref[0] = run_max + jnp.log(run_sum)


def _backward_kernel(
    heads,
    count,
    key_span,
    place_ref,
    ends_ref,
    own_ref,
    other_ref,
    grad_ref,
    keep_ref,
    lse_ref,
    gq_ref,
    gown_ref,
    gother_ref,
    keys,
    keys_t,
    values,
    gkeys,
    gvalues,
):
    step = pl.program_id(0)
    members, _, tok, width = own_ref.shape
    piece = tok // 2
    own_pieces = members * 2
    all_pieces = own_pieces * (1 + other_ref.shape[0])

    @pl.when(step == 0)
    def _():
        for s in range(all_pieces):
            part, rest = divmod(s, own_pieces)
            member, half = divmod(rest, 2)
            rows = pl.ds(half * piece, piece)
            if part == 0:
                k_rows, v_rows = own_ref[member, 1, rows, :], own_ref[member, 2, rows, :]
            else:
                k_rows = other_ref[part - 1, member, 0, rows, :]
                v_rows = other_ref[part - 1, member, 1, rows, :]
            at = pl.ds(pl.multiple_of(place_ref[s] * piece, piece), piece)
            keys[at, :] = k_rows
            keys_t[:, at] = k_rows.astype(jnp.float32).T.astype(jnp.bfloat16)
            values[at, :] = v_rows
        gkeys[...] = jnp.zeros_like(gkeys)
        gvalues[...] = jnp.zeros_like(gvalues)

    place = place_ref[step]
    query_pos, query_start, begin, end = _query_geometry(place, ends_ref, count, piece, key_span)
    rows = pl.ds(pl.multiple_of((step % 2) * piece, piece), piece)
    stacked = _stack_heads(own_ref[step // 2, 0, rows, :], heads)
    grad = grad_ref[step // 2, rows, :]
    grad_stacked = _stack_heads(grad, heads)
    product = grad.astype(jnp.float32).T * keep_ref[0]
    head_dim = width // heads
    delta = jnp.concatenate(
        [
            jnp.sum(product[h * head_dim : (h + 1) * head_dim, :], axis=0, keepdims=True)
            for h in range(heads)
        ],
        axis=1,
    )
    lse = lse_ref[0]

    def retreat(block, acc):
        first = pl.multiple_of(block * key_span, key_span)
        at = pl.ds(first, key_span)
        scores = _dot_nt(keys[at, :], stacked)
        allowed = _mask(first, key_span, query_pos, query_start, heads)
        probs = jnp.where(allowed, jnp.exp(scores - lse), 0.0)
        grad_probs = _dot_nt(values[at, :], grad_stacked)
        grad_scores = (probs * (grad_probs - delta)).astype(jnp.bfloat16)
        gvalues[at, :] += _dot(probs.astype(jnp.bfloat16), grad_stacked)
        gkeys[at, :] += _dot(grad_scores, stacked)
        return acc + _dot(keys_t[:, at], grad_scores)

    acc = lax.fori_loop(
        begin, end, retreat, jnp.zeros((width, heads * piece), jnp.float32)
    )
    gq_ref[0] = _own_heads(acc, heads, piece).T.astype(jnp.bfloat16)

    @pl.when(step == pl.num_programs(0) - 1)
    def _():
        for s in range(all_pieces):
            part, rest = divmod(s, own_pieces)
            member, half = divmod(rest, 2)
            rows = pl.ds(half * piece, piece)
            at = pl.ds(pl.multiple_of(place_ref[s] * piece, piece), piece)
            if part == 0:
                gown_ref[member, 0, rows, :] = gkeys[at, :]
                gown_ref[member, 1, rows, :] = gvalues[at, :]
            else:
                gother_ref[part - 1, member, 0, rows, :] = gkeys[at, :].astype(jnp.bfloat16)
                gother_ref[part - 1, member, 1, rows, :] = gvalues[at, :].astype(jnp.bfloat16)


def _whole(shape):
    return pl.BlockSpec(shape, lambda i, *_: (0,) * len(shape))


def attend(own, other, place, ends, heads, key_span):
    members, _, tok, width = own.shape
    piece = tok // 2
    steps = members * 2
    slots = tok * members * (1 + other.shape[0])
    return pl.pallas_call(
        functools.partial(_forward_kernel, heads, ends.shape[0], key_span),
        grid_spec=pltpu.PrefetchScalarGridSpec(
            num_scalar_prefetch=2,
            grid=(steps,),
            in_specs=[_whole(own.shape), _whole(other.shape)],
            out_specs=[
                pl.BlockSpec((1, piece, width), lambda i, *_: (i, 0, 0)),
                pl.BlockSpec((1, width, piece), lambda i, *_: (i, 0, 0)),
                pl.BlockSpec((1, 1, heads * piece), lambda i, *_: (i, 0, 0)),
            ],
            scratch_shapes=[
                pltpu.VMEM((slots, width), jnp.bfloat16),
                pltpu.VMEM((width, slots), jnp.bfloat16),
            ],
        ),
        out_shape=[
            jax.ShapeDtypeStruct((steps, piece, width), jnp.bfloat16),
            jax.ShapeDtypeStruct((steps, width, piece), jnp.float32),
            jax.ShapeDtypeStruct((steps, 1, heads * piece), jnp.float32),
        ],
        compiler_params=pltpu.CompilerParams(vmem_limit_bytes=VMEM_LIMIT),
        cost_estimate=pl.CostEstimate(
            flops=4 * steps * piece * slots * width, bytes_accessed=8 * slots * width,
            transcendentals=steps * piece * slots * heads // 2,
        ),
    )(place, ends, own, other)


def attend_grads(own, other, grad, keep, lse, place, ends, heads, key_span):
    members, _, tok, width = own.shape
    piece = tok // 2
    steps = members * 2
    slots = tok * members * (1 + other.shape[0])
    return pl.pallas_call(
        functools.partial(_backward_kernel, heads, ends.shape[0], key_span),
        grid_spec=pltpu.PrefetchScalarGridSpec(
            num_scalar_prefetch=2,
            grid=(steps,),
            in_specs=[
                _whole(own.shape),
                _whole(other.shape),
                _whole(grad.shape),
                pl.BlockSpec((1, width, piece), lambda i, *_: (i, 0, 0)),
                pl.BlockSpec((1, 1, heads * piece), lambda i, *_: (i, 0, 0)),
            ],
            out_specs=[
                pl.BlockSpec((1, piece, width), lambda i, *_: (i, 0, 0)),
                _whole((members, 2, tok, width)),
                _whole(other.shape),
            ],
            scratch_shapes=[
                pltpu.VMEM((slots, width), jnp.bfloat16),
                pltpu.VMEM((width, slots), jnp.bfloat16),
                pltpu.VMEM((slots, width), jnp.bfloat16),
                pltpu.VMEM((slots, width), jnp.float32),
                pltpu.VMEM((slots, width), jnp.float32),
            ],
        ),
        out_shape=[
            jax.ShapeDtypeStruct((steps, piece, width), jnp.bfloat16),
            jax.ShapeDtypeStruct((members, 2, tok, width), jnp.float32),
            jax.ShapeDtypeStruct(other.shape, jnp.bfloat16),
        ],
        compiler_params=pltpu.CompilerParams(vmem_limit_bytes=VMEM_LIMIT),
        cost_estimate=pl.CostEstimate(
            flops=10 * steps * piece * slots * width, bytes_accessed=12 * slots * width,
            transcendentals=steps * piece * slots * heads // 2,
        ),
    )(place, ends, own, other, grad, keep, lse)


BOTH = ("ctx", "fsdp")


def swap(values, axis, mask):
    count = lax.axis_size(axis)
    return lax.ppermute(values, axis, [(i, i ^ mask) for i in range(count)])


def gather_shards(shard):
    near = swap(shard, "fsdp", 1)
    far = swap(shard, "fsdp", 2)
    return (shard, near, far, swap(far, "fsdp", 1))


def in_order(shards):
    own = lax.axis_index("fsdp")
    buffer = jnp.zeros((len(shards),) + shards[0].shape, shards[0].dtype)
    for k, shard in enumerate(shards):
        buffer = lax.dynamic_update_index_in_dim(buffer, shard, own ^ k, 0)
    return buffer


def gather_rows(shard):
    return in_order(gather_shards(shard)).reshape(-1, shard.shape[1])


def weight_grad(left, right):
    own = lax.axis_index("fsdp")
    width = left.shape[1] // 4

    def pick(k):
        return lax.dynamic_slice_in_dim(left, (own ^ k) * width, width, 1)

    mine = jnp.concatenate([pick(0), pick(2)], axis=1)
    theirs = swap(jnp.concatenate([pick(1), pick(3)], axis=1), "fsdp", 1)
    right_all = jnp.concatenate([right, swap(right, "fsdp", 1)], axis=0)
    left_all = jnp.concatenate([mine, theirs], axis=0)
    grads = jnp.einsum("tr,tn->rn", left_all, right_all, preferred_element_type=jnp.float32)
    arrived = swap(grads[width:].astype(jnp.bfloat16), "fsdp", 2)
    return (grads[:width] + arrived.astype(jnp.float32)).astype(jnp.bfloat16)


def total(grads):
    return tuple(g.astype(jnp.float32) for g in lax.psum(grads, "ctx"))


def layout(lengths_row, order_row, piece_len):
    all_slots = order_row.shape[0] * piece_len
    position = (
        order_row[:, None] * piece_len + jnp.arange(piece_len, dtype=jnp.int32)[None, :]
    ).reshape(all_slots)
    count = jnp.arange(lengths_row.shape[0], dtype=jnp.int32)
    seq_ends = jnp.sum(
        jnp.where(count[:, None] <= count[None, :], lengths_row[:, None], 0), axis=0, dtype=jnp.int32
    )
    segment = jnp.sum(
        (position[:, None] >= seq_ends[None, :]).astype(jnp.int32), axis=1, dtype=jnp.int32
    )
    seq_start = jnp.sum(
        jnp.where(segment[:, None] > count[None, :], lengths_row[None, :], 0),
        axis=1,
        dtype=jnp.int32,
    )
    return (seq_ends, position - seq_start)


def angles(offset, head_dim):
    freq_table = jnp.exp(
        jnp.arange(head_dim // 2, dtype=jnp.float32) * (-2.0 * math.log(10000.0) / head_dim)
    )
    theta = offset.astype(jnp.float32)[..., None] * freq_table
    cosine, sine = jnp.cos(theta), jnp.sin(theta)
    return (
        jnp.tile(cosine, (1, 2 * HEADS)),
        jnp.tile(jnp.concatenate([-sine, sine], axis=1), (1, HEADS)),
    )


def partner(values):
    lane = lax.broadcasted_iota(jnp.int32, values.shape, 1)
    half = HD // 2
    return jnp.where(
        lane % HD < half, jnp.roll(values, -half, axis=1), jnp.roll(values, half, axis=1)
    )


def rotate(values, tables):
    return values * tables[0] + partner(values) * tables[1]


def unrotate(grads, tables):
    return grads * tables[0] - partner(grads) * tables[1]


def rms_apply(resid, gain_row):
    inv_rms = lax.rsqrt(jnp.mean(resid * resid, axis=-1, keepdims=True) + EPSILON)
    return ((resid * inv_rms * gain_row).astype(jnp.bfloat16), inv_rms)


def rms_back(resid, inv_rms, gain_row, grad_normed):
    weighted = grad_normed * gain_row
    grad_resid = inv_rms * weighted - resid * inv_rms**3 * jnp.mean(
        weighted * resid, axis=-1, keepdims=True
    )
    return (grad_resid, jnp.sum(grad_normed * resid * inv_rms, axis=0))


def feed_forward(normed, w_in, w_out):
    mixed_proj = jnp.dot(normed, w_in, preferred_element_type=jnp.float32)
    hidden_width = w_out.shape[0]
    hidden = (jax.nn.silu(mixed_proj[:, :hidden_width]) * mixed_proj[:, hidden_width:]).astype(
        jnp.bfloat16
    )
    return (jnp.dot(hidden, w_out, preferred_element_type=jnp.float32), mixed_proj, hidden)


def hidden_back(gate_pre, up_pre, grad_hidden):
    sigmoid_gate = jax.nn.sigmoid(gate_pre)
    grad_gate = grad_hidden * up_pre * sigmoid_gate * (1.0 + gate_pre * (1.0 - sigmoid_gate))
    grad_up = grad_hidden * gate_pre * sigmoid_gate
    return (grad_gate.astype(jnp.bfloat16), grad_up.astype(jnp.bfloat16))


def feed_back(mixed_proj, grad_result, w_in, w_out):
    hidden_width = w_out.shape[0]
    grad_hidden = (
        jnp.einsum("td,fd->tf", grad_result, w_out, preferred_element_type=jnp.float32)
        .astype(jnp.bfloat16)
        .astype(jnp.float32)
    )
    grad_mixed = jnp.concatenate(
        hidden_back(mixed_proj[:, :hidden_width], mixed_proj[:, hidden_width:], grad_hidden), axis=1
    )
    grad_normed = jnp.einsum("tf,df->td", grad_mixed, w_in, preferred_element_type=jnp.float32)
    return (grad_normed, grad_mixed)


def head_groups():
    count = lax.axis_size("ctx")
    parts = count // HEAD_GROUPS
    return (parts, [[h * parts + q for h in range(HEAD_GROUPS)] for q in range(parts)])


def to_heads(values):
    return lax.all_to_all(
        values, "ctx", 0, 0, tiled=True, axis_index_groups=head_groups()[1]
    )


def split_heads(values, kinds):
    rows = values.shape[0]
    return jnp.transpose(values.reshape(rows, kinds, HEAD_GROUPS, -1), (2, 1, 0, 3))


def join_heads(values):
    rows = values.shape[2]
    return jnp.transpose(values, (2, 1, 0, 3)).reshape(rows, -1)


def attend_forward(resid, gain_row, w_in, w_out, geometry):
    tables, place, ends = geometry
    tok_rows, model_width = resid.shape
    normed, inv_rms = rms_apply(resid, gain_row)
    mixed_proj = jnp.dot(normed, w_in, preferred_element_type=jnp.float32)
    queries = rotate(mixed_proj[:, :model_width], tables) * 0.125
    keys_rot = rotate(mixed_proj[:, model_width : 2 * model_width], tables)
    mixed = jnp.concatenate([queries, keys_rot, mixed_proj[:, 2 * model_width :]], axis=1).astype(
        jnp.bfloat16
    )
    own = to_heads(split_heads(mixed, 3))
    parts = head_groups()[0]
    other = jnp.stack([swap(own[:, 1:], "ctx", k) for k in range(1, parts)])
    out, keep, lse = attend(own, other, place, ends, HEADS // HEAD_GROUPS, KEY_SPAN)
    back = to_heads(out.reshape(HEAD_GROUPS, tok_rows, -1))
    attended = join_heads(back[:, None])
    branch = jnp.dot(attended, w_out, preferred_element_type=jnp.float32)
    return (resid + branch, (resid, inv_rms, normed, own, other, keep, lse, attended))


def attend_backward(grad_resid, kept, gain_row, w_in, w_out, geometry):
    resid, inv_rms, normed, own, other, keep, lse, attended = kept
    tables, place, ends = geometry
    tok_rows, model_width = resid.shape
    parts = head_groups()[0]
    grad_branch = grad_resid.astype(jnp.bfloat16)
    grad_attended = jnp.einsum(
        "te,de->td", grad_branch, w_out, preferred_element_type=jnp.float32
    ).astype(jnp.bfloat16)
    grad_heads = to_heads(split_heads(grad_attended, 1))[:, 0]
    grad_query, grad_own, grad_other = attend_grads(
        own, other, grad_heads, keep, lse, place, ends, HEADS // HEAD_GROUPS, KEY_SPAN
    )
    for k in range(1, parts):
        grad_own = grad_own + swap(grad_other[k - 1], "ctx", k).astype(jnp.float32)
    grad_out = jnp.concatenate(
        [grad_query.reshape(HEAD_GROUPS, 1, tok_rows, -1), grad_own.astype(jnp.bfloat16)], axis=1
    )
    grad_rot = join_heads(to_heads(grad_out)).astype(jnp.float32)
    grad_mixed = jnp.concatenate(
        [
            unrotate(grad_rot[:, :model_width] * 0.125, tables),
            unrotate(grad_rot[:, model_width : 2 * model_width], tables),
            grad_rot[:, 2 * model_width :],
        ],
        axis=1,
    ).astype(jnp.bfloat16)
    grad_normed = jnp.einsum("te,de->td", grad_mixed, w_in, preferred_element_type=jnp.float32)
    grad_in, grad_gain = rms_back(resid, inv_rms, gain_row, grad_normed)
    weights = (weight_grad(normed, grad_mixed), weight_grad(attended, grad_branch))
    return (grad_resid + grad_in, weights, grad_gain)


def per_device(
    tokens,
    cotangent,
    lengths,
    piece_order,
    routes,
    attn_in,
    attn_out,
    norm_gain,
    mlp_in,
    mlp_out,
    router,
    expert_in,
    expert_out,
):
    tok_rows, model_width = tokens.shape[1:]
    shard_width = router.shape[0]
    num_experts = router.shape[1]
    own_ctx, own_fsdp = lax.axis_index("ctx"), lax.axis_index("fsdp")
    ctx_count, fsdp_count = lax.axis_size("ctx"), lax.axis_size("fsdp")
    units = ctx_count * fsdp_count // num_experts
    hid_unit = expert_out.shape[0] // fsdp_count
    members = [
        [i for i in range(ctx_count * fsdp_count) if i % units == lane] for lane in range(units)
    ]

    def dispatch(values):
        return lax.all_to_all(values, BOTH, 0, 0, tiled=True, axis_index_groups=members)

    def to_units(values):
        return jnp.stack([values] + [swap(values, BOTH, k) for k in range(1, units)])

    def from_units(partial):
        summed = partial[0]
        for k in range(1, units):
            summed = summed + swap(partial[k].astype(jnp.bfloat16), BOTH, k).astype(jnp.float32)
        return summed.astype(jnp.bfloat16)

    small = gather_shards(jnp.concatenate([norm_gain.reshape(4, shard_width), router.T], axis=0))
    small = jnp.transpose(in_order(small), (1, 0, 2)).reshape(-1, model_width)
    gains = small[:4].astype(jnp.float32)
    router_full = small[4:].T
    weights = [
        [gather_rows(w[layer]) for w in (attn_in, attn_out, mlp_in, mlp_out)] for layer in range(2)
    ]

    seq_ends, offset = layout(lengths[0], piece_order[0], tok_rows // 2)
    tables = angles(lax.dynamic_slice_in_dim(offset, own_ctx * tok_rows, tok_rows, 0), HD)
    parts = ctx_count // HEAD_GROUPS
    order = piece_order[0].reshape(HEAD_GROUPS, parts, 2)
    place = jnp.stack(
        [
            lax.dynamic_index_in_dim(order, (own_ctx % parts) ^ k, 1, keepdims=False)
            for k in range(parts)
        ]
    ).reshape(-1)
    geometry = (tables, place, seq_ends)

    item_count = tok_rows * TOP
    capacity = 2 * item_count // num_experts
    slot_count = num_experts * capacity
    expert_ids = jnp.arange(num_experts, dtype=jnp.int32)
    chosen = routes[0][:, :, None] == expert_ids[None, None, :]
    flat_chosen = chosen.reshape(item_count, num_experts).astype(jnp.bfloat16)
    items = jnp.arange(item_count, dtype=jnp.int32)
    earlier = jnp.dot(
        (items[None, :] < items[:, None]).astype(jnp.bfloat16),
        flat_chosen,
        preferred_element_type=jnp.float32,
    )
    slot_rank = jnp.sum(earlier * flat_chosen.astype(jnp.float32), axis=1).astype(jnp.int32)
    slot_target = (routes[0].reshape(item_count) * capacity + slot_rank).reshape(tok_rows, TOP)
    slots = jnp.arange(slot_count, dtype=jnp.int32)
    at_slot = [slots[:, None] == slot_target[None, :, k] for k in range(TOP)]
    of_token = [(slots[None, :] == slot_target[:, k, None]).astype(jnp.bfloat16) for k in range(TOP)]
    fill = (at_slot[0] | at_slot[1]).astype(jnp.bfloat16)

    def to_slots(rows):
        return jnp.dot(fill, rows, preferred_element_type=jnp.float32).astype(jnp.bfloat16)

    def send_rows(rows):
        return to_units(
            dispatch(to_slots(rows).reshape(num_experts, capacity, model_width))
        ).reshape(-1, model_width)

    grad_arrived = send_rows(cotangent[0])
    expert_w = lax.all_to_all(
        jnp.concatenate([expert_in, expert_out[None]]).reshape(3, fsdp_count, hid_unit, -1),
        "fsdp",
        1,
        1,
        tiled=True,
    )
    expert_w = jnp.transpose(expert_w, (0, 2, 1, 3)).reshape(3, hid_unit, model_width)

    resid_in = tokens[0].astype(jnp.float32)
    after_one, kept_one = attend_forward(
        resid_in, gains[0], weights[0][0], weights[0][1], geometry
    )
    normed_two, inv_two = rms_apply(after_one, gains[1])
    dense_branch, mixed_two, hidden_two = feed_forward(normed_two, weights[0][2], weights[0][3])
    middle = after_one + dense_branch
    after_two, kept_two = attend_forward(
        middle, gains[2], weights[1][0], weights[1][1], geometry
    )
    normed_three, inv_three = rms_apply(after_two, gains[3])

    logits = jnp.dot(normed_three, router_full, preferred_element_type=jnp.float32)
    picked = jnp.sum(jnp.where(chosen, logits[:, None, :], 0.0), axis=-1)
    gate_probs = jax.nn.softmax(picked, axis=-1)
    arrived = send_rows(normed_three)
    slot_gates = sum(
        jnp.sum(jnp.where(at_slot[k], gate_probs[None, :, k], 0.0), axis=1) for k in range(TOP)
    )
    arrived_gates = to_units(dispatch(slot_gates.reshape(num_experts, capacity))).reshape(-1, 1)

    shared, mixed_three, hidden_three = feed_forward(normed_three, weights[1][2], weights[1][3])
    grad_shared_in, grad_mixed_three = feed_back(
        mixed_three, cotangent[0], weights[1][2], weights[1][3]
    )

    gate_pre = jnp.einsum("rd,fd->rf", arrived, expert_w[0], preferred_element_type=jnp.float32)
    up_pre = jnp.einsum("rd,fd->rf", arrived, expert_w[1], preferred_element_type=jnp.float32)
    hidden_rows = (jax.nn.silu(gate_pre) * up_pre).astype(jnp.bfloat16)
    partial_rows = jnp.dot(hidden_rows, expert_w[2], preferred_element_type=jnp.float32)
    expert_rows = dispatch(
        from_units(partial_rows.reshape(units, num_experts, capacity, model_width))
    ).reshape(slot_count, model_width)

    grad_rows = (arrived_gates * grad_arrived.astype(jnp.float32)).astype(jnp.bfloat16)
    grad_hidden = (
        jnp.einsum("rd,fd->rf", grad_rows, expert_w[2], preferred_element_type=jnp.float32)
        .astype(jnp.bfloat16)
        .astype(jnp.float32)
    )
    grad_gate, grad_up = hidden_back(gate_pre, up_pre, grad_hidden)
    grad_copies = jnp.dot(grad_gate, expert_w[0], preferred_element_type=jnp.float32) + jnp.dot(
        grad_up, expert_w[1], preferred_element_type=jnp.float32
    )
    grad_back = dispatch(
        from_units(grad_copies.reshape(units, num_experts, capacity, model_width))
    ).reshape(slot_count, model_width)
    grad_experts = jnp.stack(
        [
            jnp.einsum("rf,rd->fd", left, right, preferred_element_type=jnp.float32).astype(
                jnp.bfloat16
            )
            for left, right in ((grad_gate, arrived), (grad_up, arrived), (hidden_rows, grad_rows))
        ]
    ).reshape(3, hid_unit, fsdp_count, -1)
    grad_experts = lax.all_to_all(
        jnp.transpose(grad_experts, (0, 2, 1, 3)), "fsdp", 1, 1, tiled=True
    ).astype(jnp.float32)
    grad_experts = grad_experts.reshape(3, hid_unit * fsdp_count, -1)

    back_rows = [jnp.dot(p, expert_rows, preferred_element_type=jnp.float32) for p in of_token]
    output = after_two + shared + sum(gate_probs[:, k, None] * back_rows[k] for k in range(TOP))
    grad_out = cotangent[0].astype(jnp.float32)
    grad_gates = jnp.stack([jnp.sum(rows * grad_out, axis=-1) for rows in back_rows], axis=1)
    grad_picked = gate_probs * (
        grad_gates - jnp.sum(gate_probs * grad_gates, axis=-1, keepdims=True)
    )
    grad_logits = jnp.sum(jnp.where(chosen, grad_picked[..., None], 0.0), axis=1)
    grad_router = jnp.einsum(
        "te,td->ed", grad_logits, normed_three.astype(jnp.float32), precision=HIGHEST
    )
    grad_normed = (
        grad_shared_in
        + jnp.dot(of_token[0] + of_token[1], grad_back, preferred_element_type=jnp.float32)
        + jnp.einsum(
            "te,de->td", grad_logits, router_full.astype(jnp.float32), precision=HIGHEST
        )
    )
    grad_in, grad_gain_three = rms_back(after_two, inv_three, gains[3], grad_normed)
    shared_grads = (
        weight_grad(normed_three, grad_mixed_three),
        weight_grad(hidden_three, cotangent[0]),
    )
    shared_total = total(shared_grads)
    grad_resid, attn_grads, grad_gain_two = attend_backward(
        grad_out + grad_in, kept_two, gains[2], weights[1][0], weights[1][1], geometry
    )
    attn_total_two = total(attn_grads)
    grad_branch = grad_resid.astype(jnp.bfloat16)
    grad_dense_in, grad_mixed_two = feed_back(
        mixed_two, grad_branch, weights[0][2], weights[0][3]
    )
    dense_total = total(
        (weight_grad(normed_two, grad_mixed_two), weight_grad(hidden_two, grad_branch))
    )
    grad_in_two, grad_gain_dense = rms_back(after_one, inv_two, gains[1], grad_dense_in)
    grad_resid, attn_grads, grad_gain_one = attend_backward(
        grad_resid + grad_in_two, kept_one, gains[0], weights[0][0], weights[0][1], geometry
    )
    attn_total_one = total(attn_grads)
    small_grads = lax.psum(
        jnp.concatenate(
            [
                jnp.stack([grad_gain_one, grad_gain_dense, grad_gain_two, grad_gain_three]),
                grad_router,
            ]
        ),
        BOTH,
    )
    small_grads = lax.dynamic_slice_in_dim(small_grads, own_fsdp * shard_width, shard_width, 1)
    return (
        output[None],
        grad_resid[None],
        jnp.stack([attn_total_one[0], attn_total_two[0]]),
        jnp.stack([attn_total_one[1], attn_total_two[1]]),
        small_grads[:4].reshape(2, 2, shard_width),
        jnp.stack([dense_total[0], shared_total[0]]),
        jnp.stack([dense_total[1], shared_total[1]]),
        small_grads[4:].T,
        grad_experts[:2],
        grad_experts[2],
    )


def solution(mesh):
    placed = (
        P("fsdp", "ctx", None),
        P("fsdp", "ctx", None),
        P("fsdp", None),
        P("fsdp", None),
        P("fsdp", "ctx", None),
        P(None, "fsdp", None),
        P(None, "fsdp", None),
        P(None, None, "fsdp"),
        P(None, "fsdp", None),
        P(None, "fsdp", None),
        P("fsdp", None),
        P(None, "ctx", "fsdp"),
        P("ctx", "fsdp"),
    )
    return jax.shard_map(
        per_device,
        mesh=mesh,
        in_specs=placed,
        out_specs=(
            P("fsdp", "ctx", None),
            P("fsdp", "ctx", None),
            P(None, "fsdp", None),
            P(None, "fsdp", None),
            P(None, None, "fsdp"),
            P(None, "fsdp", None),
            P(None, "fsdp", None),
            P("fsdp", None),
            P(None, "ctx", "fsdp"),
            P("ctx", "fsdp"),
        ),
        check_vma=False,
    )
```

```python
import functools
import math

import jax
import jax.numpy as jnp
from jax import lax
from jax.experimental import pallas as pl
from jax.experimental.pallas import tpu as pltpu
from jax.sharding import PartitionSpec as P

HEADS = 12
HD = 64
FF = 2048
TOP = 2
HEAD_GROUPS = 4
KEY_SPAN = 512
VMEM_LIMIT = 60 * 1024 * 1024


HIGHEST = lax.Precision.HIGHEST
EPSILON = 1e-06
NEGATIVE = -1e30


BOTH = ("ctx", "fsdp")


def swap(values, axis, mask):
    count = lax.axis_size(axis)
    return lax.ppermute(values, axis, [(i, i ^ mask) for i in range(count)])


def gather_shards(shard):
    near = swap(shard, "fsdp", 1)
    far = swap(shard, "fsdp", 2)
    return (shard, near, far, swap(far, "fsdp", 1))


def in_order(shards):
    own = lax.axis_index("fsdp")
    buffer = jnp.zeros((len(shards),) + shards[0].shape, shards[0].dtype)
    for k, shard in enumerate(shards):
        buffer = lax.dynamic_update_index_in_dim(buffer, shard, own ^ k, 0)
    return buffer


NT = (((1,), (1,)), ((), ()))


def _dot(a, b):
    return jnp.dot(a, b, preferred_element_type=jnp.float32)


def _dot_nt(a, b):
    return lax.dot_general(a, b, NT, preferred_element_type=jnp.float32)


def _flip(values):
    return values.astype(jnp.float32).T.astype(values.dtype)


def _shape(shape, dtype=jnp.bfloat16):
    return jax.ShapeDtypeStruct(shape, dtype)


def _whole(shape):
    return pl.BlockSpec(tuple(shape), lambda *_: (0,) * len(shape))


def operands(shards, part=None):
    if isinstance(shards, (tuple, list)):
        arrays, rows, place = shards, shards[0].shape[0], lambda m, k: 0
    else:
        arrays, rows, place = (shards,) * 4, shards.shape[0] // 4, lambda m, k: m[0] ^ k
    width = arrays[0].shape[1]
    if part is None:
        specs = [
            pl.BlockSpec((rows, width), lambda i, m, k=k: (place(m, k), 0)) for k in range(4)
        ]
    else:
        size, first = part
        specs = [
            pl.BlockSpec((rows, size), lambda i, m, k=k: (place(m, k), first + (m[0] ^ i)))
            for k in range(4)
        ]
    return list(arrays), specs


def call(body, meta, inputs, outputs, scratch=(), flops=0, in_specs=None, out_specs=None, grid=(1,)):
    moved = sum(math.prod(a.shape) * a.dtype.itemsize for a in (*inputs, *outputs))
    return pl.pallas_call(
        body,
        grid_spec=pltpu.PrefetchScalarGridSpec(
            num_scalar_prefetch=1,
            grid=grid,
            in_specs=in_specs or [_whole(a.shape) for a in inputs],
            out_specs=out_specs or [_whole(a.shape) for a in outputs],
            scratch_shapes=list(scratch),
        ),
        out_shape=list(outputs),
        compiler_params=pltpu.CompilerParams(vmem_limit_bytes=VMEM_LIMIT),
        cost_estimate=pl.CostEstimate(flops=flops, bytes_accessed=moved, transcendentals=0),
    )(meta, *inputs)


def _stack(refs, cols=slice(None)):
    return jnp.concatenate([w[:, cols] for w in refs], axis=0)


def _mine(blocks, own):
    return jnp.concatenate([blocks[own ^ k] for k in range(4)], axis=1)


def _norm(rows, gain):
    inverse = lax.rsqrt(jnp.mean(rows * rows, axis=-1, keepdims=True) + EPSILON)
    return rows * inverse * gain


def _norm_back(rows, gain, grad):
    inverse = lax.rsqrt(jnp.mean(rows * rows, axis=-1, keepdims=True) + EPSILON)
    weighted = grad * gain
    scaled = rows * inverse
    back = inverse * (weighted - scaled * jnp.mean(weighted * scaled, axis=-1, keepdims=True))
    return back, jnp.sum(grad * scaled, axis=0, keepdims=True)


def _split(rows, blocks):
    width = rows.shape[1] // len(blocks)
    for b, ref in enumerate(blocks):
        ref[...] = rows[:, b * width : (b + 1) * width]


def _turn(rows, cosine, sine, sign):
    lane = lax.broadcasted_iota(jnp.int32, cosine.shape, 1)
    low = lane % HD < HD // 2
    turned = []
    for b in range(rows.shape[1] // 128):
        part = rows[:, b * 128 : (b + 1) * 128]
        other = jnp.where(low, pltpu.roll(part, 128 - HD // 2, 1), pltpu.roll(part, HD // 2, 1))
        turned.append(part * cosine + sign * (other * sine))
    return jnp.concatenate(turned, axis=1)


def _pre_kernel(meta, x, gain, cosine, sine, w0, w1, w2, w3, keep, send, *rest):
    qkv, (blocks, heads) = rest[:4], rest[4:]
    own, line = meta[0], meta[1]
    width = x.shape[1]
    normed = _norm(x[...], gain[...]).astype(jnp.bfloat16)
    _split(normed, [blocks.at[b] for b in range(4)])
    for j in range(2):
        keep[j] = blocks[own ^ (2 * j)]
        send[j] = blocks[own ^ (2 * j + 1)]
    piece = x.shape[0] // 2
    mine = _mine(blocks, own)
    for kind in range(3):
        mixed = _dot(mine, _stack((w0, w1, w2, w3), slice(kind * width, (kind + 1) * width)))
        if kind < 2:
            mixed = _turn(mixed, cosine[...], sine[...], 1.0)
        if kind == 0:
            mixed = mixed * 0.125
        turned = mixed.T.astype(jnp.bfloat16)
        block = width // 4
        for b in range(4):
            for p in range(2):
                heads[b, p, kind] = turned[
                    b * block : (b + 1) * block, p * piece : (p + 1) * piece
                ]
    for k in range(4):
        qkv[k][...] = heads[line ^ k]


def pre(meta, x, gain, tables, shards):
    rows, width = x.shape
    block = width // 4
    outs = [_shape((2, rows, block))] * 2 + [_shape((2, 3, block, rows // 2))] * 4
    shards, specs = operands(shards)
    inputs = (x, gain, *tables)
    got = call(
        _pre_kernel,
        meta,
        (*inputs, *shards),
        outs,
        [
            pltpu.VMEM((4, rows, block), jnp.bfloat16),
            pltpu.VMEM((4, 2, 3, block, rows // 2), jnp.bfloat16),
        ],
        flops=6 * rows * width * width,
        in_specs=[_whole(a.shape) for a in inputs] + specs,
    )
    return got[0], got[1], got[2:6]


def _pre_back_kernel(meta, x, gain, cosine, sine, resid, *rest):
    qkv, w = rest[:4], rest[4:8]
    mixed_out, resid_out, gain_out, heads, blocks = rest[8:]
    own, line = meta[0], meta[1]
    width = x.shape[1]
    for k in range(4):
        heads[line ^ k] = qkv[k][...]
    for kind in range(3):
        mixed = jnp.concatenate(
            [
                jnp.concatenate([heads[b, p, kind] for b in range(4)], axis=0)
                for p in range(2)
            ],
            axis=1,
        )
        mixed = mixed.astype(jnp.float32).T
        if kind < 2:
            mixed = mixed * (0.125 if kind == 0 else 1.0)
            mixed = _turn(mixed, cosine[...], sine[...], -1.0)
        mixed_out[0, :, kind * width : (kind + 1) * width] = mixed.astype(jnp.bfloat16)
    grads = _dot_nt(mixed_out[0], _stack(w))
    _split(grads, [blocks.at[own ^ k] for k in range(4)])
    grad = jnp.concatenate([blocks[b] for b in range(4)], axis=1)
    back, grad_gain = _norm_back(x[...], gain[...], grad)
    resid_out[...] = resid[...] + back
    gain_out[...] = grad_gain


def pre_back(meta, x, gain, tables, resid, qkv, shards):
    rows, width = x.shape
    shards, specs = operands(shards)
    inputs = (x, gain, *tables, resid, *qkv)
    return call(
        _pre_back_kernel,
        meta,
        (*inputs, *shards),
        [
            _shape((1, rows, 3 * width)),
            _shape((rows, width), jnp.float32),
            _shape((1, width), jnp.float32),
        ],
        [
            pltpu.VMEM((4, 2, 3, width // 4, rows // 2), jnp.bfloat16),
            pltpu.VMEM((4, rows, width // 4), jnp.float32),
        ],
        flops=6 * rows * width * width,
        in_specs=[_whole(a.shape) for a in inputs] + specs,
    )


def _post_kernel(meta, x, gain, o0, o1, o2, o3, w0, w1, w2, w3, *rest):
    after, plain, blocks_out, keep, send, att_keep, att_send, att = rest
    own, line = meta[0], meta[1]
    piece = x.shape[0] // 2
    for k, o in enumerate((o0, o1, o2, o3)):
        for p in range(2):
            att[line ^ k, p * piece : (p + 1) * piece, :] = _flip(o[p])
    for j in range(2):
        att_keep[j] = att[own ^ (2 * j)]
        att_send[j] = att[own ^ (2 * j + 1)]
    rows = x[...] + _dot(_mine(att, own), _stack((w0, w1, w2, w3)))
    after[...] = rows
    normed = _norm(rows, gain[...]).astype(jnp.bfloat16)
    plain[...] = normed
    _split(normed, [att.at[b] for b in range(4)])
    blocks_out[...] = att[...]
    for j in range(2):
        keep[j] = att[own ^ (2 * j)]
        send[j] = att[own ^ (2 * j + 1)]


def post(meta, x, gain, heads, shards):
    rows, width = x.shape
    block = width // 4
    shards, specs = operands(shards)
    inputs = (x, gain, *heads)
    return call(
        _post_kernel,
        meta,
        (*inputs, *shards),
        [_shape((rows, width), jnp.float32), _shape((rows, width)), _shape((4, rows, block))]
        + [_shape((2, rows, block))] * 4,
        [pltpu.VMEM((4, rows, block), jnp.bfloat16)],
        flops=2 * rows * width * width,
        in_specs=[_whole(a.shape) for a in inputs] + specs,
    )


def _post_back_kernel(meta, x, gain, resid, grad, w0, w1, w2, w3, *rest):
    heads, (resid_out, branch, gain_out, att) = rest[:4], rest[4:]
    own, line = meta[0], meta[1]
    back, grad_gain = _norm_back(x[...], gain[...], grad[...])
    gain_out[...] = grad_gain
    rows = resid[...] + back
    resid_out[...] = rows
    rows = rows.astype(jnp.bfloat16)
    branch[0] = rows
    grads = _dot_nt(rows, _stack((w0, w1, w2, w3))).astype(jnp.bfloat16)
    _split(grads, [att.at[own ^ k] for k in range(4)])
    piece = x.shape[0] // 2
    for k in range(4):
        for p in range(2):
            heads[k][p] = _flip(att[line ^ k, p * piece : (p + 1) * piece, :])


def post_back(meta, x, gain, resid, grad, shards):
    rows, width = x.shape
    block = width // 4
    shards, specs = operands(shards)
    inputs = (x, gain, resid, grad)
    got = call(
        _post_back_kernel,
        meta,
        (*inputs, *shards),
        [_shape((2, block, rows // 2))] * 4
        + [
            _shape((rows, width), jnp.float32),
            _shape((1, rows, width)),
            _shape((1, width), jnp.float32),
        ],
        [pltpu.VMEM((4, rows, block), jnp.bfloat16)],
        flops=2 * rows * width * width,
        in_specs=[_whole(a.shape) for a in inputs] + specs,
    )
    return got[:4], got[4], got[5], got[6]


def _mlp_kernel(meta, x, blocks, *rest):
    gates, ups, downs = rest[:4], rest[4:8], rest[8:12]
    out, mixed, keep, send, acc = rest[12:]
    own, step = meta[0], pl.program_id(0)
    rows = _mine(blocks, own)
    gate = _dot(rows, _stack(gates))
    up = _dot(rows, _stack(ups))
    mixed[0], mixed[1] = gate, up
    hidden = (gate * jax.nn.sigmoid(gate) * up).astype(jnp.bfloat16)
    for k in range(4):

        @pl.when(step == k)
        def _(k=k):
            (send if k % 2 else keep)[k // 2] = hidden
            part = _dot(hidden, downs[k][...])
            if k == 0:
                acc[...] = x[...] + part
            elif k < 3:
                acc[...] += part
            else:
                out[...] = acc[...] + part


def mlp_width(shards):
    first = shards[0] if isinstance(shards, (tuple, list)) else shards
    return first.shape[1] // 2


def mlp(meta, x, blocks, shards_in, shards_out):
    rows, width = x.shape
    hidden = mlp_width(shards_in)
    part = hidden // 4
    gates, gate_specs = operands(shards_in, (part, 0))
    ups, up_specs = operands(shards_in, (part, 4))
    downs, down_specs = operands(shards_out)
    return call(
        _mlp_kernel,
        meta,
        (x, blocks, *gates, *ups, *downs),
        [
            _shape((rows, width), jnp.float32),
            _shape((2, rows, hidden), jnp.float32),
            _shape((2, rows, part)),
            _shape((2, rows, part)),
        ],
        [pltpu.VMEM((rows, width), jnp.float32)],
        flops=6 * rows * width * hidden,
        in_specs=[_whole(x.shape), _whole(blocks.shape), *gate_specs, *up_specs, *down_specs],
        out_specs=[
            _whole((rows, width)),
            pl.BlockSpec((2, rows, part), lambda i, m: (0, 0, m[0] ^ i)),
            _whole((2, rows, part)),
            _whole((2, rows, part)),
        ],
        grid=(4,),
    )


def _mlp_back_kernel(meta, branch, mixed, *rest):
    gates, ups, downs = rest[:4], rest[4:8], rest[8:12]
    grad_mixed, grad_out, grad_hidden, acc, turned = rest[12:]
    own, step = meta[0], pl.program_id(0)
    for k in range(4):

        @pl.when(step == k)
        def _(k=k):
            grad_hidden[...] = _dot_nt(branch[0], downs[k][...]).astype(jnp.bfloat16)

    grad_h = grad_hidden[...].astype(jnp.float32)
    gate, up = mixed[0], mixed[1]
    sigmoid = jax.nn.sigmoid(gate)
    grad_gate = (grad_h * up * sigmoid * (1.0 + gate * (1.0 - sigmoid))).astype(jnp.bfloat16)
    grad_up = (grad_h * gate * sigmoid).astype(jnp.bfloat16)
    grad_mixed[0], grad_mixed[1] = grad_gate, grad_up
    part = _dot_nt(grad_gate, _stack(gates)) + _dot_nt(grad_up, _stack(ups))

    @pl.when(step == 0)
    def _():
        acc[...] = part

    @pl.when((step > 0) & (step < 3))
    def _():
        acc[...] += part

    @pl.when(step == 3)
    def _():
        _split(acc[...] + part, [turned.at[own ^ k] for k in range(4)])
        grad_out[...] = jnp.concatenate([turned[b] for b in range(4)], axis=1)


def mlp_back(meta, branch, mixed, shards_in, shards_out):
    _, rows, width = branch.shape
    hidden = mixed.shape[2]
    part = hidden // 4
    block = width // 4
    gates, gate_specs = operands(shards_in, (part, 0))
    ups, up_specs = operands(shards_in, (part, 4))
    downs, down_specs = operands(shards_out)
    return call(
        _mlp_back_kernel,
        meta,
        (branch, mixed, *gates, *ups, *downs),
        [_shape((2, rows, hidden)), _shape((rows, width), jnp.float32)],
        [
            pltpu.VMEM((rows, part), jnp.bfloat16),
            pltpu.VMEM((rows, width), jnp.float32),
            pltpu.VMEM((4, rows, block), jnp.float32),
        ],
        flops=6 * rows * width * hidden,
        in_specs=[
            _whole(branch.shape),
            pl.BlockSpec((2, rows, part), lambda i, m: (0, 0, m[0] ^ i)),
            *gate_specs,
            *up_specs,
            *down_specs,
        ],
        out_specs=[
            pl.BlockSpec((2, rows, part), lambda i, m: (0, 0, m[0] ^ i)),
            _whole((rows, width)),
        ],
        grid=(4,),
    )


def _grad_kernel(meta, left, left_near, right, right_near, own, send, flipped):
    rows, depth = left.shape[1:]

    @pl.when((pl.program_id(0) == 0) & (pl.program_id(1) == 0))
    def _():
        for j in range(2):
            flipped[j * depth : (j + 1) * depth, :rows] = _flip(left[j])
            flipped[j * depth : (j + 1) * depth, rows:] = _flip(left_near[j])

    both = jnp.concatenate([right[0], right_near[0]], axis=0)
    grads = _dot(flipped[...], both).astype(jnp.bfloat16)
    own[...] = grads[:depth]
    send[...] = grads[depth:]


def weight_grad(meta, left, left_near, right, right_near):
    groups, rows, width = right.shape
    depth = left.shape[2]
    chunk = 512 if width % 768 else 768
    steps = width // chunk
    right_spec = pl.BlockSpec((1, rows, chunk), lambda g, i, m: (g, 0, i))
    out_spec = pl.BlockSpec((depth, chunk), lambda g, i, m: (0, g * steps + i))
    return call(
        _grad_kernel,
        meta,
        (left, left_near, right, right_near),
        [_shape((depth, groups * width))] * 2,
        [pltpu.VMEM((2 * depth, 2 * rows), jnp.bfloat16)],
        flops=8 * rows * depth * groups * width,
        in_specs=[_whole(left.shape), _whole(left.shape), right_spec, right_spec],
        out_specs=[out_spec, out_spec],
        grid=(groups, steps),
    )


def _mask(first_key, keys, query_pos, query_start, copies):
    key_pos = first_key + lax.broadcasted_iota(jnp.int32, (keys, query_pos.shape[1]), 0)
    allowed = (key_pos <= query_pos) & (key_pos >= query_start)
    return jnp.concatenate([allowed] * copies, axis=1)


def _tables(meta, parts):
    return (lambda s: meta[2 + s], lambda k: meta[2 + 8 * parts + k])


def _query_geometry(place, ends, count, piece, key_span):
    query_pos = place * piece + lax.broadcasted_iota(jnp.int32, (1, piece), 1)
    query_start = jnp.zeros_like(query_pos)
    first = place * piece
    least = jnp.int32(0)
    for k in range(count):
        last = k == count - 1
        query_start = jnp.where(query_pos >= ends(k), query_pos if last else ends(k), query_start)
        least = jnp.where(first >= ends(k), first if last else ends(k), least)
    return (query_pos, query_start, least // key_span, (first + piece - 1) // key_span + 1)


def _stack_heads(rows, heads):
    head_dim = rows.shape[0] // heads
    head = lax.broadcasted_iota(jnp.int32, rows.shape, 0) // head_dim
    zero = jnp.zeros_like(rows)
    return jnp.concatenate([jnp.where(head == h, rows, zero) for h in range(heads)], axis=1)


def _own_heads(acc, heads, piece):
    head_dim = acc.shape[0] // heads
    return jnp.concatenate(
        [
            acc[h * head_dim : (h + 1) * head_dim, h * piece : (h + 1) * piece]
            for h in range(heads)
        ],
        axis=0,
    )


def _attend_kernel(heads, count, key_span, parts, meta, *refs):
    inputs, o, (keep, lse, keys, values_t) = (
        refs[: 4 * parts],
        refs[4 * parts : 4 * parts + 4],
        refs[4 * parts + 4 :],
    )
    width, piece = inputs[0].shape[2:]
    place, ends = _tables(meta, parts)
    for s in range(8 * parts):
        at = pl.ds(pl.multiple_of(place(s) * piece, piece), piece)
        keys[at, :] = _flip(inputs[s // 2][s % 2, 1])
        values_t[:, at] = inputs[s // 2][s % 2, 2]
    cols = heads * piece
    for s in range(8):
        query_pos, query_start, begin, end = _query_geometry(
            place(s), ends, count, piece, key_span
        )
        stacked = _stack_heads(inputs[s // 2][s % 2, 0], heads)

        def advance(block, carried):
            run_max, run_sum, acc = carried
            first = pl.multiple_of(block * key_span, key_span)
            scores = _dot(keys[pl.ds(first, key_span), :], stacked)
            allowed = _mask(first, key_span, query_pos, query_start, heads)
            scores = jnp.where(allowed, scores, NEGATIVE)
            new_max = jnp.maximum(run_max, jnp.max(scores, axis=0, keepdims=True))
            weights = jnp.exp(scores - new_max)
            factor = jnp.exp(run_max - new_max)
            run_sum = run_sum * factor + jnp.sum(weights, axis=0, keepdims=True)
            part = _dot(values_t[:, pl.ds(first, key_span)], weights.astype(jnp.bfloat16))
            return (new_max, run_sum, acc * factor + part)

        run_max, run_sum, acc = lax.fori_loop(
            begin,
            end,
            advance,
            (
                jnp.full((1, cols), NEGATIVE, jnp.float32),
                jnp.zeros((1, cols), jnp.float32),
                jnp.zeros((width, cols), jnp.float32),
            ),
        )
        kept = _own_heads(acc / run_sum, heads, piece)
        keep[s] = kept
        o[s // 2][s % 2] = kept.astype(jnp.bfloat16)
        lse[s] = run_max + jnp.log(run_sum)


def attend(meta, inputs, count):
    _, _, width, piece = inputs[0].shape
    heads = width // HD
    parts = len(inputs) // 4
    slots = parts * 8 * piece
    got = call(
        functools.partial(_attend_kernel, heads, count, KEY_SPAN, parts),
        meta,
        inputs,
        [_shape((2, width, piece))] * 4
        + [_shape((8, width, piece), jnp.float32), _shape((8, 1, heads * piece), jnp.float32)],
        [
            pltpu.VMEM((slots, width), jnp.bfloat16),
            pltpu.VMEM((width, slots), jnp.bfloat16),
        ],
        flops=32 * piece * slots * width,
    )
    return got[:4], got[4], got[5]


def _attend_back_kernel(heads, count, key_span, parts, meta, *refs):
    inputs, grads, (keep, lse), rest = (
        refs[: 4 * parts],
        refs[4 * parts : 4 * parts + 4],
        refs[4 * parts + 4 : 4 * parts + 6],
        refs[4 * parts + 6 :],
    )
    gq, gkv = rest[0], rest[1 : 1 + parts]
    keys, keys_t, values, gkeys, gvalues = rest[1 + parts :]
    width, piece = inputs[0].shape[2:]
    head_dim = width // heads
    place, ends = _tables(meta, parts)
    for s in range(8 * parts):
        at = pl.ds(pl.multiple_of(place(s) * piece, piece), piece)
        key_rows = inputs[s // 2][s % 2, 1]
        keys_t[:, at] = key_rows
        keys[at, :] = _flip(key_rows)
        values[at, :] = _flip(inputs[s // 2][s % 2, 2])
    gkeys[...] = jnp.zeros_like(gkeys)
    gvalues[...] = jnp.zeros_like(gvalues)
    for s in range(8):
        query_pos, query_start, begin, end = _query_geometry(
            place(s), ends, count, piece, key_span
        )
        stacked = _stack_heads(inputs[s // 2][s % 2, 0], heads)
        grad = grads[s // 2][s % 2]
        grad_stacked = _stack_heads(grad, heads)
        product = grad.astype(jnp.float32) * keep[s]
        delta = jnp.concatenate(
            [
                jnp.sum(product[h * head_dim : (h + 1) * head_dim, :], axis=0, keepdims=True)
                for h in range(heads)
            ],
            axis=1,
        )
        log_sum = lse[s]

        def retreat(block, acc):
            first = pl.multiple_of(block * key_span, key_span)
            at = pl.ds(first, key_span)
            scores = _dot(keys[at, :], stacked)
            allowed = _mask(first, key_span, query_pos, query_start, heads)
            probs = jnp.where(allowed, jnp.exp(scores - log_sum), 0.0)
            grad_probs = _dot(values[at, :], grad_stacked)
            grad_scores = (probs * (grad_probs - delta)).astype(jnp.bfloat16)
            gvalues[:, at] += _dot_nt(grad_stacked, probs.astype(jnp.bfloat16))
            gkeys[:, at] += _dot_nt(stacked, grad_scores)
            return acc + _dot(keys_t[:, at], grad_scores)

        acc = lax.fori_loop(begin, end, retreat, jnp.zeros((width, heads * piece), jnp.float32))
        gq[s] = _own_heads(acc, heads, piece).astype(jnp.bfloat16)
    for s in range(8 * parts):
        at = pl.ds(pl.multiple_of(place(s) * piece, piece), piece)
        out = gkv[s // 8]
        out[s % 8, 0] = gkeys[:, at].astype(out.dtype)
        out[s % 8, 1] = gvalues[:, at].astype(out.dtype)


def attend_back(meta, inputs, grads, keep, lse, count):
    _, _, width, piece = inputs[0].shape
    heads = width // HD
    parts = len(inputs) // 4
    slots = parts * 8 * piece
    got = call(
        functools.partial(_attend_back_kernel, heads, count, KEY_SPAN, parts),
        meta,
        (*inputs, *grads, keep, lse),
        [_shape((8, width, piece)), _shape((8, 2, width, piece), jnp.float32)]
        + [_shape((8, 2, width, piece))] * (parts - 1),
        [
            pltpu.VMEM((slots, width), jnp.bfloat16),
            pltpu.VMEM((width, slots), jnp.bfloat16),
            pltpu.VMEM((slots, width), jnp.bfloat16),
            pltpu.VMEM((width, slots), jnp.float32),
            pltpu.VMEM((width, slots), jnp.float32),
        ],
        flops=80 * piece * slots * width,
    )
    return got[0], got[1], got[2:]


def _merge_kernel(meta, gq, own, *rest):
    arrived, out = rest[:-4], rest[-4:]
    for s in range(8):
        total = own[s]
        for other in arrived:
            total = total + other[s].astype(jnp.float32)
        out[s // 2][s % 2, 0] = gq[s]
        out[s // 2][s % 2, 1:3] = total.astype(jnp.bfloat16)


def merge(meta, gq, own, arrived):
    _, width, piece = gq.shape
    return call(
        _merge_kernel, meta, (gq, own, *arrived), [_shape((2, 3, width, piece))] * 4
    )


def _halve_kernel(meta, first, second, sent, kept):
    summed = (first[...].astype(jnp.float32) + second[...].astype(jnp.float32)).astype(jnp.bfloat16)
    half = sent.shape[1]
    left, right = summed[:, :half], summed[:, half:]
    side = meta[0] == 0
    sent[...] = jnp.where(side, right, left)
    kept[...] = jnp.where(side, left, right)


def _quarter_kernel(meta, first, second, *rest):
    parts, summed = rest[:-1], rest[-1]
    summed[...] = (first[...].astype(jnp.float32) + second[...].astype(jnp.float32)).astype(
        jnp.bfloat16
    )
    chunk = parts[0].shape[0]
    for k, part in enumerate(parts):
        at = pl.multiple_of((meta[1] ^ k) * chunk, chunk)
        part[...] = summed[pl.ds(at, chunk), :]


def _place_kernel(meta, other, *refs):
    out, parts = refs[-1], refs[:-1]
    _, rows, width = out.shape
    lines = len(parts) // 2
    chunk, half = rows // lines, width // 2
    side = meta[0] == 0
    for k in range(lines):
        at = pl.multiple_of((meta[1] ^ k) * chunk, chunk)
        own = parts[k][...].astype(jnp.float32)
        near = parts[lines + k][...].astype(jnp.float32)
        out[0, pl.ds(at, chunk), :half] = jnp.where(side, own, near)
        out[0, pl.ds(at, chunk), half:] = jnp.where(side, near, own)
    out[1] = other[...].astype(jnp.float32)


def reduce_last(place, own, arrived, other, held):
    lines = lax.axis_size("ctx") // 2
    rows, width = own.shape
    chunk, half = rows // lines, width // 2
    if chunk % 16:
        summed = lax.psum(own + arrived, "ctx")
        return jnp.stack([summed, other]).astype(jnp.float32), held
    sent, kept = call(_halve_kernel, place, (own, arrived), [_shape((rows, half))] * 2)
    parts = call(
        _quarter_kernel,
        place,
        (kept, swap(sent, "ctx", 1)),
        [_shape((chunk, half))] * lines,
        [pltpu.VMEM((rows, half), jnp.bfloat16)],
    )
    summed = parts[0].astype(jnp.float32)
    for k in range(1, lines):
        summed = summed + swap(parts[k], "ctx", 2 * k).astype(jnp.float32)
    summed = summed.astype(jnp.bfloat16)
    column = [swap(summed, "ctx", 2 * k) if k else summed for k in range(lines)]
    column, held = lax.optimization_barrier((column, held))
    parts = column + [swap(c, "ctx", 1) for c in column]
    return (
        call(
            _place_kernel, place, (other, *parts), [_shape((2, rows, width), jnp.float32)]
        )[0],
        held,
    )


def _expert_kernel(units, meta, *refs):
    xs, cs = refs[:units], refs[units : 2 * units]
    router, ids, w_in, w_out = refs[2 * units : 2 * units + 4]
    outs = refs[2 * units + 4 :]
    parts, backs = outs[:units], outs[units : 2 * units]
    rows_out, grads_out, hidden_out, gate_out, up_out, dots_out = outs[2 * units : 2 * units + 6]
    gates, ups, downs, x, c = outs[2 * units + 6 :]
    step = pl.program_id(0)
    tiles = pl.num_programs(0) // units

    @pl.when(step == 0)
    def _():
        width = w_in.shape[2]
        for f in range(4):
            part = slice(f * width, (f + 1) * width)
            gates[part, :] = w_in[f, 0]
            ups[part, :] = w_in[f, 1]
            downs[part, :] = w_out[f]

    for u in range(units):

        @pl.when(step // tiles == u)
        def _(u=u):
            x[...] = xs[u][...]
            c[...] = cs[u][...]

    rows = x[...]
    rows_out[...] = rows
    incoming = c[...].astype(jnp.float32)
    logits = _dot(rows, router[...])
    lane = lax.broadcasted_iota(jnp.int32, logits.shape, 1)
    gap = jnp.sum(
        jnp.where(lane == meta[0], logits, 0.0)
        - jnp.where(lane.astype(jnp.float32) == ids[...], logits, 0.0),
        axis=1,
        keepdims=True,
    )
    grads = (jax.nn.sigmoid(gap) * incoming).astype(jnp.bfloat16)
    grads_out[...] = grads
    gate = _dot(rows, gates[...])
    up = _dot(rows, ups[...])
    sigmoid = jax.nn.sigmoid(gate)
    silu = gate * sigmoid
    hidden = (silu * up).astype(jnp.bfloat16)
    hidden_out[...] = hidden
    part = _dot_nt(hidden, downs[...])
    dots_out[...] = jnp.sum(part * incoming, axis=1, keepdims=True)
    grad_h = _dot(grads, downs[...]).astype(jnp.bfloat16).astype(jnp.float32)
    grad_gate = (grad_h * up * sigmoid * (1.0 + gate * (1.0 - sigmoid))).astype(jnp.bfloat16)
    grad_up = (grad_h * silu).astype(jnp.bfloat16)
    gate_out[...] = grad_gate
    up_out[...] = grad_up
    back = _dot_nt(grad_gate, gates[...]) + _dot_nt(grad_up, ups[...])
    for u in range(units):

        @pl.when(step // tiles == u)
        def _(u=u):
            parts[u][...] = part.astype(jnp.bfloat16)
            backs[u][...] = back.astype(jnp.bfloat16)


def experts(meta, xs, cs, router, ids, w_in, w_out):
    units, (rows, width), tile = len(xs), xs[0].shape, 256
    tiles, hidden = rows // tile, w_out.shape[2]
    total_rows = units * rows
    slabs = [
        pl.BlockSpec((tile, width), lambda i, m, u=u: (jnp.clip(i - u * tiles, 0, tiles - 1), 0))
        for u in range(units)
    ]

    def rowed(columns):
        return pl.BlockSpec((tile, columns), lambda i, m: (i, 0))

    got = call(
        functools.partial(_expert_kernel, units),
        meta,
        (*xs, *cs, router, ids, w_in, w_out),
        [_shape((rows, width))] * (2 * units)
        + [_shape((total_rows, width))] * 2
        + [_shape((total_rows, hidden))] * 3
        + [_shape((total_rows, 1), jnp.float32)],
        [pltpu.VMEM((width, hidden), jnp.bfloat16)] * 3
        + [pltpu.VMEM((tile, width), jnp.bfloat16)] * 2,
        flops=12 * total_rows * width * hidden,
        in_specs=slabs
        + slabs
        + [_whole(router.shape), rowed(1), _whole(w_in.shape), _whole(w_out.shape)],
        out_specs=slabs + slabs + [rowed(width)] * 2 + [rowed(hidden)] * 3 + [rowed(1)],
        grid=(units * tiles,),
    )
    return got[:units], got[units : 2 * units], got[2 * units :]


def layout(lengths_row, order_row, piece_len):
    all_slots = order_row.shape[0] * piece_len
    position = (
        order_row[:, None] * piece_len + jnp.arange(piece_len, dtype=jnp.int32)[None, :]
    ).reshape(all_slots)
    count = jnp.arange(lengths_row.shape[0], dtype=jnp.int32)
    seq_ends = jnp.sum(
        jnp.where(count[:, None] <= count[None, :], lengths_row[:, None], 0), axis=0, dtype=jnp.int32
    )
    segment = jnp.sum(
        (position[:, None] >= seq_ends[None, :]).astype(jnp.int32), axis=1, dtype=jnp.int32
    )
    seq_start = jnp.sum(
        jnp.where(segment[:, None] > count[None, :], lengths_row[None, :], 0),
        axis=1,
        dtype=jnp.int32,
    )
    return (seq_ends, position - seq_start)


def angles(offset):
    freq_table = jnp.exp(
        jnp.arange(HD // 2, dtype=jnp.float32) * (-2.0 * math.log(10000.0) / HD)
    )
    theta = offset.astype(jnp.float32)[..., None] * freq_table
    cosine, sine = jnp.cos(theta), jnp.sin(theta)
    return (
        jnp.tile(cosine, (1, 256 // HD)),
        jnp.tile(jnp.concatenate([-sine, sine], axis=1), (1, 128 // HD)),
    )


def hidden_back(gate_pre, up_pre, grad_hidden):
    sigmoid_gate = jax.nn.sigmoid(gate_pre)
    grad_gate = grad_hidden * up_pre * sigmoid_gate * (1.0 + gate_pre * (1.0 - sigmoid_gate))
    grad_up = grad_hidden * gate_pre * sigmoid_gate
    return (grad_gate.astype(jnp.bfloat16), grad_up.astype(jnp.bfloat16))


def head_parts():
    return lax.axis_size("ctx") // HEAD_GROUPS


def exchange(values):
    return [values[0]] + [swap(values[k], "ctx", k * head_parts()) for k in range(1, 4)]


def attend_forward(meta, count, resid, gain, tables, w_in, early):
    keep, send, qkv = pre(meta, resid, gain, tables, w_in)
    qkv = exchange(qkv)
    inputs = list(qkv)
    for part in range(1, head_parts()):
        inputs += [swap(values, "ctx", part) for values in qkv]
    qkv[1], early = lax.optimization_barrier((qkv[1], early))
    inputs[1] = qkv[1]
    heads, acc, lse = attend(meta, inputs, count)
    return heads, (keep, send, inputs, acc, lse), early


def near(*values):
    return [swap(v, "fsdp", 1) for v in values]


def add_arrived(grads):
    return grads[0] + swap(grads[1], "fsdp", 2)


def total(bucket, grads):
    count = lax.axis_size("ctx")
    ring = [[(i + bucket) % count for i in range(count)]]
    return lax.psum(tuple(grads), "ctx", axis_index_groups=ring)


def total_small(values):
    for axis in BOTH:
        step = 1
        while step < lax.axis_size(axis):
            values = values + swap(values, axis, step)
            step *= 2
    return values


def per_device(
    tokens,
    cotangent,
    lengths,
    piece_order,
    routes,
    attn_in,
    attn_out,
    norm_gain,
    mlp_in,
    mlp_out,
    router,
    expert_in,
    expert_out,
):
    tok_rows, model_width = tokens.shape[1:]
    shard_width = router.shape[0]
    num_experts = router.shape[1]
    own_ctx, own_fsdp = lax.axis_index("ctx"), lax.axis_index("fsdp")
    ctx_count, fsdp_count = lax.axis_size("ctx"), lax.axis_size("fsdp")
    units = ctx_count * fsdp_count // num_experts
    hid_unit = expert_out.shape[0] // fsdp_count
    members = [
        [i for i in range(ctx_count * fsdp_count) if i % units == lane] for lane in range(units)
    ]

    def dispatch(values):
        return lax.all_to_all(values, BOTH, 0, 0, tiled=True, axis_index_groups=members)

    def to_units(values):
        return [values] + [swap(values, BOTH, k) for k in range(1, units)]

    def from_units(partial):
        summed = partial[0].astype(jnp.float32)
        for k in range(1, units):
            summed = summed + swap(partial[k], BOTH, k).astype(jnp.float32)
        return summed

    def gathered(shard):
        return lax.all_gather(shard, "fsdp", axis=0, tiled=True)

    seq_ends, offset = layout(lengths[0], piece_order[0], tok_rows // 2)
    tables = angles(lax.dynamic_slice_in_dim(offset, own_ctx * tok_rows, tok_rows, 0))
    parts = ctx_count // HEAD_GROUPS
    line, side = own_ctx // parts, own_ctx % parts
    order = piece_order[0].reshape(HEAD_GROUPS, parts, 2)
    place = [order[line ^ k, side ^ part] for part in range(parts) for k in range(HEAD_GROUPS)]
    meta = jnp.concatenate([jnp.stack([own_fsdp, line]), jnp.concatenate(place), seq_ends])
    at_ctx = jnp.stack([own_ctx % 2, own_ctx // 2])
    count = lengths.shape[1]

    item_count = tok_rows * TOP
    capacity = 2 * item_count // num_experts
    slot_count = num_experts * capacity
    expert_ids = jnp.arange(num_experts, dtype=jnp.int32)
    chosen = routes[0][:, :, None] == expert_ids[None, None, :]
    flat_chosen = chosen.reshape(item_count, num_experts).astype(jnp.bfloat16)
    items = jnp.arange(item_count, dtype=jnp.int32)
    earlier = jnp.dot(
        (items[None, :] < items[:, None]).astype(jnp.bfloat16),
        flat_chosen,
        preferred_element_type=jnp.float32,
    )
    slot_rank = jnp.sum(earlier * flat_chosen.astype(jnp.float32), axis=1).astype(jnp.int32)
    slot_target = (routes[0].reshape(item_count) * capacity + slot_rank).reshape(tok_rows, TOP)
    slots = jnp.arange(slot_count, dtype=jnp.int32)
    at_slot = [slots[:, None] == slot_target[None, :, k] for k in range(TOP)]
    of_token = [(slots[None, :] == slot_target[:, k, None]).astype(jnp.bfloat16) for k in range(TOP)]
    fill = (at_slot[0] | at_slot[1]).astype(jnp.bfloat16)

    def to_slots(rows):
        return jnp.dot(fill, rows, preferred_element_type=jnp.float32).astype(jnp.bfloat16)

    def send_rows(rows):
        return dispatch(to_slots(rows).reshape(num_experts, capacity, model_width))

    other_ids = sum(
        jnp.sum(
            jnp.where(at_slot[k], routes[0][None, :, 1 - k].astype(jnp.float32), 0.0), axis=1
        )
        for k in range(TOP)
    )

    def with_notes(rows, *notes):
        extra = jnp.stack(notes, axis=1).astype(jnp.bfloat16)
        extra = jnp.pad(extra, ((0, 0), (0, 8 - len(notes)), (0, model_width - capacity)))
        return jnp.concatenate([rows, extra], axis=1)

    shard = attn_in[0]
    near_shard, far_shard = swap(shard, "fsdp", 1), swap(shard, "fsdp", 2)
    small = gather_shards(jnp.concatenate([norm_gain.reshape(4, shard_width), router.T], axis=0))
    ordered = []
    for i in range(4):
        block = small[3]
        for j in range(3):
            block = jnp.where(own_fsdp ^ j == i, small[j], block)
        ordered.append(block)
    small = jnp.concatenate(ordered, axis=1)
    gains = [small[i : i + 1].astype(jnp.float32) for i in range(4)]
    router_full = small[4:].T
    grad_rows = to_slots(cotangent[0]).reshape(num_experts, capacity, model_width)
    grad_sent = dispatch(with_notes(grad_rows, other_ids.reshape(num_experts, capacity)))
    far_shard, tables, meta, gains = lax.optimization_barrier((far_shard, tables, meta, gains))
    w_attn_in_one = (shard, near_shard, far_shard, swap(far_shard, "fsdp", 1))
    near_shard, attn_in, attn_out, mlp_in, mlp_out = lax.optimization_barrier(
        (near_shard, attn_in, attn_out, mlp_in, mlp_out)
    )
    w_attn_out_one, w_mlp_in_one, w_mlp_out_one = (
        gathered(attn_out[0]), gathered(mlp_in[0]), gathered(mlp_out[0])
    )
    w_attn_in_two, w_attn_out_two = gathered(attn_in[1]), gathered(attn_out[1])
    w_mlp_in_two, w_mlp_out_two = gathered(mlp_in[1]), gathered(mlp_out[1])

    resid_in = tokens[0].astype(jnp.float32)
    heads_one, kept_one, (grad_sent, expert_parts) = attend_forward(
        meta,
        count,
        resid_in,
        gains[0],
        tables,
        w_attn_in_one,
        (
            grad_sent,
            (
                jnp.swapaxes(expert_in, 1, 2).reshape(2, shard_width, fsdp_count, hid_unit),
                jnp.swapaxes(expert_out, 0, 1).reshape(shard_width, fsdp_count, hid_unit),
            ),
        ),
    )
    expert_w_out = lax.all_to_all(
        jnp.transpose(expert_parts[1], (1, 0, 2)), "fsdp", 0, 0, tiled=True
    )
    heads_one, expert_w_out, expert_part = lax.optimization_barrier(
        (heads_one, expert_w_out, expert_parts[0])
    )
    heads_one = exchange(heads_one)
    after_one, _, blocks_one, keep_one, send_one, att_keep_one, att_send_one = post(
        meta, resid_in, gains[1], heads_one, w_attn_out_one
    )
    middle, mixed_one, hid_keep_one, hid_send_one = mlp(
        meta, after_one, blocks_one, w_mlp_in_one, w_mlp_out_one
    )
    near_one = near(send_one, att_send_one, hid_send_one)
    heads_two, kept_two, (expert_part, grad_sent) = attend_forward(
        meta, count, middle, gains[2], tables, w_attn_in_two, (expert_part, grad_sent)
    )
    expert_w = lax.all_to_all(
        jnp.transpose(expert_part, (2, 0, 1, 3)), "fsdp", 0, 0, tiled=True
    )
    grad_arrived = to_units(grad_sent[:, :capacity].reshape(slot_count, model_width))
    arrived_ids = jnp.concatenate(
        to_units(grad_sent[:, capacity, :capacity].astype(jnp.float32))
    ).reshape(-1, 1)
    heads_two, grad_arrived, arrived_ids = lax.optimization_barrier(
        (heads_two, grad_arrived, arrived_ids)
    )
    heads_two = exchange(heads_two)
    heads_two, w_attn_out_two, expert_w = lax.optimization_barrier(
        (heads_two, w_attn_out_two, expert_w)
    )
    after_two, normed_three, blocks_two, keep_two, send_two, att_keep_two, att_send_two = post(
        meta, middle, gains[3], heads_two, w_attn_out_two
    )

    rows_sent = send_rows(normed_three)
    shared, mixed_two, hid_keep_two, hid_send_two = mlp(
        meta, after_two, blocks_two, w_mlp_in_two, w_mlp_out_two
    )
    grad_mixed_two, grad_shared_in = mlp_back(
        meta, cotangent, mixed_two, w_mlp_in_two, w_mlp_out_two
    )
    grad_mlp_out_two = weight_grad(
        meta, hid_keep_two, *near(hid_send_two), cotangent, *near(cotangent)
    )
    logits = jnp.dot(normed_three, router_full, preferred_element_type=jnp.float32)
    picked = jnp.sum(jnp.where(chosen, logits[:, None, :], 0.0), axis=-1)
    gate_probs = jax.nn.softmax(picked, axis=-1)
    rows_sent, grad_shared_in, grad_mlp_out_two, gate_probs = lax.optimization_barrier(
        (rows_sent, grad_shared_in, grad_mlp_out_two, gate_probs)
    )
    sum_mlp_out_two = add_arrived(grad_mlp_out_two)
    router_wide = jnp.pad(router_full, ((0, 0), (0, 128 - num_experts)))
    own_expert = ((own_ctx * fsdp_count + own_fsdp) // units).reshape(1)
    partial_rows, partial_back, kept_rows = experts(
        own_expert,
        to_units(rows_sent.reshape(slot_count, model_width)),
        grad_arrived,
        router_wide,
        arrived_ids,
        expert_w,
        expert_w_out,
    )
    arrived, grad_rows, hidden_rows, grad_gate, grad_up, dots = kept_rows
    dots = from_units(dots.reshape(units, num_experts, capacity))
    coarse = lax.optimization_barrier(dots.astype(jnp.bfloat16))
    payload = with_notes(
        from_units(partial_back).astype(jnp.bfloat16).reshape(num_experts, capacity, model_width),
        coarse,
        dots - coarse.astype(jnp.float32),
    )
    payload, kept_rows, partial_rows = lax.optimization_barrier((payload, kept_rows, partial_rows))
    arrived, grad_rows, hidden_rows, grad_gate, grad_up, _ = kept_rows
    back = dispatch(payload)
    grad_experts = jnp.stack(
        [
            jnp.einsum("rd,rf->df", left, right, preferred_element_type=jnp.float32)
            .astype(jnp.bfloat16)
            .reshape(fsdp_count, shard_width, hid_unit)
            for left, right in ((arrived, grad_gate), (arrived, grad_up), (grad_rows, hidden_rows))
        ],
        axis=1,
    )
    grad_mlp_in_two = weight_grad(
        meta, keep_two, *near(send_two), grad_mixed_two, *near(grad_mixed_two)
    )
    back, grad_experts, grad_mlp_in_two, sum_mlp_out_two = lax.optimization_barrier(
        (back, grad_experts, grad_mlp_in_two, sum_mlp_out_two)
    )
    grad_out = cotangent[0].astype(jnp.float32)
    stride = back.shape[1]
    notes = back[:, capacity : capacity + 2, :capacity].astype(jnp.float32)
    slot_dots = jnp.sum(notes, axis=1).reshape(1, slot_count)
    grad_gates = jnp.stack(
        [
            jnp.sum(
                jnp.where(slots[None, :] == slot_target[:, k, None], slot_dots, 0.0), axis=-1
            )
            for k in range(TOP)
        ],
        axis=1,
    )
    grad_picked = gate_probs * (
        grad_gates - jnp.sum(gate_probs * grad_gates, axis=-1, keepdims=True)
    )
    grad_logits = jnp.sum(jnp.where(chosen, grad_picked[..., None], 0.0), axis=1)
    grad_router = jnp.einsum(
        "te,td->ed", grad_logits, normed_three.astype(jnp.float32), precision=HIGHEST
    )
    wide = jnp.arange(num_experts * stride, dtype=jnp.int32)[None, :]
    wide_target = slot_target + (stride - capacity) * routes[0]
    spread = (wide == wide_target[:, 0, None]) | (wide == wide_target[:, 1, None])
    grad_normed = (
        grad_shared_in
        + jnp.dot(
            spread.astype(jnp.bfloat16),
            back.reshape(num_experts * stride, model_width),
            preferred_element_type=jnp.float32,
        )
        + jnp.einsum(
            "te,de->td", grad_logits, router_full.astype(jnp.float32), precision=HIGHEST
        )
    )
    grad_heads, grad_resid, branch, gain_three = post_back(
        meta, after_two, gains[3], grad_out, grad_normed, w_attn_out_two
    )
    grad_heads = exchange(grad_heads)
    grad_attn_out_two = weight_grad(
        meta, att_keep_two, *near(att_send_two), branch, *near(branch)
    )
    grad_heads, grad_attn_out_two = lax.optimization_barrier((grad_heads, grad_attn_out_two))
    grad_q, own, others = attend_back(
        meta, kept_two[2], grad_heads, kept_two[3], kept_two[4], count
    )
    arrived_kv = [swap(values, "ctx", part + 1) for part, values in enumerate(others)]
    sum_mlp_in_two = add_arrived(grad_mlp_in_two)
    sum_attn_out_two = add_arrived(grad_attn_out_two)
    arrived_kv, grad_experts, *sums_two = lax.optimization_barrier(
        (arrived_kv, grad_experts, sum_mlp_in_two, sum_mlp_out_two, sum_attn_out_two)
    )
    sums_two = total(0, sums_two)
    grad_qkv = exchange(merge(meta, grad_q, own, arrived_kv))
    expert_rows = from_units(partial_rows).astype(jnp.bfloat16)
    grad_qkv, expert_rows = lax.optimization_barrier((grad_qkv, expert_rows))
    grad_experts = lax.all_to_all(grad_experts, "fsdp", 0, 0, tiled=True)
    grad_mixed, grad_resid, gain_two = pre_back(
        meta, middle, gains[2], tables, grad_resid, grad_qkv, w_attn_in_two
    )
    branch = grad_resid.astype(jnp.bfloat16)[None]
    grad_mixed_one, grad_normed = mlp_back(
        meta, branch, mixed_one, w_mlp_in_one, w_mlp_out_one
    )
    near_mixed = near(grad_mixed, branch, grad_mixed_one)
    grad_heads, grad_resid, att_branch, gain_one = post_back(
        meta, after_one, gains[1], grad_resid, grad_normed, w_attn_out_one
    )
    near_branch = near(att_branch)[0]
    grad_heads = exchange(grad_heads)
    grad_mlp_in_one = weight_grad(meta, keep_one, near_one[0], grad_mixed_one, near_mixed[2])
    grad_mlp_out_one = weight_grad(meta, hid_keep_one, near_one[2], branch, near_mixed[1])
    grad_heads, grad_mlp_out_one, grad_mlp_in_one = lax.optimization_barrier(
        (grad_heads, grad_mlp_out_one, grad_mlp_in_one)
    )
    grad_q, own, others = attend_back(
        meta, kept_one[2], grad_heads, kept_one[3], kept_one[4], count
    )
    arrived_kv = [swap(values, "ctx", part + 1) for part, values in enumerate(others)]
    grad_attn_in_two = weight_grad(
        meta, kept_two[0], *near(kept_two[1]), grad_mixed, near_mixed[0]
    )
    grad_attn_out_one = weight_grad(meta, att_keep_one, near_one[1], att_branch, near_branch)
    arrived_kv, grad_attn_in_two, grad_attn_out_one, grad_experts = lax.optimization_barrier(
        (arrived_kv, grad_attn_in_two, grad_attn_out_one, grad_experts)
    )
    grad_qkv = exchange(merge(meta, grad_q, own, arrived_kv))
    sums_one = [
        add_arrived(g)
        for g in (grad_attn_in_two, grad_mlp_in_one, grad_mlp_out_one, grad_attn_out_one)
    ]
    grad_experts = jnp.transpose(grad_experts, (1, 2, 0, 3)).astype(jnp.float32)
    grad_experts = grad_experts.reshape(3, shard_width, hid_unit * fsdp_count)
    grad_qkv, sums_two, expert_rows, grad_experts, *sums_one = lax.optimization_barrier(
        (grad_qkv, sums_two, expert_rows, grad_experts, *sums_one)
    )
    sums_one = total(1, sums_one)
    grad_mixed, grad_resid, gain_zero = pre_back(
        meta, resid_in, gains[0], tables, grad_resid, grad_qkv, w_attn_in_one
    )
    grad_attn_in_one = weight_grad(
        meta, kept_one[0], *near(kept_one[1]), grad_mixed, *near(grad_mixed)
    )
    grad_attn_in_one, expert_rows = lax.optimization_barrier((grad_attn_in_one, expert_rows))
    expert_rows = dispatch(expert_rows.reshape(num_experts, capacity, model_width))
    expert_rows = expert_rows.reshape(slot_count, model_width)
    back_rows = [jnp.dot(p, expert_rows, preferred_element_type=jnp.float32) for p in of_token]
    output = shared + sum(gate_probs[:, k, None] * back_rows[k] for k in range(TOP))
    small_grads = total_small(
        jnp.concatenate([gain_zero, gain_one, gain_two, gain_three, grad_router])
    )
    small_grads = lax.dynamic_slice_in_dim(small_grads, own_fsdp * shard_width, shard_width, 1)
    attn_in_grad, sums_one = reduce_last(
        at_ctx,
        grad_attn_in_one[0],
        swap(grad_attn_in_one[1], "fsdp", 2),
        sums_one[0],
        sums_one,
    )
    dense_grads = [attn_in_grad] + [
        jnp.stack(pair).astype(jnp.float32)
        for pair in (
            (sums_one[3], sums_two[2]),
            (sums_one[1], sums_two[0]),
            (sums_one[2], sums_two[1]),
        )
    ]
    return (
        output[None],
        grad_resid[None],
        dense_grads[0],
        dense_grads[1],
        small_grads[:4].reshape(2, 2, shard_width),
        dense_grads[2],
        dense_grads[3],
        small_grads[4:].T,
        jnp.swapaxes(grad_experts[:2], 1, 2),
        grad_experts[2].T,
    )


def solution(mesh):
    placed = (
        P("fsdp", "ctx", None),
        P("fsdp", "ctx", None),
        P("fsdp", None),
        P("fsdp", None),
        P("fsdp", "ctx", None),
        P(None, "fsdp", None),
        P(None, "fsdp", None),
        P(None, None, "fsdp"),
        P(None, "fsdp", None),
        P(None, "fsdp", None),
        P("fsdp", None),
        P(None, "ctx", "fsdp"),
        P("ctx", "fsdp"),
    )
    return jax.shard_map(
        per_device,
        mesh=mesh,
        in_specs=placed,
        out_specs=(
            P("fsdp", "ctx", None),
            P("fsdp", "ctx", None),
            P(None, "fsdp", None),
            P(None, "fsdp", None),
            P(None, None, "fsdp"),
            P(None, "fsdp", None),
            P(None, "fsdp", None),
            P("fsdp", None),
            P(None, "ctx", "fsdp"),
            P("ctx", "fsdp"),
        ),
        check_vma=False,
    )
```

```python
import functools
import math

import jax
import jax.numpy as jnp
from jax import lax
from jax.experimental import pallas as pl
from jax.experimental.pallas import tpu as pltpu
from jax.sharding import PartitionSpec as P

HEADS = 12
HD = 64
FF = 2048
TOP = 2
HEAD_GROUPS = 4
KEY_SPAN = 512
VMEM_LIMIT = 60 * 1024 * 1024


HIGHEST = lax.Precision.HIGHEST
EPSILON = 1e-06
NEGATIVE = -1e30


BOTH = ("ctx", "fsdp")


def swap(values, axis, mask):
    count = lax.axis_size(axis)
    return lax.ppermute(values, axis, [(i, i ^ mask) for i in range(count)])


def gather_shards(shard):
    near = swap(shard, "fsdp", 1)
    far = swap(shard, "fsdp", 2)
    return (shard, near, far, swap(far, "fsdp", 1))


def in_order(shards):
    own = lax.axis_index("fsdp")
    buffer = jnp.zeros((len(shards),) + shards[0].shape, shards[0].dtype)
    for k, shard in enumerate(shards):
        buffer = lax.dynamic_update_index_in_dim(buffer, shard, own ^ k, 0)
    return buffer


NT = (((1,), (1,)), ((), ()))


def _dot(a, b):
    return jnp.dot(a, b, preferred_element_type=jnp.float32)


def _dot_nt(a, b):
    return lax.dot_general(a, b, NT, preferred_element_type=jnp.float32)


def _flip(values):
    return values.astype(jnp.float32).T.astype(values.dtype)


def _shape(shape, dtype=jnp.bfloat16):
    return jax.ShapeDtypeStruct(shape, dtype)


def _whole(shape):
    return pl.BlockSpec(tuple(shape), lambda *_: (0,) * len(shape))


def operands(shards, part=None):
    if isinstance(shards, (tuple, list)):
        arrays, rows, place = shards, shards[0].shape[0], lambda m, k: 0
    else:
        arrays, rows, place = (shards,) * 4, shards.shape[0] // 4, lambda m, k: m[0] ^ k
    width = arrays[0].shape[1]
    if part is None:
        specs = [
            pl.BlockSpec((rows, width), lambda i, m, k=k: (place(m, k), 0)) for k in range(4)
        ]
    else:
        size, first = part
        specs = [
            pl.BlockSpec((rows, size), lambda i, m, k=k: (place(m, k), first + (m[0] ^ i)))
            for k in range(4)
        ]
    return list(arrays), specs


def call(body, meta, inputs, outputs, scratch=(), flops=0, in_specs=None, out_specs=None, grid=(1,)):
    moved = sum(math.prod(a.shape) * a.dtype.itemsize for a in (*inputs, *outputs))
    return pl.pallas_call(
        body,
        grid_spec=pltpu.PrefetchScalarGridSpec(
            num_scalar_prefetch=1,
            grid=grid,
            in_specs=in_specs or [_whole(a.shape) for a in inputs],
            out_specs=out_specs or [_whole(a.shape) for a in outputs],
            scratch_shapes=list(scratch),
        ),
        out_shape=list(outputs),
        compiler_params=pltpu.CompilerParams(vmem_limit_bytes=VMEM_LIMIT),
        cost_estimate=pl.CostEstimate(flops=flops, bytes_accessed=moved, transcendentals=0),
    )(meta, *inputs)


def _stack(refs, cols=slice(None)):
    return jnp.concatenate([w[:, cols] for w in refs], axis=0)


def _mine(blocks, own):
    return jnp.concatenate([blocks[own ^ k] for k in range(4)], axis=1)


def _norm(rows, gain):
    inverse = lax.rsqrt(jnp.mean(rows * rows, axis=-1, keepdims=True) + EPSILON)
    return rows * inverse * gain


def _norm_back(rows, gain, grad):
    inverse = lax.rsqrt(jnp.mean(rows * rows, axis=-1, keepdims=True) + EPSILON)
    weighted = grad * gain
    scaled = rows * inverse
    back = inverse * (weighted - scaled * jnp.mean(weighted * scaled, axis=-1, keepdims=True))
    return back, jnp.sum(grad * scaled, axis=0, keepdims=True)


def _split(rows, blocks):
    width = rows.shape[1] // len(blocks)
    for b, ref in enumerate(blocks):
        ref[...] = rows[:, b * width : (b + 1) * width]


def _turn(rows, cosine, sine, sign):
    lane = lax.broadcasted_iota(jnp.int32, cosine.shape, 1)
    low = lane % HD < HD // 2
    turned = []
    for b in range(rows.shape[1] // 128):
        part = rows[:, b * 128 : (b + 1) * 128]
        other = jnp.where(low, pltpu.roll(part, 128 - HD // 2, 1), pltpu.roll(part, HD // 2, 1))
        turned.append(part * cosine + sign * (other * sine))
    return jnp.concatenate(turned, axis=1)


def _pre_kernel(meta, x, gain, cosine, sine, w0, w1, w2, w3, keep, send, *rest):
    qkv, (blocks, heads) = rest[:4], rest[4:]
    own, line = meta[0], meta[1]
    width = x.shape[1]
    normed = _norm(x[...], gain[...]).astype(jnp.bfloat16)
    _split(normed, [blocks.at[b] for b in range(4)])
    for j in range(2):
        keep[j] = blocks[own ^ (2 * j)]
        send[j] = blocks[own ^ (2 * j + 1)]
    piece = x.shape[0] // 2
    mine = _mine(blocks, own)
    for kind in range(3):
        mixed = _dot(mine, _stack((w0, w1, w2, w3), slice(kind * width, (kind + 1) * width)))
        if kind < 2:
            mixed = _turn(mixed, cosine[...], sine[...], 1.0)
        if kind == 0:
            mixed = mixed * 0.125
        turned = mixed.T.astype(jnp.bfloat16)
        block = width // 4
        for b in range(4):
            for p in range(2):
                heads[b, p, kind] = turned[
                    b * block : (b + 1) * block, p * piece : (p + 1) * piece
                ]
    for k in range(4):
        qkv[k][...] = heads[line ^ k]


def pre(meta, x, gain, tables, shards):
    rows, width = x.shape
    block = width // 4
    outs = [_shape((2, rows, block))] * 2 + [_shape((2, 3, block, rows // 2))] * 4
    shards, specs = operands(shards)
    inputs = (x, gain, *tables)
    got = call(
        _pre_kernel,
        meta,
        (*inputs, *shards),
        outs,
        [
            pltpu.VMEM((4, rows, block), jnp.bfloat16),
            pltpu.VMEM((4, 2, 3, block, rows // 2), jnp.bfloat16),
        ],
        flops=6 * rows * width * width,
        in_specs=[_whole(a.shape) for a in inputs] + specs,
    )
    return got[0], got[1], got[2:6]


def _pre_back_kernel(meta, x, gain, cosine, sine, resid, *rest):
    qkv, w = rest[:4], rest[4:8]
    mixed_out, resid_out, gain_out, heads, blocks = rest[8:]
    own, line = meta[0], meta[1]
    width = x.shape[1]
    for k in range(4):
        heads[line ^ k] = qkv[k][...]
    for kind in range(3):
        mixed = jnp.concatenate(
            [
                jnp.concatenate([heads[b, p, kind] for b in range(4)], axis=0)
                for p in range(2)
            ],
            axis=1,
        )
        mixed = mixed.astype(jnp.float32).T
        if kind < 2:
            mixed = mixed * (0.125 if kind == 0 else 1.0)
            mixed = _turn(mixed, cosine[...], sine[...], -1.0)
        mixed_out[0, :, kind * width : (kind + 1) * width] = mixed.astype(jnp.bfloat16)
    grads = _dot_nt(mixed_out[0], _stack(w))
    _split(grads, [blocks.at[own ^ k] for k in range(4)])
    grad = jnp.concatenate([blocks[b] for b in range(4)], axis=1)
    back, grad_gain = _norm_back(x[...], gain[...], grad)
    resid_out[...] = resid[...] + back
    gain_out[...] = grad_gain


def pre_back(meta, x, gain, tables, resid, qkv, shards):
    rows, width = x.shape
    shards, specs = operands(shards)
    inputs = (x, gain, *tables, resid, *qkv)
    return call(
        _pre_back_kernel,
        meta,
        (*inputs, *shards),
        [
            _shape((1, rows, 3 * width)),
            _shape((rows, width), jnp.float32),
            _shape((1, width), jnp.float32),
        ],
        [
            pltpu.VMEM((4, 2, 3, width // 4, rows // 2), jnp.bfloat16),
            pltpu.VMEM((4, rows, width // 4), jnp.float32),
        ],
        flops=6 * rows * width * width,
        in_specs=[_whole(a.shape) for a in inputs] + specs,
    )


def _post_kernel(meta, x, gain, o0, o1, o2, o3, w0, w1, w2, w3, *rest):
    after, plain, blocks_out, keep, send, att_keep, att_send, att = rest
    own, line = meta[0], meta[1]
    piece = x.shape[0] // 2
    for k, o in enumerate((o0, o1, o2, o3)):
        for p in range(2):
            att[line ^ k, p * piece : (p + 1) * piece, :] = _flip(o[p])
    for j in range(2):
        att_keep[j] = att[own ^ (2 * j)]
        att_send[j] = att[own ^ (2 * j + 1)]
    rows = x[...] + _dot(_mine(att, own), _stack((w0, w1, w2, w3)))
    after[...] = rows
    normed = _norm(rows, gain[...]).astype(jnp.bfloat16)
    plain[...] = normed
    _split(normed, [att.at[b] for b in range(4)])
    blocks_out[...] = att[...]
    for j in range(2):
        keep[j] = att[own ^ (2 * j)]
        send[j] = att[own ^ (2 * j + 1)]


def post(meta, x, gain, heads, shards):
    rows, width = x.shape
    block = width // 4
    shards, specs = operands(shards)
    inputs = (x, gain, *heads)
    return call(
        _post_kernel,
        meta,
        (*inputs, *shards),
        [_shape((rows, width), jnp.float32), _shape((rows, width)), _shape((4, rows, block))]
        + [_shape((2, rows, block))] * 4,
        [pltpu.VMEM((4, rows, block), jnp.bfloat16)],
        flops=2 * rows * width * width,
        in_specs=[_whole(a.shape) for a in inputs] + specs,
    )


def _post_back_kernel(meta, x, gain, resid, grad, w0, w1, w2, w3, *rest):
    heads, (resid_out, branch, gain_out, att) = rest[:4], rest[4:]
    own, line = meta[0], meta[1]
    back, grad_gain = _norm_back(x[...], gain[...], grad[...])
    gain_out[...] = grad_gain
    rows = resid[...] + back
    resid_out[...] = rows
    rows = rows.astype(jnp.bfloat16)
    branch[0] = rows
    grads = _dot_nt(rows, _stack((w0, w1, w2, w3))).astype(jnp.bfloat16)
    _split(grads, [att.at[own ^ k] for k in range(4)])
    piece = x.shape[0] // 2
    for k in range(4):
        for p in range(2):
            heads[k][p] = _flip(att[line ^ k, p * piece : (p + 1) * piece, :])


def post_back(meta, x, gain, resid, grad, shards):
    rows, width = x.shape
    block = width // 4
    shards, specs = operands(shards)
    inputs = (x, gain, resid, grad)
    got = call(
        _post_back_kernel,
        meta,
        (*inputs, *shards),
        [_shape((2, block, rows // 2))] * 4
        + [
            _shape((rows, width), jnp.float32),
            _shape((1, rows, width)),
            _shape((1, width), jnp.float32),
        ],
        [pltpu.VMEM((4, rows, block), jnp.bfloat16)],
        flops=2 * rows * width * width,
        in_specs=[_whole(a.shape) for a in inputs] + specs,
    )
    return got[:4], got[4], got[5], got[6]


def _mlp_kernel(meta, x, blocks, *rest):
    gates, ups, downs = rest[:4], rest[4:8], rest[8:12]
    out, mixed, keep, send, acc = rest[12:]
    own, step = meta[0], pl.program_id(0)
    rows = _mine(blocks, own)
    gate = _dot(rows, _stack(gates))
    up = _dot(rows, _stack(ups))
    mixed[0], mixed[1] = gate, up
    hidden = (gate * jax.nn.sigmoid(gate) * up).astype(jnp.bfloat16)
    for k in range(4):

        @pl.when(step == k)
        def _(k=k):
            (send if k % 2 else keep)[k // 2] = hidden
            part = _dot(hidden, downs[k][...])
            if k == 0:
                acc[...] = x[...] + part
            elif k < 3:
                acc[...] += part
            else:
                out[...] = acc[...] + part


def mlp_width(shards):
    first = shards[0] if isinstance(shards, (tuple, list)) else shards
    return first.shape[1] // 2


def mlp(meta, x, blocks, shards_in, shards_out):
    rows, width = x.shape
    hidden = mlp_width(shards_in)
    part = hidden // 4
    gates, gate_specs = operands(shards_in, (part, 0))
    ups, up_specs = operands(shards_in, (part, 4))
    downs, down_specs = operands(shards_out)
    return call(
        _mlp_kernel,
        meta,
        (x, blocks, *gates, *ups, *downs),
        [
            _shape((rows, width), jnp.float32),
            _shape((2, rows, hidden), jnp.float32),
            _shape((2, rows, part)),
            _shape((2, rows, part)),
        ],
        [pltpu.VMEM((rows, width), jnp.float32)],
        flops=6 * rows * width * hidden,
        in_specs=[_whole(x.shape), _whole(blocks.shape), *gate_specs, *up_specs, *down_specs],
        out_specs=[
            _whole((rows, width)),
            pl.BlockSpec((2, rows, part), lambda i, m: (0, 0, m[0] ^ i)),
            _whole((2, rows, part)),
            _whole((2, rows, part)),
        ],
        grid=(4,),
    )


def _mlp_back_kernel(meta, branch, mixed, *rest):
    gates, ups, downs = rest[:4], rest[4:8], rest[8:12]
    grad_mixed, grad_out, grad_hidden, acc, turned = rest[12:]
    own, step = meta[0], pl.program_id(0)
    for k in range(4):

        @pl.when(step == k)
        def _(k=k):
            grad_hidden[...] = _dot_nt(branch[0], downs[k][...]).astype(jnp.bfloat16)

    grad_h = grad_hidden[...].astype(jnp.float32)
    gate, up = mixed[0], mixed[1]
    sigmoid = jax.nn.sigmoid(gate)
    grad_gate = (grad_h * up * sigmoid * (1.0 + gate * (1.0 - sigmoid))).astype(jnp.bfloat16)
    grad_up = (grad_h * gate * sigmoid).astype(jnp.bfloat16)
    grad_mixed[0], grad_mixed[1] = grad_gate, grad_up
    part = _dot_nt(grad_gate, _stack(gates)) + _dot_nt(grad_up, _stack(ups))

    @pl.when(step == 0)
    def _():
        acc[...] = part

    @pl.when((step > 0) & (step < 3))
    def _():
        acc[...] += part

    @pl.when(step == 3)
    def _():
        _split(acc[...] + part, [turned.at[own ^ k] for k in range(4)])
        grad_out[...] = jnp.concatenate([turned[b] for b in range(4)], axis=1)


def mlp_back(meta, branch, mixed, shards_in, shards_out):
    _, rows, width = branch.shape
    hidden = mixed.shape[2]
    part = hidden // 4
    block = width // 4
    gates, gate_specs = operands(shards_in, (part, 0))
    ups, up_specs = operands(shards_in, (part, 4))
    downs, down_specs = operands(shards_out)
    return call(
        _mlp_back_kernel,
        meta,
        (branch, mixed, *gates, *ups, *downs),
        [_shape((2, rows, hidden)), _shape((rows, width), jnp.float32)],
        [
            pltpu.VMEM((rows, part), jnp.bfloat16),
            pltpu.VMEM((rows, width), jnp.float32),
            pltpu.VMEM((4, rows, block), jnp.float32),
        ],
        flops=6 * rows * width * hidden,
        in_specs=[
            _whole(branch.shape),
            pl.BlockSpec((2, rows, part), lambda i, m: (0, 0, m[0] ^ i)),
            *gate_specs,
            *up_specs,
            *down_specs,
        ],
        out_specs=[
            pl.BlockSpec((2, rows, part), lambda i, m: (0, 0, m[0] ^ i)),
            _whole((rows, width)),
        ],
        grid=(4,),
    )


def _grad_kernel(meta, left, left_near, right, right_near, own, send, flipped):
    rows, depth = left.shape[1:]

    @pl.when((pl.program_id(0) == 0) & (pl.program_id(1) == 0))
    def _():
        for j in range(2):
            flipped[j * depth : (j + 1) * depth, :rows] = _flip(left[j])
            flipped[j * depth : (j + 1) * depth, rows:] = _flip(left_near[j])

    both = jnp.concatenate([right[0], right_near[0]], axis=0)
    grads = _dot(flipped[...], both).astype(jnp.bfloat16)
    own[...] = grads[:depth]
    send[...] = grads[depth:]


def weight_grad(meta, left, left_near, right, right_near):
    groups, rows, width = right.shape
    depth = left.shape[2]
    chunk = 512 if width % 768 else 768
    steps = width // chunk
    right_spec = pl.BlockSpec((1, rows, chunk), lambda g, i, m: (g, 0, i))
    out_spec = pl.BlockSpec((depth, chunk), lambda g, i, m: (0, g * steps + i))
    return call(
        _grad_kernel,
        meta,
        (left, left_near, right, right_near),
        [_shape((depth, groups * width))] * 2,
        [pltpu.VMEM((2 * depth, 2 * rows), jnp.bfloat16)],
        flops=8 * rows * depth * groups * width,
        in_specs=[_whole(left.shape), _whole(left.shape), right_spec, right_spec],
        out_specs=[out_spec, out_spec],
        grid=(groups, steps),
    )


def _mask(first_key, keys, query_pos, query_start, copies):
    key_pos = first_key + lax.broadcasted_iota(jnp.int32, (keys, query_pos.shape[1]), 0)
    allowed = (key_pos <= query_pos) & (key_pos >= query_start)
    return jnp.concatenate([allowed] * copies, axis=1)


def _tables(meta, parts):
    return (lambda s: meta[2 + s], lambda k: meta[2 + 8 * parts + k])


def _query_geometry(place, ends, count, piece, key_span):
    query_pos = place * piece + lax.broadcasted_iota(jnp.int32, (1, piece), 1)
    query_start = jnp.zeros_like(query_pos)
    first = place * piece
    least = jnp.int32(0)
    for k in range(count):
        last = k == count - 1
        query_start = jnp.where(query_pos >= ends(k), query_pos if last else ends(k), query_start)
        least = jnp.where(first >= ends(k), first if last else ends(k), least)
    return (query_pos, query_start, least // key_span, (first + piece - 1) // key_span + 1)


def _stack_heads(rows, heads):
    head_dim = rows.shape[0] // heads
    head = lax.broadcasted_iota(jnp.int32, rows.shape, 0) // head_dim
    zero = jnp.zeros_like(rows)
    return jnp.concatenate([jnp.where(head == h, rows, zero) for h in range(heads)], axis=1)


def _own_heads(acc, heads, piece):
    head_dim = acc.shape[0] // heads
    return jnp.concatenate(
        [
            acc[h * head_dim : (h + 1) * head_dim, h * piece : (h + 1) * piece]
            for h in range(heads)
        ],
        axis=0,
    )


def _attend_kernel(heads, count, key_span, parts, meta, *refs):
    inputs, o, (keep, lse, keys, values_t) = (
        refs[: 4 * parts],
        refs[4 * parts : 4 * parts + 4],
        refs[4 * parts + 4 :],
    )
    width, piece = inputs[0].shape[2:]
    place, ends = _tables(meta, parts)
    for s in range(8 * parts):
        at = pl.ds(pl.multiple_of(place(s) * piece, piece), piece)
        keys[at, :] = _flip(inputs[s // 2][s % 2, 1])
        values_t[:, at] = inputs[s // 2][s % 2, 2]
    cols = heads * piece
    for s in range(8):
        query_pos, query_start, begin, end = _query_geometry(
            place(s), ends, count, piece, key_span
        )
        stacked = _stack_heads(inputs[s // 2][s % 2, 0], heads)

        def advance(block, carried):
            run_max, run_sum, acc = carried
            first = pl.multiple_of(block * key_span, key_span)
            scores = _dot(keys[pl.ds(first, key_span), :], stacked)
            allowed = _mask(first, key_span, query_pos, query_start, heads)
            scores = jnp.where(allowed, scores, NEGATIVE)
            new_max = jnp.maximum(run_max, jnp.max(scores, axis=0, keepdims=True))
            weights = jnp.exp(scores - new_max)
            factor = jnp.exp(run_max - new_max)
            run_sum = run_sum * factor + jnp.sum(weights, axis=0, keepdims=True)
            part = _dot(values_t[:, pl.ds(first, key_span)], weights.astype(jnp.bfloat16))
            return (new_max, run_sum, acc * factor + part)

        run_max, run_sum, acc = lax.fori_loop(
            begin,
            end,
            advance,
            (
                jnp.full((1, cols), NEGATIVE, jnp.float32),
                jnp.zeros((1, cols), jnp.float32),
                jnp.zeros((width, cols), jnp.float32),
            ),
        )
        kept = _own_heads(acc / run_sum, heads, piece)
        keep[s] = kept
        o[s // 2][s % 2] = kept.astype(jnp.bfloat16)
        lse[s] = run_max + jnp.log(run_sum)


def attend(meta, inputs, count):
    _, _, width, piece = inputs[0].shape
    heads = width // HD
    parts = len(inputs) // 4
    slots = parts * 8 * piece
    got = call(
        functools.partial(_attend_kernel, heads, count, KEY_SPAN, parts),
        meta,
        inputs,
        [_shape((2, width, piece))] * 4
        + [_shape((8, width, piece), jnp.float32), _shape((8, 1, heads * piece), jnp.float32)],
        [
            pltpu.VMEM((slots, width), jnp.bfloat16),
            pltpu.VMEM((width, slots), jnp.bfloat16),
        ],
        flops=32 * piece * slots * width,
    )
    return got[:4], got[4], got[5]


def _attend_back_kernel(heads, count, key_span, parts, meta, *refs):
    inputs, grads, (keep, lse), rest = (
        refs[: 4 * parts],
        refs[4 * parts : 4 * parts + 4],
        refs[4 * parts + 4 : 4 * parts + 6],
        refs[4 * parts + 6 :],
    )
    gq, gkv = rest[0], rest[1 : 1 + parts]
    keys, keys_t, values, gkeys, gvalues = rest[1 + parts :]
    width, piece = inputs[0].shape[2:]
    head_dim = width // heads
    place, ends = _tables(meta, parts)
    for s in range(8 * parts):
        at = pl.ds(pl.multiple_of(place(s) * piece, piece), piece)
        key_rows = inputs[s // 2][s % 2, 1]
        keys_t[:, at] = key_rows
        keys[at, :] = _flip(key_rows)
        values[at, :] = _flip(inputs[s // 2][s % 2, 2])
    gkeys[...] = jnp.zeros_like(gkeys)
    gvalues[...] = jnp.zeros_like(gvalues)
    for s in range(8):
        query_pos, query_start, begin, end = _query_geometry(
            place(s), ends, count, piece, key_span
        )
        stacked = _stack_heads(inputs[s // 2][s % 2, 0], heads)
        grad = grads[s // 2][s % 2]
        grad_stacked = _stack_heads(grad, heads)
        product = grad.astype(jnp.float32) * keep[s]
        delta = jnp.concatenate(
            [
                jnp.sum(product[h * head_dim : (h + 1) * head_dim, :], axis=0, keepdims=True)
                for h in range(heads)
            ],
            axis=1,
        )
        log_sum = lse[s]

        def retreat(block, acc):
            first = pl.multiple_of(block * key_span, key_span)
            at = pl.ds(first, key_span)
            scores = _dot(keys[at, :], stacked)
            allowed = _mask(first, key_span, query_pos, query_start, heads)
            probs = jnp.where(allowed, jnp.exp(scores - log_sum), 0.0)
            grad_probs = _dot(values[at, :], grad_stacked)
            grad_scores = (probs * (grad_probs - delta)).astype(jnp.bfloat16)
            gvalues[:, at] += _dot_nt(grad_stacked, probs.astype(jnp.bfloat16))
            gkeys[:, at] += _dot_nt(stacked, grad_scores)
            return acc + _dot(keys_t[:, at], grad_scores)

        acc = lax.fori_loop(begin, end, retreat, jnp.zeros((width, heads * piece), jnp.float32))
        gq[s] = _own_heads(acc, heads, piece).astype(jnp.bfloat16)
    for s in range(8 * parts):
        at = pl.ds(pl.multiple_of(place(s) * piece, piece), piece)
        out = gkv[s // 8]
        out[s % 8, 0] = gkeys[:, at].astype(out.dtype)
        out[s % 8, 1] = gvalues[:, at].astype(out.dtype)


def attend_back(meta, inputs, grads, keep, lse, count):
    _, _, width, piece = inputs[0].shape
    heads = width // HD
    parts = len(inputs) // 4
    slots = parts * 8 * piece
    got = call(
        functools.partial(_attend_back_kernel, heads, count, KEY_SPAN, parts),
        meta,
        (*inputs, *grads, keep, lse),
        [_shape((8, width, piece)), _shape((8, 2, width, piece), jnp.float32)]
        + [_shape((8, 2, width, piece))] * (parts - 1),
        [
            pltpu.VMEM((slots, width), jnp.bfloat16),
            pltpu.VMEM((width, slots), jnp.bfloat16),
            pltpu.VMEM((slots, width), jnp.bfloat16),
            pltpu.VMEM((width, slots), jnp.float32),
            pltpu.VMEM((width, slots), jnp.float32),
        ],
        flops=80 * piece * slots * width,
    )
    return got[0], got[1], got[2:]


def _merge_kernel(meta, gq, own, *rest):
    arrived, out = rest[:-4], rest[-4:]
    for s in range(8):
        total = own[s]
        for other in arrived:
            total = total + other[s].astype(jnp.float32)
        out[s // 2][s % 2, 0] = gq[s]
        out[s // 2][s % 2, 1:3] = total.astype(jnp.bfloat16)


def merge(meta, gq, own, arrived):
    _, width, piece = gq.shape
    return call(
        _merge_kernel, meta, (gq, own, *arrived), [_shape((2, 3, width, piece))] * 4
    )


def _halve_kernel(meta, first, second, sent, kept):
    summed = (first[...].astype(jnp.float32) + second[...].astype(jnp.float32)).astype(jnp.bfloat16)
    half = sent.shape[1]
    left, right = summed[:, :half], summed[:, half:]
    side = meta[0] == 0
    sent[...] = jnp.where(side, right, left)
    kept[...] = jnp.where(side, left, right)


def _quarter_kernel(meta, first, second, *rest):
    parts, summed = rest[:-1], rest[-1]
    summed[...] = (first[...].astype(jnp.float32) + second[...].astype(jnp.float32)).astype(
        jnp.bfloat16
    )
    chunk = parts[0].shape[0]
    for k, part in enumerate(parts):
        at = pl.multiple_of((meta[1] ^ k) * chunk, chunk)
        part[...] = summed[pl.ds(at, chunk), :]


def _place_kernel(meta, other, *refs):
    out, parts = refs[-1], refs[:-1]
    _, rows, width = out.shape
    lines = len(parts) // 2
    chunk, half = rows // lines, width // 2
    side = meta[0] == 0
    for k in range(lines):
        at = pl.multiple_of((meta[1] ^ k) * chunk, chunk)
        own = parts[k][...].astype(jnp.float32)
        near = parts[lines + k][...].astype(jnp.float32)
        out[0, pl.ds(at, chunk), :half] = jnp.where(side, own, near)
        out[0, pl.ds(at, chunk), half:] = jnp.where(side, near, own)
    out[1] = other[...].astype(jnp.float32)


def reduce_last(place, own, arrived, other, held, small):
    lines = lax.axis_size("ctx") // 2
    rows, width = own.shape
    chunk, half = rows // lines, width // 2
    if chunk % 16:
        summed = lax.psum(own + arrived, "ctx")
        return jnp.stack([summed, other]).astype(jnp.float32), held, total_small(small)
    sent, kept = call(_halve_kernel, place, (own, arrived), [_shape((rows, half))] * 2)
    kept, small = lax.optimization_barrier((kept, small))
    small = total_small(small)
    parts = call(
        _quarter_kernel,
        place,
        (kept, swap(sent, "ctx", 1)),
        [_shape((chunk, half))] * lines,
        [pltpu.VMEM((rows, half), jnp.bfloat16)],
    )
    summed = parts[0].astype(jnp.float32)
    for k in range(1, lines):
        summed = summed + swap(parts[k], "ctx", 2 * k).astype(jnp.float32)
    summed = summed.astype(jnp.bfloat16)
    column = [swap(summed, "ctx", 2 * k) if k else summed for k in range(lines)]
    column, held = lax.optimization_barrier((column, held))
    parts = column + [swap(c, "ctx", 1) for c in column]
    return (
        call(
            _place_kernel, place, (other, *parts), [_shape((2, rows, width), jnp.float32)]
        )[0],
        held,
        small,
    )


def _expert_kernel(units, meta, *refs):
    xs, cs = refs[:units], refs[units : 2 * units]
    router, ids, w = refs[2 * units : 2 * units + 3]
    outs = refs[2 * units + 3 :]
    parts, backs = outs[:units], outs[units : 2 * units]
    rows_out, grads_out, hidden_out, gate_out, up_out, dots_out = outs[2 * units : 2 * units + 6]
    gates, ups, downs, x, c = outs[2 * units + 6 :]
    step = pl.program_id(0)
    tiles = pl.num_programs(0) // units

    @pl.when(step == 0)
    def _():
        width = w.shape[2]
        for f in range(4):
            part = slice(f * width, (f + 1) * width)
            gates[part, :] = w[f, 0]
            ups[part, :] = w[f, 1]
            downs[part, :] = w[f, 2]

    for u in range(units):

        @pl.when(step // tiles == u)
        def _(u=u):
            x[...] = xs[u][...]
            c[...] = cs[u][...]

    rows = x[...]
    rows_out[...] = rows
    incoming = c[...].astype(jnp.float32)
    logits = _dot(rows, router[...])
    lane = lax.broadcasted_iota(jnp.int32, logits.shape, 1)
    gap = jnp.sum(
        jnp.where(lane == meta[0], logits, 0.0)
        - jnp.where(lane.astype(jnp.float32) == ids[...], logits, 0.0),
        axis=1,
        keepdims=True,
    )
    grads = (jax.nn.sigmoid(gap) * incoming).astype(jnp.bfloat16)
    grads_out[...] = grads
    gate = _dot(rows, gates[...])
    up = _dot(rows, ups[...])
    sigmoid = jax.nn.sigmoid(gate)
    silu = gate * sigmoid
    hidden = (silu * up).astype(jnp.bfloat16)
    hidden_out[...] = hidden
    part = _dot_nt(hidden, downs[...])
    dots_out[...] = jnp.sum(part * incoming, axis=1, keepdims=True)
    grad_h = _dot(grads, downs[...]).astype(jnp.bfloat16).astype(jnp.float32)
    grad_gate = (grad_h * up * sigmoid * (1.0 + gate * (1.0 - sigmoid))).astype(jnp.bfloat16)
    grad_up = (grad_h * silu).astype(jnp.bfloat16)
    gate_out[...] = grad_gate
    up_out[...] = grad_up
    back = _dot_nt(grad_gate, gates[...]) + _dot_nt(grad_up, ups[...])
    for u in range(units):

        @pl.when(step // tiles == u)
        def _(u=u):
            parts[u][...] = part.astype(jnp.bfloat16)
            backs[u][...] = back.astype(jnp.bfloat16)


def experts(meta, xs, cs, router, ids, w):
    units, (rows, width), tile = len(xs), xs[0].shape, 1024 // len(xs)
    tiles, hidden = rows // tile, w.shape[3]
    total_rows = units * rows
    slabs = [
        pl.BlockSpec((tile, width), lambda i, m, u=u: (jnp.clip(i - u * tiles, 0, tiles - 1), 0))
        for u in range(units)
    ]

    def rowed(columns):
        return pl.BlockSpec((tile, columns), lambda i, m: (i, 0))

    got = call(
        functools.partial(_expert_kernel, units),
        meta,
        (*xs, *cs, router, ids, w),
        [_shape((rows, width))] * (2 * units)
        + [_shape((total_rows, width))] * 2
        + [_shape((total_rows, hidden))] * 3
        + [_shape((total_rows, 1), jnp.float32)],
        [pltpu.VMEM((width, hidden), jnp.bfloat16)] * 3
        + [pltpu.VMEM((tile, width), jnp.bfloat16)] * 2,
        flops=12 * total_rows * width * hidden,
        in_specs=slabs
        + slabs
        + [_whole(router.shape), rowed(1), _whole(w.shape)],
        out_specs=slabs + slabs + [rowed(width)] * 2 + [rowed(hidden)] * 3 + [rowed(1)],
        grid=(units * tiles,),
    )
    return got[:units], got[units : 2 * units], got[2 * units :]


def layout(lengths_row, order_row, piece_len):
    all_slots = order_row.shape[0] * piece_len
    position = (
        order_row[:, None] * piece_len + jnp.arange(piece_len, dtype=jnp.int32)[None, :]
    ).reshape(all_slots)
    count = jnp.arange(lengths_row.shape[0], dtype=jnp.int32)
    seq_ends = jnp.sum(
        jnp.where(count[:, None] <= count[None, :], lengths_row[:, None], 0), axis=0, dtype=jnp.int32
    )
    segment = jnp.sum(
        (position[:, None] >= seq_ends[None, :]).astype(jnp.int32), axis=1, dtype=jnp.int32
    )
    seq_start = jnp.sum(
        jnp.where(segment[:, None] > count[None, :], lengths_row[None, :], 0),
        axis=1,
        dtype=jnp.int32,
    )
    return (seq_ends, position - seq_start)


def angles(offset):
    freq_table = jnp.exp(
        jnp.arange(HD // 2, dtype=jnp.float32) * (-2.0 * math.log(10000.0) / HD)
    )
    theta = offset.astype(jnp.float32)[..., None] * freq_table
    cosine, sine = jnp.cos(theta), jnp.sin(theta)
    return (
        jnp.tile(cosine, (1, 256 // HD)),
        jnp.tile(jnp.concatenate([-sine, sine], axis=1), (1, 128 // HD)),
    )


def hidden_back(gate_pre, up_pre, grad_hidden):
    sigmoid_gate = jax.nn.sigmoid(gate_pre)
    grad_gate = grad_hidden * up_pre * sigmoid_gate * (1.0 + gate_pre * (1.0 - sigmoid_gate))
    grad_up = grad_hidden * gate_pre * sigmoid_gate
    return (grad_gate.astype(jnp.bfloat16), grad_up.astype(jnp.bfloat16))


def head_parts():
    return lax.axis_size("ctx") // HEAD_GROUPS


def exchange(values):
    return [values[0]] + [swap(values[k], "ctx", k * head_parts()) for k in range(1, 4)]


def attend_forward(meta, count, resid, gain, tables, w_in, early):
    keep, send, qkv = pre(meta, resid, gain, tables, w_in)
    qkv = exchange(qkv)
    inputs = list(qkv)
    for part in range(1, head_parts()):
        inputs += [swap(values, "ctx", part) for values in qkv]
    inputs, early = lax.optimization_barrier((inputs, early))
    heads, acc, lse = attend(meta, inputs, count)
    return heads, (keep, send, inputs, acc, lse), early


def near(*values):
    return [swap(v, "fsdp", 1) for v in values]


def add_arrived(grads):
    return grads[0] + swap(grads[1], "fsdp", 2)


def total(bucket, grads):
    count = lax.axis_size("ctx")
    ring = [[(i + bucket) % count for i in range(count)]]
    return lax.psum(tuple(grads), "ctx", axis_index_groups=ring)


def total_small(values):
    for axis in BOTH:
        step = 1
        while step < lax.axis_size(axis):
            values = values + swap(values, axis, step)
            step *= 2
    return values


def per_device(
    tokens,
    cotangent,
    lengths,
    piece_order,
    routes,
    attn_in,
    attn_out,
    norm_gain,
    mlp_in,
    mlp_out,
    router,
    expert_in,
    expert_out,
):
    tok_rows, model_width = tokens.shape[1:]
    shard_width = router.shape[0]
    num_experts = router.shape[1]
    own_ctx, own_fsdp = lax.axis_index("ctx"), lax.axis_index("fsdp")
    ctx_count, fsdp_count = lax.axis_size("ctx"), lax.axis_size("fsdp")
    units = ctx_count * fsdp_count // num_experts
    hid_unit = expert_out.shape[0] // fsdp_count
    members = [
        [i for i in range(ctx_count * fsdp_count) if i % units == lane] for lane in range(units)
    ]

    def dispatch(values):
        return lax.all_to_all(values, BOTH, 0, 0, tiled=True, axis_index_groups=members)

    def to_units(values):
        return [values] + [swap(values, BOTH, k) for k in range(1, units)]

    def from_units(partial):
        summed = partial[0].astype(jnp.float32)
        for k in range(1, units):
            summed = summed + swap(partial[k], BOTH, k).astype(jnp.float32)
        return summed

    def gathered(shard):
        return lax.all_gather(shard, "fsdp", axis=0, tiled=True)

    seq_ends, offset = layout(lengths[0], piece_order[0], tok_rows // 2)
    tables = angles(lax.dynamic_slice_in_dim(offset, own_ctx * tok_rows, tok_rows, 0))
    parts = ctx_count // HEAD_GROUPS
    line, side = own_ctx // parts, own_ctx % parts
    order = piece_order[0].reshape(HEAD_GROUPS, parts, 2)
    place = [order[line ^ k, side ^ part] for part in range(parts) for k in range(HEAD_GROUPS)]
    meta = jnp.concatenate([jnp.stack([own_fsdp, line]), jnp.concatenate(place), seq_ends])
    at_ctx = jnp.stack([own_ctx % 2, own_ctx // 2])
    count = lengths.shape[1]

    item_count = tok_rows * TOP
    capacity = 2 * item_count // num_experts
    slot_count = num_experts * capacity
    expert_ids = jnp.arange(num_experts, dtype=jnp.int32)
    chosen = routes[0][:, :, None] == expert_ids[None, None, :]
    flat_chosen = chosen.reshape(item_count, num_experts).astype(jnp.bfloat16)
    items = jnp.arange(item_count, dtype=jnp.int32)
    earlier = jnp.dot(
        (items[None, :] < items[:, None]).astype(jnp.bfloat16),
        flat_chosen,
        preferred_element_type=jnp.float32,
    )
    slot_rank = jnp.sum(earlier * flat_chosen.astype(jnp.float32), axis=1).astype(jnp.int32)
    slot_target = (routes[0].reshape(item_count) * capacity + slot_rank).reshape(tok_rows, TOP)
    slots = jnp.arange(slot_count, dtype=jnp.int32)
    at_slot = [slots[:, None] == slot_target[None, :, k] for k in range(TOP)]
    of_token = [(slots[None, :] == slot_target[:, k, None]).astype(jnp.bfloat16) for k in range(TOP)]
    fill = (at_slot[0] | at_slot[1]).astype(jnp.bfloat16)

    def to_slots(rows):
        return jnp.dot(fill, rows, preferred_element_type=jnp.float32).astype(jnp.bfloat16)

    def send_rows(rows):
        return dispatch(to_slots(rows).reshape(num_experts, capacity, model_width))

    other_ids = sum(
        jnp.sum(
            jnp.where(at_slot[k], routes[0][None, :, 1 - k].astype(jnp.float32), 0.0), axis=1
        )
        for k in range(TOP)
    )

    def with_notes(rows, *notes):
        extra = jnp.stack(notes, axis=1).astype(jnp.bfloat16)
        extra = jnp.pad(extra, ((0, 0), (0, 8 - len(notes)), (0, model_width - capacity)))
        return jnp.concatenate([rows, extra], axis=1)

    shard = attn_in[0]
    near_shard, far_shard = swap(shard, "fsdp", 1), swap(shard, "fsdp", 2)
    small = gather_shards(jnp.concatenate([norm_gain.reshape(4, shard_width), router.T], axis=0))
    ordered = []
    for i in range(4):
        block = small[3]
        for j in range(3):
            block = jnp.where(own_fsdp ^ j == i, small[j], block)
        ordered.append(block)
    small = jnp.concatenate(ordered, axis=1)
    gains = [small[i : i + 1].astype(jnp.float32) for i in range(4)]
    router_full = small[4:].T
    grad_rows = to_slots(cotangent[0]).reshape(num_experts, capacity, model_width)
    grad_sent = with_notes(grad_rows, other_ids.reshape(num_experts, capacity))
    stored = jnp.concatenate(
        [jnp.swapaxes(expert_in, 1, 2), jnp.swapaxes(expert_out, 0, 1)[None]]
    )
    expert_part = jnp.stack(
        [stored[:, :, f * hid_unit : (f + 1) * hid_unit] for f in range(fsdp_count)]
    )
    near_out, far_out = swap(attn_out[0], "fsdp", 1), swap(attn_out[0], "fsdp", 2)
    far_shard, tables, meta, gains, expert_part = lax.optimization_barrier(
        (far_shard, tables, meta, gains, expert_part)
    )
    w_attn_in_one = (shard, near_shard, far_shard, swap(far_shard, "fsdp", 1))
    own_out = attn_out[0]
    far_shard, far_out, attn_in, attn_out, mlp_in, mlp_out = lax.optimization_barrier(
        (far_shard, far_out, attn_in, attn_out, mlp_in, mlp_out)
    )
    w_attn_out_one = (own_out, near_out, far_out, swap(far_out, "fsdp", 1))
    w_mlp_in_one, w_mlp_out_one = gathered(mlp_in[0]), gathered(mlp_out[0])
    w_mlp_in_two, w_mlp_out_two = gathered(mlp_in[1]), gathered(mlp_out[1])

    resid_in = tokens[0].astype(jnp.float32)
    heads_one, kept_one, (grad_sent, attn_in, attn_out) = attend_forward(
        meta, count, resid_in, gains[0], tables, w_attn_in_one, (grad_sent, attn_in, attn_out)
    )
    far_in, far_out = swap(attn_in[1], "fsdp", 2), swap(attn_out[1], "fsdp", 2)
    grad_sent = dispatch(grad_sent)
    heads_one = exchange(heads_one)
    heads_one, far_in, far_out = lax.optimization_barrier((heads_one, far_in, far_out))
    w_attn_in_two, w_attn_out_two = [
        (own, swap(own, "fsdp", 1), far, swap(far, "fsdp", 1))
        for own, far in ((attn_in[1], far_in), (attn_out[1], far_out))
    ]
    after_one, _, blocks_one, keep_one, send_one, att_keep_one, att_send_one = post(
        meta, resid_in, gains[1], heads_one, w_attn_out_one
    )
    after_one, grad_sent, expert_part = lax.optimization_barrier(
        (after_one, grad_sent, expert_part)
    )
    expert_w = lax.all_to_all(expert_part, "fsdp", 0, 0, tiled=True)
    middle, mixed_one, hid_keep_one, hid_send_one = mlp(
        meta, after_one, blocks_one, w_mlp_in_one, w_mlp_out_one
    )
    near_one = near(send_one, att_send_one, hid_send_one)
    heads_two, kept_two, grad_sent = attend_forward(
        meta, count, middle, gains[2], tables, w_attn_in_two, grad_sent
    )
    grad_arrived = to_units(grad_sent[:, :capacity].reshape(slot_count, model_width))
    arrived_ids = jnp.concatenate(
        to_units(grad_sent[:, capacity, :capacity].astype(jnp.float32))
    ).reshape(-1, 1)
    heads_two, grad_arrived, arrived_ids = lax.optimization_barrier(
        (heads_two, grad_arrived, arrived_ids)
    )
    heads_two = exchange(heads_two)
    heads_two, w_attn_out_two, expert_w = lax.optimization_barrier(
        (heads_two, w_attn_out_two, expert_w)
    )
    after_two, normed_three, blocks_two, keep_two, send_two, att_keep_two, att_send_two = post(
        meta, middle, gains[3], heads_two, w_attn_out_two
    )

    rows_sent = send_rows(normed_three)
    shared, mixed_two, hid_keep_two, hid_send_two = mlp(
        meta, after_two, blocks_two, w_mlp_in_two, w_mlp_out_two
    )
    grad_mixed_two, grad_shared_in = mlp_back(
        meta, cotangent, mixed_two, w_mlp_in_two, w_mlp_out_two
    )
    grad_mlp_out_two = weight_grad(
        meta, hid_keep_two, *near(hid_send_two), cotangent, *near(cotangent)
    )
    logits = jnp.dot(normed_three, router_full, preferred_element_type=jnp.float32)
    picked = jnp.sum(jnp.where(chosen, logits[:, None, :], 0.0), axis=-1)
    gate_probs = jax.nn.softmax(picked, axis=-1)
    rows_sent, grad_shared_in, grad_mlp_out_two, gate_probs = lax.optimization_barrier(
        (rows_sent, grad_shared_in, grad_mlp_out_two, gate_probs)
    )
    sum_mlp_out_two = add_arrived(grad_mlp_out_two)
    router_wide = jnp.pad(router_full, ((0, 0), (0, 128 - num_experts)))
    own_expert = ((own_ctx * fsdp_count + own_fsdp) // units).reshape(1)
    partial_rows, partial_back, kept_rows = experts(
        own_expert,
        to_units(rows_sent.reshape(slot_count, model_width)),
        grad_arrived,
        router_wide,
        arrived_ids,
        expert_w,
    )
    arrived, grad_rows, hidden_rows, grad_gate, grad_up, dots = kept_rows
    dots = from_units(dots.reshape(units, num_experts, capacity))
    coarse = lax.optimization_barrier(dots.astype(jnp.bfloat16))
    payload = with_notes(
        from_units(partial_back).astype(jnp.bfloat16).reshape(num_experts, capacity, model_width),
        coarse,
        dots - coarse.astype(jnp.float32),
    )
    payload, kept_rows, partial_rows = lax.optimization_barrier((payload, kept_rows, partial_rows))
    arrived, grad_rows, hidden_rows, grad_gate, grad_up, _ = kept_rows
    back = dispatch(payload)
    grad_experts = jnp.stack(
        [
            jnp.einsum("rd,rf->df", left, right, preferred_element_type=jnp.float32)
            .astype(jnp.bfloat16)
            .reshape(fsdp_count, shard_width, hid_unit)
            for left, right in ((arrived, grad_gate), (arrived, grad_up), (grad_rows, hidden_rows))
        ],
        axis=1,
    )
    grad_mlp_in_two = weight_grad(
        meta, keep_two, *near(send_two), grad_mixed_two, *near(grad_mixed_two)
    )
    back, grad_experts, grad_mlp_in_two, sum_mlp_out_two = lax.optimization_barrier(
        (back, grad_experts, grad_mlp_in_two, sum_mlp_out_two)
    )
    grad_out = cotangent[0].astype(jnp.float32)
    stride = back.shape[1]
    notes = back[:, capacity : capacity + 2, :capacity].astype(jnp.float32)
    slot_dots = jnp.sum(notes, axis=1).reshape(1, slot_count)
    grad_gates = jnp.stack(
        [
            jnp.sum(
                jnp.where(slots[None, :] == slot_target[:, k, None], slot_dots, 0.0), axis=-1
            )
            for k in range(TOP)
        ],
        axis=1,
    )
    grad_picked = gate_probs * (
        grad_gates - jnp.sum(gate_probs * grad_gates, axis=-1, keepdims=True)
    )
    grad_logits = jnp.sum(jnp.where(chosen, grad_picked[..., None], 0.0), axis=1)
    grad_router = jnp.einsum(
        "te,td->ed", grad_logits, normed_three.astype(jnp.float32), precision=HIGHEST
    )
    wide = jnp.arange(num_experts * stride, dtype=jnp.int32)[None, :]
    wide_target = slot_target + (stride - capacity) * routes[0]
    spread = (wide == wide_target[:, 0, None]) | (wide == wide_target[:, 1, None])
    grad_normed = (
        grad_shared_in
        + jnp.dot(
            spread.astype(jnp.bfloat16),
            back.reshape(num_experts * stride, model_width),
            preferred_element_type=jnp.float32,
        )
        + jnp.einsum(
            "te,de->td", grad_logits, router_full.astype(jnp.float32), precision=HIGHEST
        )
    )
    grad_heads, grad_resid, branch, gain_three = post_back(
        meta, after_two, gains[3], grad_out, grad_normed, w_attn_out_two
    )
    grad_heads = exchange(grad_heads)
    grad_attn_out_two = weight_grad(
        meta, att_keep_two, *near(att_send_two), branch, *near(branch)
    )
    sum_mlp_in_two = add_arrived(grad_mlp_in_two)
    grad_heads, grad_attn_out_two, grad_experts, sum_mlp_in_two, sum_mlp_out_two = (
        lax.optimization_barrier(
            (grad_heads, grad_attn_out_two, grad_experts, sum_mlp_in_two, sum_mlp_out_two)
        )
    )
    grad_experts = lax.all_to_all(grad_experts, "fsdp", 0, 0, tiled=True)
    grad_q, own, others = attend_back(
        meta, kept_two[2], grad_heads, kept_two[3], kept_two[4], count
    )
    arrived_kv = [swap(values, "ctx", part + 1) for part, values in enumerate(others)]
    sum_attn_out_two = add_arrived(grad_attn_out_two)
    grad_qkv = exchange(merge(meta, grad_q, own, arrived_kv))
    expert_rows = from_units(partial_rows).astype(jnp.bfloat16)
    sums_two = jnp.concatenate(
        [sum_mlp_in_two, sum_mlp_out_two.reshape(shard_width, -1)], axis=1
    ).reshape(ctx_count, shard_width // ctx_count, -1)
    grad_qkv, expert_rows, grad_experts, sums_two, sum_attn_out_two = lax.optimization_barrier(
        (grad_qkv, expert_rows, grad_experts, sums_two, sum_attn_out_two)
    )
    sums_two = lax.all_to_all(sums_two, "ctx", 0, 0, tiled=True)
    grad_mixed, grad_resid, gain_two = pre_back(
        meta, middle, gains[2], tables, grad_resid, grad_qkv, w_attn_in_two
    )
    near_qkv = near(kept_two[1], grad_mixed)
    branch = grad_resid.astype(jnp.bfloat16)[None]
    grad_mixed_one, grad_normed = mlp_back(
        meta, branch, mixed_one, w_mlp_in_one, w_mlp_out_one
    )
    grad_attn_in_two = weight_grad(meta, kept_two[0], near_qkv[0], grad_mixed, near_qkv[1])
    grad_normed, grad_attn_in_two = lax.optimization_barrier((grad_normed, grad_attn_in_two))
    near_mixed = [None] + near(branch, grad_mixed_one)
    grad_heads, grad_resid, att_branch, gain_one = post_back(
        meta, after_one, gains[1], grad_resid, grad_normed, w_attn_out_one
    )
    near_branch = near(att_branch)[0]
    grad_heads = exchange(grad_heads)
    grad_mlp_in_one = weight_grad(meta, keep_one, near_one[0], grad_mixed_one, near_mixed[2])
    first_sent = jnp.concatenate([grad_mlp_in_one[1], grad_attn_in_two[1]], axis=1)
    grad_heads, first_sent, expert_rows, sums_two = lax.optimization_barrier(
        (grad_heads, first_sent, expert_rows, sums_two)
    )
    sums_two = jnp.sum(sums_two.astype(jnp.float32), axis=0).astype(jnp.bfloat16)
    sums_two = lax.all_gather(sums_two, "ctx", axis=0, tiled=True)
    expert_rows = dispatch(expert_rows.reshape(num_experts, capacity, model_width))
    expert_rows = expert_rows.reshape(slot_count, model_width)
    first_arrived = swap(first_sent, "fsdp", 2)
    grad_q, own, others = attend_back(
        meta, kept_one[2], grad_heads, kept_one[3], kept_one[4], count
    )
    arrived_kv = [swap(values, "ctx", part + 1) for part, values in enumerate(others)]
    grad_mlp_out_one = weight_grad(meta, hid_keep_one, near_one[2], branch, near_mixed[1])
    grad_attn_out_one = weight_grad(meta, att_keep_one, near_one[1], att_branch, near_branch)
    second_sent = jnp.concatenate([grad_mlp_out_one[1], grad_attn_out_one[1]], axis=0)
    wide = grad_mlp_in_one[0].shape[1]
    first_sums = (
        grad_attn_in_two[0] + first_arrived[:, wide:],
        grad_mlp_in_one[0] + first_arrived[:, :wide],
    )
    arrived_kv, second_sent, first_sums = lax.optimization_barrier(
        (arrived_kv, second_sent, first_sums)
    )
    grad_qkv = exchange(merge(meta, grad_q, own, arrived_kv))
    second_arrived = swap(second_sent, "fsdp", 2)
    tall = grad_mlp_out_one[0].shape[0]
    sums_one = [
        *first_sums,
        grad_mlp_out_one[0] + second_arrived[:tall],
        grad_attn_out_one[0] + second_arrived[tall:],
        sum_attn_out_two,
    ]
    grad_qkv, expert_rows, sums_two, *sums_one = lax.optimization_barrier(
        (grad_qkv, expert_rows, sums_two, *sums_one)
    )
    sums_one = total(1, sums_one)
    grad_mixed, grad_resid, gain_zero = pre_back(
        meta, resid_in, gains[0], tables, grad_resid, grad_qkv, w_attn_in_one
    )
    near_qkv = near(kept_one[1], grad_mixed)
    grad_attn_in_one = weight_grad(meta, kept_one[0], near_qkv[0], grad_mixed, near_qkv[1])
    grad_attn_in_one, expert_rows, grad_experts = lax.optimization_barrier(
        (grad_attn_in_one, expert_rows, grad_experts)
    )
    grad_experts = jnp.transpose(grad_experts, (1, 2, 0, 3)).astype(jnp.float32)
    grad_experts = grad_experts.reshape(3, shard_width, hid_unit * fsdp_count)
    back_rows = [jnp.dot(p, expert_rows, preferred_element_type=jnp.float32) for p in of_token]
    output = shared + sum(gate_probs[:, k, None] * back_rows[k] for k in range(TOP))
    small_grads = jnp.concatenate([gain_zero, gain_one, gain_two, gain_three, grad_router])
    attn_in_grad, sums_one, small_grads = reduce_last(
        at_ctx,
        grad_attn_in_one[0],
        swap(grad_attn_in_one[1], "fsdp", 2),
        sums_one[0],
        sums_one,
        small_grads,
    )
    small_grads = lax.dynamic_slice_in_dim(small_grads, own_fsdp * shard_width, shard_width, 1)
    wide = sums_one[1].shape[1]
    dense_grads = [attn_in_grad] + [
        jnp.stack(pair).astype(jnp.float32)
        for pair in (
            (sums_one[3], sums_one[4]),
            (sums_one[1], sums_two[:, :wide]),
            (sums_one[2], sums_two[:, wide:].reshape(sums_one[2].shape)),
        )
    ]
    return (
        output[None],
        grad_resid[None],
        dense_grads[0],
        dense_grads[1],
        small_grads[:4].reshape(2, 2, shard_width),
        dense_grads[2],
        dense_grads[3],
        small_grads[4:].T,
        jnp.swapaxes(grad_experts[:2], 1, 2),
        grad_experts[2].T,
    )


def solution(mesh):
    placed = (
        P("fsdp", "ctx", None),
        P("fsdp", "ctx", None),
        P("fsdp", None),
        P("fsdp", None),
        P("fsdp", "ctx", None),
        P(None, "fsdp", None),
        P(None, "fsdp", None),
        P(None, None, "fsdp"),
        P(None, "fsdp", None),
        P(None, "fsdp", None),
        P("fsdp", None),
        P(None, "ctx", "fsdp"),
        P("ctx", "fsdp"),
    )
    return jax.shard_map(
        per_device,
        mesh=mesh,
        in_specs=placed,
        out_specs=(
            P("fsdp", "ctx", None),
            P("fsdp", "ctx", None),
            P(None, "fsdp", None),
            P(None, "fsdp", None),
            P(None, None, "fsdp"),
            P(None, "fsdp", None),
            P(None, "fsdp", None),
            P("fsdp", None),
            P(None, "ctx", "fsdp"),
            P("ctx", "fsdp"),
        ),
        check_vma=False,
    )
```

```python
import functools
import math

import jax
import jax.numpy as jnp
from jax import lax
from jax.experimental import pallas as pl
from jax.experimental.pallas import tpu as pltpu
from jax.sharding import PartitionSpec as P

HEADS = 12
HD = 64
FF = 2048
TOP = 2
HEAD_GROUPS = 4
KEY_SPAN = 512
VMEM_LIMIT = 60 * 1024 * 1024


HIGHEST = lax.Precision.HIGHEST
EPSILON = 1e-06
NEGATIVE = -1e30


BOTH = ("ctx", "fsdp")


def swap(values, axis, mask):
    count = lax.axis_size(axis)
    return lax.ppermute(values, axis, [(i, i ^ mask) for i in range(count)])


def gather_shards(shard):
    near = swap(shard, "fsdp", 1)
    far = swap(shard, "fsdp", 2)
    return (shard, near, far, swap(far, "fsdp", 1))


def in_order(shards):
    own = lax.axis_index("fsdp")
    buffer = jnp.zeros((len(shards),) + shards[0].shape, shards[0].dtype)
    for k, shard in enumerate(shards):
        buffer = lax.dynamic_update_index_in_dim(buffer, shard, own ^ k, 0)
    return buffer


NT = (((1,), (1,)), ((), ()))


def _dot(a, b):
    return jnp.dot(a, b, preferred_element_type=jnp.float32)


def _dot_nt(a, b):
    return lax.dot_general(a, b, NT, preferred_element_type=jnp.float32)


def _flip(values):
    return values.astype(jnp.float32).T.astype(values.dtype)


def _shape(shape, dtype=jnp.bfloat16):
    return jax.ShapeDtypeStruct(shape, dtype)


def _whole(shape):
    return pl.BlockSpec(tuple(shape), lambda *_: (0,) * len(shape))


def operands(shards, part=None):
    if isinstance(shards, (tuple, list)):
        arrays, rows, place = shards, shards[0].shape[0], lambda m, k: 0
    else:
        arrays, rows, place = (shards,) * 4, shards.shape[0] // 4, lambda m, k: m[0] ^ k
    width = arrays[0].shape[1]
    if part is None:
        specs = [
            pl.BlockSpec((rows, width), lambda i, m, k=k: (place(m, k), 0)) for k in range(4)
        ]
    else:
        size, first = part
        specs = [
            pl.BlockSpec((rows, size), lambda i, m, k=k: (place(m, k), first + (m[0] ^ i)))
            for k in range(4)
        ]
    return list(arrays), specs


def call(body, meta, inputs, outputs, scratch=(), flops=0, in_specs=None, out_specs=None, grid=(1,)):
    moved = sum(math.prod(a.shape) * a.dtype.itemsize for a in (*inputs, *outputs))
    return pl.pallas_call(
        body,
        grid_spec=pltpu.PrefetchScalarGridSpec(
            num_scalar_prefetch=1,
            grid=grid,
            in_specs=in_specs or [_whole(a.shape) for a in inputs],
            out_specs=out_specs or [_whole(a.shape) for a in outputs],
            scratch_shapes=list(scratch),
        ),
        out_shape=list(outputs),
        compiler_params=pltpu.CompilerParams(vmem_limit_bytes=VMEM_LIMIT),
        cost_estimate=pl.CostEstimate(flops=flops, bytes_accessed=moved, transcendentals=0),
    )(meta, *inputs)


def _stack(refs, cols=slice(None)):
    return jnp.concatenate([w[:, cols] for w in refs], axis=0)


def _mine(blocks, own):
    return jnp.concatenate([blocks[own ^ k] for k in range(4)], axis=1)


def _norm(rows, gain):
    inverse = lax.rsqrt(jnp.mean(rows * rows, axis=-1, keepdims=True) + EPSILON)
    return rows * inverse * gain


def _norm_back(rows, gain, grad):
    inverse = lax.rsqrt(jnp.mean(rows * rows, axis=-1, keepdims=True) + EPSILON)
    weighted = grad * gain
    scaled = rows * inverse
    back = inverse * (weighted - scaled * jnp.mean(weighted * scaled, axis=-1, keepdims=True))
    return back, jnp.sum(grad * scaled, axis=0, keepdims=True)


def _split(rows, blocks):
    width = rows.shape[1] // len(blocks)
    for b, ref in enumerate(blocks):
        ref[...] = rows[:, b * width : (b + 1) * width]


def _turn(rows, cosine, sine, sign):
    lane = lax.broadcasted_iota(jnp.int32, cosine.shape, 1)
    low = lane % HD < HD // 2
    turned = []
    for b in range(rows.shape[1] // 128):
        part = rows[:, b * 128 : (b + 1) * 128]
        other = jnp.where(low, pltpu.roll(part, 128 - HD // 2, 1), pltpu.roll(part, HD // 2, 1))
        turned.append(part * cosine + sign * (other * sine))
    return jnp.concatenate(turned, axis=1)


def _pre_kernel(meta, x, gain, cosine, sine, w0, w1, w2, w3, keep, send, *rest):
    qkv, (blocks, heads) = rest[:4], rest[4:]
    own, line = meta[0], meta[1]
    width = x.shape[1]
    normed = _norm(x[...], gain[...]).astype(jnp.bfloat16)
    _split(normed, [blocks.at[b] for b in range(4)])
    for j in range(2):
        keep[j] = blocks[own ^ (2 * j)]
        send[j] = blocks[own ^ (2 * j + 1)]
    piece = x.shape[0] // 2
    mine = _mine(blocks, own)
    for kind in range(3):
        mixed = _dot(mine, _stack((w0, w1, w2, w3), slice(kind * width, (kind + 1) * width)))
        if kind < 2:
            mixed = _turn(mixed, cosine[...], sine[...], 1.0)
        if kind == 0:
            mixed = mixed * 0.125
        turned = mixed.T.astype(jnp.bfloat16)
        block = width // 4
        for b in range(4):
            for p in range(2):
                heads[b, p, kind] = turned[
                    b * block : (b + 1) * block, p * piece : (p + 1) * piece
                ]
    for k in range(4):
        qkv[k][...] = heads[line ^ k]


def pre(meta, x, gain, tables, shards):
    rows, width = x.shape
    block = width // 4
    outs = [_shape((2, rows, block))] * 2 + [_shape((2, 3, block, rows // 2))] * 4
    shards, specs = operands(shards)
    inputs = (x, gain, *tables)
    got = call(
        _pre_kernel,
        meta,
        (*inputs, *shards),
        outs,
        [
            pltpu.VMEM((4, rows, block), jnp.bfloat16),
            pltpu.VMEM((4, 2, 3, block, rows // 2), jnp.bfloat16),
        ],
        flops=6 * rows * width * width,
        in_specs=[_whole(a.shape) for a in inputs] + specs,
    )
    return got[0], got[1], got[2:6]


def _pre_back_kernel(meta, x, gain, cosine, sine, resid, *rest):
    qkv, w = rest[:4], rest[4:8]
    mixed_out, resid_out, gain_out, heads, blocks = rest[8:]
    own, line = meta[0], meta[1]
    width = x.shape[1]
    for k in range(4):
        heads[line ^ k] = qkv[k][...]
    for kind in range(3):
        mixed = jnp.concatenate(
            [
                jnp.concatenate([heads[b, p, kind] for b in range(4)], axis=0)
                for p in range(2)
            ],
            axis=1,
        )
        mixed = mixed.astype(jnp.float32).T
        if kind < 2:
            mixed = mixed * (0.125 if kind == 0 else 1.0)
            mixed = _turn(mixed, cosine[...], sine[...], -1.0)
        mixed_out[0, :, kind * width : (kind + 1) * width] = mixed.astype(jnp.bfloat16)
    grads = _dot_nt(mixed_out[0], _stack(w))
    _split(grads, [blocks.at[own ^ k] for k in range(4)])
    grad = jnp.concatenate([blocks[b] for b in range(4)], axis=1)
    back, grad_gain = _norm_back(x[...], gain[...], grad)
    resid_out[...] = resid[...] + back
    gain_out[...] = grad_gain


def pre_back(meta, x, gain, tables, resid, qkv, shards):
    rows, width = x.shape
    shards, specs = operands(shards)
    inputs = (x, gain, *tables, resid, *qkv)
    return call(
        _pre_back_kernel,
        meta,
        (*inputs, *shards),
        [
            _shape((1, rows, 3 * width)),
            _shape((rows, width), jnp.float32),
            _shape((1, width), jnp.float32),
        ],
        [
            pltpu.VMEM((4, 2, 3, width // 4, rows // 2), jnp.bfloat16),
            pltpu.VMEM((4, rows, width // 4), jnp.float32),
        ],
        flops=6 * rows * width * width,
        in_specs=[_whole(a.shape) for a in inputs] + specs,
    )


def _post_kernel(meta, x, gain, o0, o1, o2, o3, w0, w1, w2, w3, *rest):
    after, plain, blocks_out, keep, send, att_keep, att_send, att = rest
    own, line = meta[0], meta[1]
    piece = x.shape[0] // 2
    for k, o in enumerate((o0, o1, o2, o3)):
        for p in range(2):
            att[line ^ k, p * piece : (p + 1) * piece, :] = _flip(o[p])
    for j in range(2):
        att_keep[j] = att[own ^ (2 * j)]
        att_send[j] = att[own ^ (2 * j + 1)]
    rows = x[...] + _dot(_mine(att, own), _stack((w0, w1, w2, w3)))
    after[...] = rows
    normed = _norm(rows, gain[...]).astype(jnp.bfloat16)
    plain[...] = normed
    _split(normed, [att.at[b] for b in range(4)])
    blocks_out[...] = att[...]
    for j in range(2):
        keep[j] = att[own ^ (2 * j)]
        send[j] = att[own ^ (2 * j + 1)]


def post(meta, x, gain, heads, shards):
    rows, width = x.shape
    block = width // 4
    shards, specs = operands(shards)
    inputs = (x, gain, *heads)
    return call(
        _post_kernel,
        meta,
        (*inputs, *shards),
        [_shape((rows, width), jnp.float32), _shape((rows, width)), _shape((4, rows, block))]
        + [_shape((2, rows, block))] * 4,
        [pltpu.VMEM((4, rows, block), jnp.bfloat16)],
        flops=2 * rows * width * width,
        in_specs=[_whole(a.shape) for a in inputs] + specs,
    )


def _post_back_kernel(meta, x, gain, resid, grad, w0, w1, w2, w3, *rest):
    heads, (resid_out, branch, gain_out, att) = rest[:4], rest[4:]
    own, line = meta[0], meta[1]
    back, grad_gain = _norm_back(x[...], gain[...], grad[...])
    gain_out[...] = grad_gain
    rows = resid[...] + back
    resid_out[...] = rows
    rows = rows.astype(jnp.bfloat16)
    branch[0] = rows
    grads = _dot_nt(rows, _stack((w0, w1, w2, w3))).astype(jnp.bfloat16)
    _split(grads, [att.at[own ^ k] for k in range(4)])
    piece = x.shape[0] // 2
    for k in range(4):
        for p in range(2):
            heads[k][p] = _flip(att[line ^ k, p * piece : (p + 1) * piece, :])


def post_back(meta, x, gain, resid, grad, shards):
    rows, width = x.shape
    block = width // 4
    shards, specs = operands(shards)
    inputs = (x, gain, resid, grad)
    got = call(
        _post_back_kernel,
        meta,
        (*inputs, *shards),
        [_shape((2, block, rows // 2))] * 4
        + [
            _shape((rows, width), jnp.float32),
            _shape((1, rows, width)),
            _shape((1, width), jnp.float32),
        ],
        [pltpu.VMEM((4, rows, block), jnp.bfloat16)],
        flops=2 * rows * width * width,
        in_specs=[_whole(a.shape) for a in inputs] + specs,
    )
    return got[:4], got[4], got[5], got[6]


def _mlp_kernel(meta, x, blocks, *rest):
    gates, ups, downs = rest[:4], rest[4:8], rest[8:12]
    out, mixed, keep, send, acc = rest[12:]
    own, step = meta[0], pl.program_id(0)
    rows = _mine(blocks, own)
    gate = _dot(rows, _stack(gates))
    up = _dot(rows, _stack(ups))
    mixed[0], mixed[1] = gate, up
    hidden = (gate * jax.nn.sigmoid(gate) * up).astype(jnp.bfloat16)
    for k in range(4):

        @pl.when(step == k)
        def _(k=k):
            (send if k % 2 else keep)[k // 2] = hidden
            part = _dot(hidden, downs[k][...])
            if k == 0:
                acc[...] = x[...] + part
            elif k < 3:
                acc[...] += part
            else:
                out[...] = acc[...] + part


def mlp_width(shards):
    first = shards[0] if isinstance(shards, (tuple, list)) else shards
    return first.shape[1] // 2


def mlp(meta, x, blocks, shards_in, shards_out):
    rows, width = x.shape
    hidden = mlp_width(shards_in)
    part = hidden // 4
    gates, gate_specs = operands(shards_in, (part, 0))
    ups, up_specs = operands(shards_in, (part, 4))
    downs, down_specs = operands(shards_out)
    return call(
        _mlp_kernel,
        meta,
        (x, blocks, *gates, *ups, *downs),
        [
            _shape((rows, width), jnp.float32),
            _shape((2, rows, hidden), jnp.float32),
            _shape((2, rows, part)),
            _shape((2, rows, part)),
        ],
        [pltpu.VMEM((rows, width), jnp.float32)],
        flops=6 * rows * width * hidden,
        in_specs=[_whole(x.shape), _whole(blocks.shape), *gate_specs, *up_specs, *down_specs],
        out_specs=[
            _whole((rows, width)),
            pl.BlockSpec((2, rows, part), lambda i, m: (0, 0, m[0] ^ i)),
            _whole((2, rows, part)),
            _whole((2, rows, part)),
        ],
        grid=(4,),
    )


def _mlp_back_kernel(meta, branch, mixed, *rest):
    gates, ups, downs = rest[:4], rest[4:8], rest[8:12]
    grad_mixed, grad_out, grad_hidden, acc, turned = rest[12:]
    own, step = meta[0], pl.program_id(0)
    for k in range(4):

        @pl.when(step == k)
        def _(k=k):
            grad_hidden[...] = _dot_nt(branch[0], downs[k][...]).astype(jnp.bfloat16)

    grad_h = grad_hidden[...].astype(jnp.float32)
    gate, up = mixed[0], mixed[1]
    sigmoid = jax.nn.sigmoid(gate)
    grad_gate = (grad_h * up * sigmoid * (1.0 + gate * (1.0 - sigmoid))).astype(jnp.bfloat16)
    grad_up = (grad_h * gate * sigmoid).astype(jnp.bfloat16)
    grad_mixed[0], grad_mixed[1] = grad_gate, grad_up
    part = _dot_nt(grad_gate, _stack(gates)) + _dot_nt(grad_up, _stack(ups))

    @pl.when(step == 0)
    def _():
        acc[...] = part

    @pl.when((step > 0) & (step < 3))
    def _():
        acc[...] += part

    @pl.when(step == 3)
    def _():
        _split(acc[...] + part, [turned.at[own ^ k] for k in range(4)])
        grad_out[...] = jnp.concatenate([turned[b] for b in range(4)], axis=1)


def mlp_back(meta, branch, mixed, shards_in, shards_out):
    _, rows, width = branch.shape
    hidden = mixed.shape[2]
    part = hidden // 4
    block = width // 4
    gates, gate_specs = operands(shards_in, (part, 0))
    ups, up_specs = operands(shards_in, (part, 4))
    downs, down_specs = operands(shards_out)
    return call(
        _mlp_back_kernel,
        meta,
        (branch, mixed, *gates, *ups, *downs),
        [_shape((2, rows, hidden)), _shape((rows, width), jnp.float32)],
        [
            pltpu.VMEM((rows, part), jnp.bfloat16),
            pltpu.VMEM((rows, width), jnp.float32),
            pltpu.VMEM((4, rows, block), jnp.float32),
        ],
        flops=6 * rows * width * hidden,
        in_specs=[
            _whole(branch.shape),
            pl.BlockSpec((2, rows, part), lambda i, m: (0, 0, m[0] ^ i)),
            *gate_specs,
            *up_specs,
            *down_specs,
        ],
        out_specs=[
            pl.BlockSpec((2, rows, part), lambda i, m: (0, 0, m[0] ^ i)),
            _whole((rows, width)),
        ],
        grid=(4,),
    )


def _grad_kernel(meta, left, left_near, right, right_near, own, send, flipped):
    rows, depth = left.shape[1:]

    @pl.when((pl.program_id(0) == 0) & (pl.program_id(1) == 0))
    def _():
        for j in range(2):
            flipped[j * depth : (j + 1) * depth, :rows] = _flip(left[j])
            flipped[j * depth : (j + 1) * depth, rows:] = _flip(left_near[j])

    both = jnp.concatenate([right[0], right_near[0]], axis=0)
    grads = _dot(flipped[...], both).astype(jnp.bfloat16)
    own[...] = grads[:depth]
    send[...] = grads[depth:]


def weight_grad(meta, left, left_near, right, right_near):
    groups, rows, width = right.shape
    depth = left.shape[2]
    chunk = 512 if width % 768 else 768
    steps = width // chunk
    right_spec = pl.BlockSpec((1, rows, chunk), lambda g, i, m: (g, 0, i))
    out_spec = pl.BlockSpec((depth, chunk), lambda g, i, m: (0, g * steps + i))
    return call(
        _grad_kernel,
        meta,
        (left, left_near, right, right_near),
        [_shape((depth, groups * width))] * 2,
        [pltpu.VMEM((2 * depth, 2 * rows), jnp.bfloat16)],
        flops=8 * rows * depth * groups * width,
        in_specs=[_whole(left.shape), _whole(left.shape), right_spec, right_spec],
        out_specs=[out_spec, out_spec],
        grid=(groups, steps),
    )


def _mask(first_key, keys, query_pos, query_start, copies):
    key_pos = first_key + lax.broadcasted_iota(jnp.int32, (keys, query_pos.shape[1]), 0)
    allowed = (key_pos <= query_pos) & (key_pos >= query_start)
    return jnp.concatenate([allowed] * copies, axis=1)


def _tables(meta, parts):
    return (lambda s: meta[2 + s], lambda k: meta[2 + 8 * parts + k])


def _query_geometry(place, ends, count, piece, key_span):
    query_pos = place * piece + lax.broadcasted_iota(jnp.int32, (1, piece), 1)
    query_start = jnp.zeros_like(query_pos)
    first = place * piece
    least = jnp.int32(0)
    for k in range(count):
        last = k == count - 1
        query_start = jnp.where(query_pos >= ends(k), query_pos if last else ends(k), query_start)
        least = jnp.where(first >= ends(k), first if last else ends(k), least)
    return (query_pos, query_start, least // key_span, (first + piece - 1) // key_span + 1)


def _stack_heads(rows, heads):
    head_dim = rows.shape[0] // heads
    head = lax.broadcasted_iota(jnp.int32, rows.shape, 0) // head_dim
    zero = jnp.zeros_like(rows)
    return jnp.concatenate([jnp.where(head == h, rows, zero) for h in range(heads)], axis=1)


def _own_heads(acc, heads, piece):
    head_dim = acc.shape[0] // heads
    return jnp.concatenate(
        [
            acc[h * head_dim : (h + 1) * head_dim, h * piece : (h + 1) * piece]
            for h in range(heads)
        ],
        axis=0,
    )


def _attend_kernel(heads, count, key_span, parts, meta, *refs):
    inputs, o, (keep, lse, keys, values_t) = (
        refs[: 4 * parts],
        refs[4 * parts : 4 * parts + 4],
        refs[4 * parts + 4 :],
    )
    width, piece = inputs[0].shape[2:]
    place, ends = _tables(meta, parts)
    for s in range(8 * parts):
        at = pl.ds(pl.multiple_of(place(s) * piece, piece), piece)
        keys[at, :] = _flip(inputs[s // 2][s % 2, 1])
        values_t[:, at] = inputs[s // 2][s % 2, 2]
    cols = heads * piece
    for s in range(8):
        query_pos, query_start, begin, end = _query_geometry(
            place(s), ends, count, piece, key_span
        )
        stacked = _stack_heads(inputs[s // 2][s % 2, 0], heads)

        def advance(block, carried):
            run_max, run_sum, acc = carried
            first = pl.multiple_of(block * key_span, key_span)
            scores = _dot(keys[pl.ds(first, key_span), :], stacked)
            allowed = _mask(first, key_span, query_pos, query_start, heads)
            scores = jnp.where(allowed, scores, NEGATIVE)
            new_max = jnp.maximum(run_max, jnp.max(scores, axis=0, keepdims=True))
            weights = jnp.exp(scores - new_max)
            factor = jnp.exp(run_max - new_max)
            run_sum = run_sum * factor + jnp.sum(weights, axis=0, keepdims=True)
            part = _dot(values_t[:, pl.ds(first, key_span)], weights.astype(jnp.bfloat16))
            return (new_max, run_sum, acc * factor + part)

        run_max, run_sum, acc = lax.fori_loop(
            begin,
            end,
            advance,
            (
                jnp.full((1, cols), NEGATIVE, jnp.float32),
                jnp.zeros((1, cols), jnp.float32),
                jnp.zeros((width, cols), jnp.float32),
            ),
        )
        kept = _own_heads(acc / run_sum, heads, piece)
        keep[s] = kept
        o[s // 2][s % 2] = kept.astype(jnp.bfloat16)
        lse[s] = run_max + jnp.log(run_sum)


def attend(meta, inputs, count):
    _, _, width, piece = inputs[0].shape
    heads = width // HD
    parts = len(inputs) // 4
    slots = parts * 8 * piece
    got = call(
        functools.partial(_attend_kernel, heads, count, KEY_SPAN, parts),
        meta,
        inputs,
        [_shape((2, width, piece))] * 4
        + [_shape((8, width, piece), jnp.float32), _shape((8, 1, heads * piece), jnp.float32)],
        [
            pltpu.VMEM((slots, width), jnp.bfloat16),
            pltpu.VMEM((width, slots), jnp.bfloat16),
        ],
        flops=32 * piece * slots * width,
    )
    return got[:4], got[4], got[5]


def _attend_back_kernel(heads, count, key_span, parts, meta, *refs):
    inputs, grads, (keep, lse), rest = (
        refs[: 4 * parts],
        refs[4 * parts : 4 * parts + 4],
        refs[4 * parts + 4 : 4 * parts + 6],
        refs[4 * parts + 6 :],
    )
    gq, gkv = rest[0], rest[1 : 1 + parts]
    keys, keys_t, values, gkeys, gvalues = rest[1 + parts :]
    width, piece = inputs[0].shape[2:]
    head_dim = width // heads
    place, ends = _tables(meta, parts)
    for s in range(8 * parts):
        at = pl.ds(pl.multiple_of(place(s) * piece, piece), piece)
        key_rows = inputs[s // 2][s % 2, 1]
        keys_t[:, at] = key_rows
        keys[at, :] = _flip(key_rows)
        values[at, :] = _flip(inputs[s // 2][s % 2, 2])
    gkeys[...] = jnp.zeros_like(gkeys)
    gvalues[...] = jnp.zeros_like(gvalues)
    for s in range(8):
        query_pos, query_start, begin, end = _query_geometry(
            place(s), ends, count, piece, key_span
        )
        stacked = _stack_heads(inputs[s // 2][s % 2, 0], heads)
        grad = grads[s // 2][s % 2]
        grad_stacked = _stack_heads(grad, heads)
        product = grad.astype(jnp.float32) * keep[s]
        delta = jnp.concatenate(
            [
                jnp.sum(product[h * head_dim : (h + 1) * head_dim, :], axis=0, keepdims=True)
                for h in range(heads)
            ],
            axis=1,
        )
        log_sum = lse[s]

        def retreat(block, acc):
            first = pl.multiple_of(block * key_span, key_span)
            at = pl.ds(first, key_span)
            scores = _dot(keys[at, :], stacked)
            allowed = _mask(first, key_span, query_pos, query_start, heads)
            probs = jnp.where(allowed, jnp.exp(scores - log_sum), 0.0)
            grad_probs = _dot(values[at, :], grad_stacked)
            grad_scores = (probs * (grad_probs - delta)).astype(jnp.bfloat16)
            gvalues[:, at] += _dot_nt(grad_stacked, probs.astype(jnp.bfloat16))
            gkeys[:, at] += _dot_nt(stacked, grad_scores)
            return acc + _dot(keys_t[:, at], grad_scores)

        acc = lax.fori_loop(begin, end, retreat, jnp.zeros((width, heads * piece), jnp.float32))
        gq[s] = _own_heads(acc, heads, piece).astype(jnp.bfloat16)
    for s in range(8 * parts):
        at = pl.ds(pl.multiple_of(place(s) * piece, piece), piece)
        out = gkv[s // 8]
        out[s % 8, 0] = gkeys[:, at].astype(out.dtype)
        out[s % 8, 1] = gvalues[:, at].astype(out.dtype)


def attend_back(meta, inputs, grads, keep, lse, count):
    _, _, width, piece = inputs[0].shape
    heads = width // HD
    parts = len(inputs) // 4
    slots = parts * 8 * piece
    got = call(
        functools.partial(_attend_back_kernel, heads, count, KEY_SPAN, parts),
        meta,
        (*inputs, *grads, keep, lse),
        [_shape((8, width, piece)), _shape((8, 2, width, piece), jnp.float32)]
        + [_shape((8, 2, width, piece))] * (parts - 1),
        [
            pltpu.VMEM((slots, width), jnp.bfloat16),
            pltpu.VMEM((width, slots), jnp.bfloat16),
            pltpu.VMEM((slots, width), jnp.bfloat16),
            pltpu.VMEM((width, slots), jnp.float32),
            pltpu.VMEM((width, slots), jnp.float32),
        ],
        flops=80 * piece * slots * width,
    )
    return got[0], got[1], got[2:]


def _merge_kernel(meta, gq, own, *rest):
    arrived, out = rest[:-4], rest[-4:]
    for s in range(8):
        total = own[s]
        for other in arrived:
            total = total + other[s].astype(jnp.float32)
        out[s // 2][s % 2, 0] = gq[s]
        out[s // 2][s % 2, 1:3] = total.astype(jnp.bfloat16)


def merge(meta, gq, own, arrived):
    _, width, piece = gq.shape
    return call(
        _merge_kernel, meta, (gq, own, *arrived), [_shape((2, 3, width, piece))] * 4
    )


def _halve_kernel(meta, first, second, sent, kept):
    summed = (first[...].astype(jnp.float32) + second[...].astype(jnp.float32)).astype(jnp.bfloat16)
    half = sent.shape[1]
    left, right = summed[:, :half], summed[:, half:]
    side = meta[0] == 0
    sent[...] = jnp.where(side, right, left)
    kept[...] = jnp.where(side, left, right)


def _quarter_kernel(meta, first, second, *rest):
    parts, summed = rest[:-1], rest[-1]
    summed[...] = (first[...].astype(jnp.float32) + second[...].astype(jnp.float32)).astype(
        jnp.bfloat16
    )
    chunk = parts[0].shape[0]
    for k, part in enumerate(parts):
        at = pl.multiple_of((meta[1] ^ k) * chunk, chunk)
        part[...] = summed[pl.ds(at, chunk), :]


def _place_kernel(meta, other, *refs):
    out, parts = refs[-1], refs[:-1]
    _, rows, width = out.shape
    lines = len(parts) // 2
    chunk, half = rows // lines, width // 2
    side = meta[0] == 0
    for k in range(lines):
        at = pl.multiple_of((meta[1] ^ k) * chunk, chunk)
        own = parts[k][...].astype(jnp.float32)
        near = parts[lines + k][...].astype(jnp.float32)
        out[0, pl.ds(at, chunk), :half] = jnp.where(side, own, near)
        out[0, pl.ds(at, chunk), half:] = jnp.where(side, near, own)
    out[1] = other[...].astype(jnp.float32)


def reduce_last(place, grads, held, small):
    lines = lax.axis_size("ctx") // 2
    if any(own.shape[0] // lines % 16 for own, _, _ in grads):
        outs = [
            jnp.stack([lax.psum(own + arrived, "ctx"), other]).astype(jnp.float32)
            for own, arrived, other in grads
        ]
        return outs, held, total_small(small)
    columns = []
    for i, (own, arrived, other) in enumerate(grads):
        rows, width = own.shape
        chunk, half = rows // lines, width // 2
        sent, kept = call(_halve_kernel, place, (own, arrived), [_shape((rows, half))] * 2)
        if i == 0:
            kept, small = lax.optimization_barrier((kept, small))
            small = total_small(small)
        parts = call(
            _quarter_kernel,
            place,
            (kept, swap(sent, "ctx", 1)),
            [_shape((chunk, half))] * lines,
            [pltpu.VMEM((rows, half), jnp.bfloat16)],
        )
        summed = parts[0].astype(jnp.float32)
        for k in range(1, lines):
            summed = summed + swap(parts[k], "ctx", 2 * k).astype(jnp.float32)
        summed = summed.astype(jnp.bfloat16)
        column = [swap(summed, "ctx", 2 * k) if k else summed for k in range(lines)]
        columns.append(column + [swap(c, "ctx", 1) for c in column])
    columns, held = lax.optimization_barrier((columns, held))
    outs = [
        call(
            _place_kernel,
            place,
            (other, *parts),
            [_shape((2, *own.shape), jnp.float32)],
        )[0]
        for (own, _, other), parts in zip(grads, columns)
    ]
    return outs, held, small


def _expert_kernel(units, meta, *refs):
    xs, cs = refs[:units], refs[units : 2 * units]
    router, ids, w = refs[2 * units : 2 * units + 3]
    outs = refs[2 * units + 3 :]
    parts, backs = outs[:units], outs[units : 2 * units]
    rows_out, grads_out, hidden_out, gate_out, up_out, dots_out = outs[2 * units : 2 * units + 6]
    gates, ups, downs, x, c = outs[2 * units + 6 :]
    step = pl.program_id(0)
    tiles = pl.num_programs(0) // units

    @pl.when(step == 0)
    def _():
        width = w.shape[2]
        for f in range(4):
            part = slice(f * width, (f + 1) * width)
            gates[part, :] = w[f, 0]
            ups[part, :] = w[f, 1]
            downs[part, :] = w[f, 2]

    for u in range(units):

        @pl.when(step // tiles == u)
        def _(u=u):
            x[...] = xs[u][...]
            c[...] = cs[u][...]

    rows = x[...]
    rows_out[...] = rows
    incoming = c[...].astype(jnp.float32)
    logits = _dot(rows, router[...])
    lane = lax.broadcasted_iota(jnp.int32, logits.shape, 1)
    gap = jnp.sum(
        jnp.where(lane == meta[0], logits, 0.0)
        - jnp.where(lane.astype(jnp.float32) == ids[...], logits, 0.0),
        axis=1,
        keepdims=True,
    )
    grads = (jax.nn.sigmoid(gap) * incoming).astype(jnp.bfloat16)
    grads_out[...] = grads
    gate = _dot(rows, gates[...])
    up = _dot(rows, ups[...])
    sigmoid = jax.nn.sigmoid(gate)
    silu = gate * sigmoid
    hidden = (silu * up).astype(jnp.bfloat16)
    hidden_out[...] = hidden
    part = _dot_nt(hidden, downs[...])
    dots_out[...] = jnp.sum(part * incoming, axis=1, keepdims=True)
    grad_h = _dot(grads, downs[...]).astype(jnp.bfloat16).astype(jnp.float32)
    grad_gate = (grad_h * up * sigmoid * (1.0 + gate * (1.0 - sigmoid))).astype(jnp.bfloat16)
    grad_up = (grad_h * silu).astype(jnp.bfloat16)
    gate_out[...] = grad_gate
    up_out[...] = grad_up
    back = _dot_nt(grad_gate, gates[...]) + _dot_nt(grad_up, ups[...])
    for u in range(units):

        @pl.when(step // tiles == u)
        def _(u=u):
            parts[u][...] = part.astype(jnp.bfloat16)
            backs[u][...] = back.astype(jnp.bfloat16)


def experts(meta, xs, cs, router, ids, w):
    units, (rows, width), tile = len(xs), xs[0].shape, 1024 // len(xs)
    tiles, hidden = rows // tile, w.shape[3]
    total_rows = units * rows
    slabs = [
        pl.BlockSpec((tile, width), lambda i, m, u=u: (jnp.clip(i - u * tiles, 0, tiles - 1), 0))
        for u in range(units)
    ]

    def rowed(columns):
        return pl.BlockSpec((tile, columns), lambda i, m: (i, 0))

    got = call(
        functools.partial(_expert_kernel, units),
        meta,
        (*xs, *cs, router, ids, w),
        [_shape((rows, width))] * (2 * units)
        + [_shape((total_rows, width))] * 2
        + [_shape((total_rows, hidden))] * 3
        + [_shape((total_rows, 1), jnp.float32)],
        [pltpu.VMEM((width, hidden), jnp.bfloat16)] * 3
        + [pltpu.VMEM((tile, width), jnp.bfloat16)] * 2,
        flops=12 * total_rows * width * hidden,
        in_specs=slabs
        + slabs
        + [_whole(router.shape), rowed(1), _whole(w.shape)],
        out_specs=slabs + slabs + [rowed(width)] * 2 + [rowed(hidden)] * 3 + [rowed(1)],
        grid=(units * tiles,),
    )
    return got[:units], got[units : 2 * units], got[2 * units :]


def layout(lengths_row, order_row, piece_len):
    all_slots = order_row.shape[0] * piece_len
    position = (
        order_row[:, None] * piece_len + jnp.arange(piece_len, dtype=jnp.int32)[None, :]
    ).reshape(all_slots)
    count = jnp.arange(lengths_row.shape[0], dtype=jnp.int32)
    seq_ends = jnp.sum(
        jnp.where(count[:, None] <= count[None, :], lengths_row[:, None], 0), axis=0, dtype=jnp.int32
    )
    segment = jnp.sum(
        (position[:, None] >= seq_ends[None, :]).astype(jnp.int32), axis=1, dtype=jnp.int32
    )
    seq_start = jnp.sum(
        jnp.where(segment[:, None] > count[None, :], lengths_row[None, :], 0),
        axis=1,
        dtype=jnp.int32,
    )
    return (seq_ends, position - seq_start)


def angles(offset):
    freq_table = jnp.exp(
        jnp.arange(HD // 2, dtype=jnp.float32) * (-2.0 * math.log(10000.0) / HD)
    )
    theta = offset.astype(jnp.float32)[..., None] * freq_table
    cosine, sine = jnp.cos(theta), jnp.sin(theta)
    return (
        jnp.tile(cosine, (1, 256 // HD)),
        jnp.tile(jnp.concatenate([-sine, sine], axis=1), (1, 128 // HD)),
    )


def hidden_back(gate_pre, up_pre, grad_hidden):
    sigmoid_gate = jax.nn.sigmoid(gate_pre)
    grad_gate = grad_hidden * up_pre * sigmoid_gate * (1.0 + gate_pre * (1.0 - sigmoid_gate))
    grad_up = grad_hidden * gate_pre * sigmoid_gate
    return (grad_gate.astype(jnp.bfloat16), grad_up.astype(jnp.bfloat16))


def head_parts():
    return lax.axis_size("ctx") // HEAD_GROUPS


def exchange(values):
    return [values[0]] + [swap(values[k], "ctx", k * head_parts()) for k in range(1, 4)]


def attend_forward(meta, count, resid, gain, tables, w_in, early):
    keep, send, qkv = pre(meta, resid, gain, tables, w_in)
    qkv = exchange(qkv)
    inputs = list(qkv)
    for part in range(1, head_parts()):
        inputs += [swap(values, "ctx", part) for values in qkv]
    inputs, early = lax.optimization_barrier((inputs, early))
    heads, acc, lse = attend(meta, inputs, count)
    return heads, (keep, send, inputs, acc, lse), early


def near(*values):
    return [swap(v, "fsdp", 1) for v in values]


def add_arrived(grads):
    return grads[0] + swap(grads[1], "fsdp", 2)


def total(bucket, grads):
    count = lax.axis_size("ctx")
    ring = [[(i + bucket) % count for i in range(count)]]
    return lax.psum(tuple(grads), "ctx", axis_index_groups=ring)


def total_small(values):
    for axis in BOTH:
        step = 1
        while step < lax.axis_size(axis):
            values = values + swap(values, axis, step)
            step *= 2
    return values


def per_device(
    tokens,
    cotangent,
    lengths,
    piece_order,
    routes,
    attn_in,
    attn_out,
    norm_gain,
    mlp_in,
    mlp_out,
    router,
    expert_in,
    expert_out,
):
    tok_rows, model_width = tokens.shape[1:]
    shard_width = router.shape[0]
    num_experts = router.shape[1]
    own_ctx, own_fsdp = lax.axis_index("ctx"), lax.axis_index("fsdp")
    ctx_count, fsdp_count = lax.axis_size("ctx"), lax.axis_size("fsdp")
    units = ctx_count * fsdp_count // num_experts
    hid_unit = expert_out.shape[0] // fsdp_count
    members = [
        [i for i in range(ctx_count * fsdp_count) if i % units == lane] for lane in range(units)
    ]

    def dispatch(values):
        return lax.all_to_all(values, BOTH, 0, 0, tiled=True, axis_index_groups=members)

    def to_units(values):
        return [values] + [swap(values, BOTH, k) for k in range(1, units)]

    def from_units(partial):
        summed = partial[0].astype(jnp.float32)
        for k in range(1, units):
            summed = summed + swap(partial[k], BOTH, k).astype(jnp.float32)
        return summed

    def gathered(shard):
        return lax.all_gather(shard, "fsdp", axis=0, tiled=True)

    seq_ends, offset = layout(lengths[0], piece_order[0], tok_rows // 2)
    tables = angles(lax.dynamic_slice_in_dim(offset, own_ctx * tok_rows, tok_rows, 0))
    parts = ctx_count // HEAD_GROUPS
    line, side = own_ctx // parts, own_ctx % parts
    order = piece_order[0].reshape(HEAD_GROUPS, parts, 2)
    place = [order[line ^ k, side ^ part] for part in range(parts) for k in range(HEAD_GROUPS)]
    meta = jnp.concatenate([jnp.stack([own_fsdp, line]), jnp.concatenate(place), seq_ends])
    at_ctx = jnp.stack([own_ctx % 2, own_ctx // 2])
    count = lengths.shape[1]

    item_count = tok_rows * TOP
    capacity = 2 * item_count // num_experts
    slot_count = num_experts * capacity
    expert_ids = jnp.arange(num_experts, dtype=jnp.int32)
    chosen = routes[0][:, :, None] == expert_ids[None, None, :]
    flat_chosen = chosen.reshape(item_count, num_experts).astype(jnp.bfloat16)
    items = jnp.arange(item_count, dtype=jnp.int32)
    earlier = jnp.dot(
        (items[None, :] < items[:, None]).astype(jnp.bfloat16),
        flat_chosen,
        preferred_element_type=jnp.float32,
    )
    slot_rank = jnp.sum(earlier * flat_chosen.astype(jnp.float32), axis=1).astype(jnp.int32)
    slot_target = (routes[0].reshape(item_count) * capacity + slot_rank).reshape(tok_rows, TOP)
    slots = jnp.arange(slot_count, dtype=jnp.int32)
    at_slot = [slots[:, None] == slot_target[None, :, k] for k in range(TOP)]
    of_token = [(slots[None, :] == slot_target[:, k, None]).astype(jnp.bfloat16) for k in range(TOP)]
    fill = (at_slot[0] | at_slot[1]).astype(jnp.bfloat16)

    def to_slots(rows):
        return jnp.dot(fill, rows, preferred_element_type=jnp.float32).astype(jnp.bfloat16)

    def send_rows(rows):
        return dispatch(to_slots(rows).reshape(num_experts, capacity, model_width))

    other_ids = sum(
        jnp.sum(
            jnp.where(at_slot[k], routes[0][None, :, 1 - k].astype(jnp.float32), 0.0), axis=1
        )
        for k in range(TOP)
    )

    def with_notes(rows, *notes):
        extra = jnp.stack(notes, axis=1).astype(jnp.bfloat16)
        extra = jnp.pad(extra, ((0, 0), (0, 8 - len(notes)), (0, model_width - capacity)))
        return jnp.concatenate([rows, extra], axis=1)

    shard = attn_in[0]
    near_shard, far_shard = swap(shard, "fsdp", 1), swap(shard, "fsdp", 2)
    small = gather_shards(jnp.concatenate([norm_gain.reshape(4, shard_width), router.T], axis=0))
    ordered = []
    for i in range(4):
        block = small[3]
        for j in range(3):
            block = jnp.where(own_fsdp ^ j == i, small[j], block)
        ordered.append(block)
    small = jnp.concatenate(ordered, axis=1)
    gains = [small[i : i + 1].astype(jnp.float32) for i in range(4)]
    router_full = small[4:].T
    grad_rows = to_slots(cotangent[0]).reshape(num_experts, capacity, model_width)
    grad_sent = with_notes(grad_rows, other_ids.reshape(num_experts, capacity))
    stored = jnp.concatenate(
        [jnp.swapaxes(expert_in, 1, 2), jnp.swapaxes(expert_out, 0, 1)[None]]
    )
    expert_part = jnp.stack(
        [stored[:, :, f * hid_unit : (f + 1) * hid_unit] for f in range(fsdp_count)]
    )
    near_out, far_out = swap(attn_out[0], "fsdp", 1), swap(attn_out[0], "fsdp", 2)
    far_shard, tables, meta, gains, expert_part = lax.optimization_barrier(
        (far_shard, tables, meta, gains, expert_part)
    )
    w_attn_in_one = (shard, near_shard, far_shard, swap(far_shard, "fsdp", 1))
    own_out = attn_out[0]
    far_shard, far_out, attn_in, attn_out, mlp_in, mlp_out = lax.optimization_barrier(
        (far_shard, far_out, attn_in, attn_out, mlp_in, mlp_out)
    )
    w_attn_out_one = (own_out, near_out, far_out, swap(far_out, "fsdp", 1))
    w_mlp_in_one, w_mlp_out_one = gathered(mlp_in[0]), gathered(mlp_out[0])
    w_mlp_in_two, w_mlp_out_two = gathered(mlp_in[1]), gathered(mlp_out[1])

    resid_in = tokens[0].astype(jnp.float32)
    heads_one, kept_one, (grad_sent, attn_in, attn_out) = attend_forward(
        meta, count, resid_in, gains[0], tables, w_attn_in_one, (grad_sent, attn_in, attn_out)
    )
    far_in, far_out = swap(attn_in[1], "fsdp", 2), swap(attn_out[1], "fsdp", 2)
    grad_sent = dispatch(grad_sent)
    heads_one = exchange(heads_one)
    heads_one, far_in, far_out = lax.optimization_barrier((heads_one, far_in, far_out))
    w_attn_in_two, w_attn_out_two = [
        (own, swap(own, "fsdp", 1), far, swap(far, "fsdp", 1))
        for own, far in ((attn_in[1], far_in), (attn_out[1], far_out))
    ]
    after_one, _, blocks_one, keep_one, send_one, att_keep_one, att_send_one = post(
        meta, resid_in, gains[1], heads_one, w_attn_out_one
    )
    after_one, grad_sent, expert_part = lax.optimization_barrier(
        (after_one, grad_sent, expert_part)
    )
    expert_w = lax.all_to_all(expert_part, "fsdp", 0, 0, tiled=True)
    middle, mixed_one, hid_keep_one, hid_send_one = mlp(
        meta, after_one, blocks_one, w_mlp_in_one, w_mlp_out_one
    )
    near_one = near(send_one, att_send_one, hid_send_one)
    heads_two, kept_two, grad_sent = attend_forward(
        meta, count, middle, gains[2], tables, w_attn_in_two, grad_sent
    )
    grad_arrived = to_units(grad_sent[:, :capacity].reshape(slot_count, model_width))
    arrived_ids = jnp.concatenate(
        to_units(grad_sent[:, capacity, :capacity].astype(jnp.float32))
    ).reshape(-1, 1)
    heads_two, grad_arrived, arrived_ids = lax.optimization_barrier(
        (heads_two, grad_arrived, arrived_ids)
    )
    heads_two = exchange(heads_two)
    heads_two, w_attn_out_two, expert_w = lax.optimization_barrier(
        (heads_two, w_attn_out_two, expert_w)
    )
    after_two, normed_three, blocks_two, keep_two, send_two, att_keep_two, att_send_two = post(
        meta, middle, gains[3], heads_two, w_attn_out_two
    )

    rows_sent = send_rows(normed_three)
    shared, mixed_two, hid_keep_two, hid_send_two = mlp(
        meta, after_two, blocks_two, w_mlp_in_two, w_mlp_out_two
    )
    grad_mixed_two, grad_shared_in = mlp_back(
        meta, cotangent, mixed_two, w_mlp_in_two, w_mlp_out_two
    )
    grad_mlp_out_two = weight_grad(
        meta, hid_keep_two, *near(hid_send_two), cotangent, *near(cotangent)
    )
    logits = jnp.dot(normed_three, router_full, preferred_element_type=jnp.float32)
    picked = jnp.sum(jnp.where(chosen, logits[:, None, :], 0.0), axis=-1)
    gate_probs = jax.nn.softmax(picked, axis=-1)
    rows_sent, grad_shared_in, grad_mlp_out_two, gate_probs = lax.optimization_barrier(
        (rows_sent, grad_shared_in, grad_mlp_out_two, gate_probs)
    )
    sum_mlp_out_two = add_arrived(grad_mlp_out_two)
    router_wide = jnp.pad(router_full, ((0, 0), (0, 128 - num_experts)))
    own_expert = ((own_ctx * fsdp_count + own_fsdp) // units).reshape(1)
    partial_rows, partial_back, kept_rows = experts(
        own_expert,
        to_units(rows_sent.reshape(slot_count, model_width)),
        grad_arrived,
        router_wide,
        arrived_ids,
        expert_w,
    )
    arrived, grad_rows, hidden_rows, grad_gate, grad_up, dots = kept_rows
    dots = from_units(dots.reshape(units, num_experts, capacity))
    coarse = lax.optimization_barrier(dots.astype(jnp.bfloat16))
    payload = with_notes(
        from_units(partial_back).astype(jnp.bfloat16).reshape(num_experts, capacity, model_width),
        coarse,
        dots - coarse.astype(jnp.float32),
    )
    payload, kept_rows, partial_rows = lax.optimization_barrier((payload, kept_rows, partial_rows))
    arrived, grad_rows, hidden_rows, grad_gate, grad_up, _ = kept_rows
    back = dispatch(payload)
    grad_experts = jnp.stack(
        [
            jnp.einsum("rd,rf->df", left, right, preferred_element_type=jnp.float32)
            .astype(jnp.bfloat16)
            .reshape(fsdp_count, shard_width, hid_unit)
            for left, right in ((arrived, grad_gate), (arrived, grad_up), (grad_rows, hidden_rows))
        ],
        axis=1,
    )
    grad_mlp_in_two = weight_grad(
        meta, keep_two, *near(send_two), grad_mixed_two, *near(grad_mixed_two)
    )
    back, grad_experts, grad_mlp_in_two, sum_mlp_out_two = lax.optimization_barrier(
        (back, grad_experts, grad_mlp_in_two, sum_mlp_out_two)
    )
    grad_out = cotangent[0].astype(jnp.float32)
    stride = back.shape[1]
    notes = back[:, capacity : capacity + 2, :capacity].astype(jnp.float32)
    slot_dots = jnp.sum(notes, axis=1).reshape(1, slot_count)
    grad_gates = jnp.stack(
        [
            jnp.sum(
                jnp.where(slots[None, :] == slot_target[:, k, None], slot_dots, 0.0), axis=-1
            )
            for k in range(TOP)
        ],
        axis=1,
    )
    grad_picked = gate_probs * (
        grad_gates - jnp.sum(gate_probs * grad_gates, axis=-1, keepdims=True)
    )
    grad_logits = jnp.sum(jnp.where(chosen, grad_picked[..., None], 0.0), axis=1)
    grad_router = jnp.einsum(
        "te,td->ed", grad_logits, normed_three.astype(jnp.float32), precision=HIGHEST
    )
    wide = jnp.arange(num_experts * stride, dtype=jnp.int32)[None, :]
    wide_target = slot_target + (stride - capacity) * routes[0]
    spread = (wide == wide_target[:, 0, None]) | (wide == wide_target[:, 1, None])
    grad_normed = (
        grad_shared_in
        + jnp.dot(
            spread.astype(jnp.bfloat16),
            back.reshape(num_experts * stride, model_width),
            preferred_element_type=jnp.float32,
        )
        + jnp.einsum(
            "te,de->td", grad_logits, router_full.astype(jnp.float32), precision=HIGHEST
        )
    )
    grad_heads, grad_resid, branch, gain_three = post_back(
        meta, after_two, gains[3], grad_out, grad_normed, w_attn_out_two
    )
    grad_heads = exchange(grad_heads)
    grad_attn_out_two = weight_grad(
        meta, att_keep_two, *near(att_send_two), branch, *near(branch)
    )
    sum_mlp_in_two = add_arrived(grad_mlp_in_two)
    grad_heads, grad_attn_out_two, grad_experts, sum_mlp_in_two, sum_mlp_out_two = (
        lax.optimization_barrier(
            (grad_heads, grad_attn_out_two, grad_experts, sum_mlp_in_two, sum_mlp_out_two)
        )
    )
    grad_experts = lax.all_to_all(grad_experts, "fsdp", 0, 0, tiled=True)
    grad_q, own, others = attend_back(
        meta, kept_two[2], grad_heads, kept_two[3], kept_two[4], count
    )
    arrived_kv = [swap(values, "ctx", part + 1) for part, values in enumerate(others)]
    sum_attn_out_two = add_arrived(grad_attn_out_two)
    grad_qkv = exchange(merge(meta, grad_q, own, arrived_kv))
    expert_rows = from_units(partial_rows).astype(jnp.bfloat16)
    sums_two = jnp.concatenate(
        [sum_mlp_in_two, sum_mlp_out_two.reshape(shard_width, -1)], axis=1
    ).reshape(ctx_count, shard_width // ctx_count, -1)
    grad_qkv, expert_rows, grad_experts, sums_two, sum_attn_out_two = lax.optimization_barrier(
        (grad_qkv, expert_rows, grad_experts, sums_two, sum_attn_out_two)
    )
    sums_two = lax.all_to_all(sums_two, "ctx", 0, 0, tiled=True)
    grad_mixed, grad_resid, gain_two = pre_back(
        meta, middle, gains[2], tables, grad_resid, grad_qkv, w_attn_in_two
    )
    near_qkv = near(kept_two[1], grad_mixed)
    branch = grad_resid.astype(jnp.bfloat16)[None]
    grad_mixed_one, grad_normed = mlp_back(
        meta, branch, mixed_one, w_mlp_in_one, w_mlp_out_one
    )
    grad_attn_in_two = weight_grad(meta, kept_two[0], near_qkv[0], grad_mixed, near_qkv[1])
    grad_normed, grad_attn_in_two = lax.optimization_barrier((grad_normed, grad_attn_in_two))
    near_mixed = [None] + near(branch, grad_mixed_one)
    grad_heads, grad_resid, att_branch, gain_one = post_back(
        meta, after_one, gains[1], grad_resid, grad_normed, w_attn_out_one
    )
    near_branch = near(att_branch)[0]
    grad_heads = exchange(grad_heads)
    grad_mlp_in_one = weight_grad(meta, keep_one, near_one[0], grad_mixed_one, near_mixed[2])
    first_sent = jnp.concatenate([grad_mlp_in_one[1], grad_attn_in_two[1]], axis=1)
    grad_heads, first_sent, expert_rows, sums_two = lax.optimization_barrier(
        (grad_heads, first_sent, expert_rows, sums_two)
    )
    sums_two = jnp.sum(sums_two.astype(jnp.float32), axis=0).astype(jnp.bfloat16)
    sums_two = lax.all_gather(sums_two, "ctx", axis=0, tiled=True)
    expert_rows = dispatch(expert_rows.reshape(num_experts, capacity, model_width))
    expert_rows = expert_rows.reshape(slot_count, model_width)
    first_arrived = swap(first_sent, "fsdp", 2)
    grad_q, own, others = attend_back(
        meta, kept_one[2], grad_heads, kept_one[3], kept_one[4], count
    )
    arrived_kv = [swap(values, "ctx", part + 1) for part, values in enumerate(others)]
    grad_mlp_out_one = weight_grad(meta, hid_keep_one, near_one[2], branch, near_mixed[1])
    grad_attn_out_one = weight_grad(meta, att_keep_one, near_one[1], att_branch, near_branch)
    second_sent = jnp.concatenate([grad_mlp_out_one[1], grad_attn_out_one[1]], axis=0)
    wide = grad_mlp_in_one[0].shape[1]
    first_sums = (
        grad_attn_in_two[0] + first_arrived[:, wide:],
        grad_mlp_in_one[0] + first_arrived[:, :wide],
    )
    arrived_kv, second_sent, first_sums = lax.optimization_barrier(
        (arrived_kv, second_sent, first_sums)
    )
    grad_qkv = exchange(merge(meta, grad_q, own, arrived_kv))
    second_arrived = swap(second_sent, "fsdp", 2)
    tall = grad_mlp_out_one[0].shape[0]
    sums_one = [
        *first_sums,
        grad_attn_out_one[0] + second_arrived[tall:],
        sum_attn_out_two,
    ]
    grad_qkv, expert_rows, sums_two, *sums_one = lax.optimization_barrier(
        (grad_qkv, expert_rows, sums_two, *sums_one)
    )
    sums_one = total(1, sums_one)
    grad_mixed, grad_resid, gain_zero = pre_back(
        meta, resid_in, gains[0], tables, grad_resid, grad_qkv, w_attn_in_one
    )
    near_qkv = near(kept_one[1], grad_mixed)
    grad_attn_in_one = weight_grad(meta, kept_one[0], near_qkv[0], grad_mixed, near_qkv[1])
    grad_attn_in_one, expert_rows, grad_experts = lax.optimization_barrier(
        (grad_attn_in_one, expert_rows, grad_experts)
    )
    grad_experts = jnp.transpose(grad_experts, (1, 2, 0, 3)).astype(jnp.float32)
    grad_experts = grad_experts.reshape(3, shard_width, hid_unit * fsdp_count)
    back_rows = [jnp.dot(p, expert_rows, preferred_element_type=jnp.float32) for p in of_token]
    output = shared + sum(gate_probs[:, k, None] * back_rows[k] for k in range(TOP))
    small_grads = jnp.concatenate([gain_zero, gain_one, gain_two, gain_three, grad_router])
    wide = sums_one[1].shape[1]
    (attn_in_grad, mlp_out_grad), sums_one, small_grads = reduce_last(
        at_ctx,
        [
            (grad_attn_in_one[0], swap(grad_attn_in_one[1], "fsdp", 2), sums_one[0]),
            (
                grad_mlp_out_one[0],
                second_arrived[:tall],
                sums_two[:, wide:].reshape(tall, model_width),
            ),
        ],
        sums_one,
        small_grads,
    )
    small_grads = lax.dynamic_slice_in_dim(small_grads, own_fsdp * shard_width, shard_width, 1)
    attn_out_grad, mlp_in_grad = [
        jnp.stack(pair).astype(jnp.float32)
        for pair in ((sums_one[2], sums_one[3]), (sums_one[1], sums_two[:, :wide]))
    ]
    return (
        output[None],
        grad_resid[None],
        attn_in_grad,
        attn_out_grad,
        small_grads[:4].reshape(2, 2, shard_width),
        mlp_in_grad,
        mlp_out_grad,
        small_grads[4:].T,
        jnp.swapaxes(grad_experts[:2], 1, 2),
        grad_experts[2].T,
    )


def solution(mesh):
    placed = (
        P("fsdp", "ctx", None),
        P("fsdp", "ctx", None),
        P("fsdp", None),
        P("fsdp", None),
        P("fsdp", "ctx", None),
        P(None, "fsdp", None),
        P(None, "fsdp", None),
        P(None, None, "fsdp"),
        P(None, "fsdp", None),
        P(None, "fsdp", None),
        P("fsdp", None),
        P(None, "ctx", "fsdp"),
        P("ctx", "fsdp"),
    )
    return jax.shard_map(
        per_device,
        mesh=mesh,
        in_specs=placed,
        out_specs=(
            P("fsdp", "ctx", None),
            P("fsdp", "ctx", None),
            P(None, "fsdp", None),
            P(None, "fsdp", None),
            P(None, None, "fsdp"),
            P(None, "fsdp", None),
            P(None, "fsdp", None),
            P("fsdp", None),
            P(None, "ctx", "fsdp"),
            P("ctx", "fsdp"),
        ),
        check_vma=False,
    )
```

```python
import functools
import math

import jax
import jax.numpy as jnp
from jax import lax
from jax.experimental import pallas as pl
from jax.experimental.pallas import tpu as pltpu
from jax.sharding import PartitionSpec as P

HEADS = 12
HD = 64
FF = 2048
TOP = 2
HEAD_GROUPS = 4
KEY_SPAN = 512
VMEM_LIMIT = 60 * 1024 * 1024


HIGHEST = lax.Precision.HIGHEST
EPSILON = 1e-06
NEGATIVE = -1e30


BOTH = ("ctx", "fsdp")


def swap(values, axis, mask):
    count = lax.axis_size(axis)
    return lax.ppermute(values, axis, [(i, i ^ mask) for i in range(count)])


def gather_shards(shard):
    near = swap(shard, "fsdp", 1)
    far = swap(shard, "fsdp", 2)
    return (shard, near, far, swap(far, "fsdp", 1))


def in_order(shards):
    own = lax.axis_index("fsdp")
    buffer = jnp.zeros((len(shards),) + shards[0].shape, shards[0].dtype)
    for k, shard in enumerate(shards):
        buffer = lax.dynamic_update_index_in_dim(buffer, shard, own ^ k, 0)
    return buffer


NT = (((1,), (1,)), ((), ()))


def _dot(a, b):
    return jnp.dot(a, b, preferred_element_type=jnp.float32)


def _dot_nt(a, b):
    return lax.dot_general(a, b, NT, preferred_element_type=jnp.float32)


def _flip(values):
    return values.astype(jnp.float32).T.astype(values.dtype)


def _shape(shape, dtype=jnp.bfloat16):
    return jax.ShapeDtypeStruct(shape, dtype)


def _whole(shape):
    return pl.BlockSpec(tuple(shape), lambda *_: (0,) * len(shape))


def operands(shards, part=None):
    if isinstance(shards, (tuple, list)):
        arrays, rows, place = shards, shards[0].shape[0], lambda m, k: 0
    else:
        arrays, rows, place = (shards,) * 4, shards.shape[0] // 4, lambda m, k: m[0] ^ k
    width = arrays[0].shape[1]
    if part is None:
        specs = [
            pl.BlockSpec((rows, width), lambda i, m, k=k: (place(m, k), 0)) for k in range(4)
        ]
    else:
        size, first = part
        specs = [
            pl.BlockSpec((rows, size), lambda i, m, k=k: (place(m, k), first + (m[0] ^ i)))
            for k in range(4)
        ]
    return list(arrays), specs


def call(body, meta, inputs, outputs, scratch=(), flops=0, in_specs=None, out_specs=None, grid=(1,)):
    moved = sum(math.prod(a.shape) * a.dtype.itemsize for a in (*inputs, *outputs))
    return pl.pallas_call(
        body,
        grid_spec=pltpu.PrefetchScalarGridSpec(
            num_scalar_prefetch=1,
            grid=grid,
            in_specs=in_specs or [_whole(a.shape) for a in inputs],
            out_specs=out_specs or [_whole(a.shape) for a in outputs],
            scratch_shapes=list(scratch),
        ),
        out_shape=list(outputs),
        compiler_params=pltpu.CompilerParams(vmem_limit_bytes=VMEM_LIMIT),
        cost_estimate=pl.CostEstimate(flops=flops, bytes_accessed=moved, transcendentals=0),
    )(meta, *inputs)


def _stack(refs, cols=slice(None)):
    return jnp.concatenate([w[:, cols] for w in refs], axis=0)


def _mine(blocks, own):
    return jnp.concatenate([blocks[own ^ k] for k in range(4)], axis=1)


def _norm(rows, gain):
    inverse = lax.rsqrt(jnp.mean(rows * rows, axis=-1, keepdims=True) + EPSILON)
    return rows * inverse * gain


def _norm_back(rows, gain, grad):
    inverse = lax.rsqrt(jnp.mean(rows * rows, axis=-1, keepdims=True) + EPSILON)
    weighted = grad * gain
    scaled = rows * inverse
    back = inverse * (weighted - scaled * jnp.mean(weighted * scaled, axis=-1, keepdims=True))
    return back, jnp.sum(grad * scaled, axis=0, keepdims=True)


def _split(rows, blocks):
    width = rows.shape[1] // len(blocks)
    for b, ref in enumerate(blocks):
        ref[...] = rows[:, b * width : (b + 1) * width]


def _turn(rows, cosine, sine, sign):
    lane = lax.broadcasted_iota(jnp.int32, cosine.shape, 1)
    low = lane % HD < HD // 2
    turned = []
    for b in range(rows.shape[1] // 128):
        part = rows[:, b * 128 : (b + 1) * 128]
        other = jnp.where(low, pltpu.roll(part, 128 - HD // 2, 1), pltpu.roll(part, HD // 2, 1))
        turned.append(part * cosine + sign * (other * sine))
    return jnp.concatenate(turned, axis=1)


def _pre_kernel(meta, x, gain, cosine, sine, w0, w1, w2, w3, keep, send, *rest):
    qkv, (blocks, heads) = rest[:4], rest[4:]
    own, line = meta[0], meta[1]
    width = x.shape[1]
    normed = _norm(x[...], gain[...]).astype(jnp.bfloat16)
    _split(normed, [blocks.at[b] for b in range(4)])
    for j in range(2):
        keep[j] = blocks[own ^ (2 * j)]
        send[j] = blocks[own ^ (2 * j + 1)]
    piece = x.shape[0] // 2
    mine = _mine(blocks, own)
    for kind in range(3):
        mixed = _dot(mine, _stack((w0, w1, w2, w3), slice(kind * width, (kind + 1) * width)))
        if kind < 2:
            mixed = _turn(mixed, cosine[...], sine[...], 1.0)
        if kind == 0:
            mixed = mixed * 0.125
        turned = mixed.T.astype(jnp.bfloat16)
        block = width // 4
        for b in range(4):
            for p in range(2):
                heads[b, p, kind] = turned[
                    b * block : (b + 1) * block, p * piece : (p + 1) * piece
                ]
    for k in range(4):
        qkv[k][...] = heads[line ^ k]


def pre(meta, x, gain, tables, shards):
    rows, width = x.shape
    block = width // 4
    outs = [_shape((2, rows, block))] * 2 + [_shape((2, 3, block, rows // 2))] * 4
    shards, specs = operands(shards)
    inputs = (x, gain, *tables)
    got = call(
        _pre_kernel,
        meta,
        (*inputs, *shards),
        outs,
        [
            pltpu.VMEM((4, rows, block), jnp.bfloat16),
            pltpu.VMEM((4, 2, 3, block, rows // 2), jnp.bfloat16),
        ],
        flops=6 * rows * width * width,
        in_specs=[_whole(a.shape) for a in inputs] + specs,
    )
    return got[0], got[1], got[2:6]


def _pre_back_kernel(meta, x, gain, cosine, sine, resid, *rest):
    qkv, w = rest[:4], rest[4:8]
    mixed_out, resid_out, gain_out, heads, blocks = rest[8:]
    own, line = meta[0], meta[1]
    width = x.shape[1]
    for k in range(4):
        heads[line ^ k] = qkv[k][...]
    for kind in range(3):
        mixed = jnp.concatenate(
            [
                jnp.concatenate([heads[b, p, kind] for b in range(4)], axis=0)
                for p in range(2)
            ],
            axis=1,
        )
        mixed = mixed.astype(jnp.float32).T
        if kind < 2:
            mixed = mixed * (0.125 if kind == 0 else 1.0)
            mixed = _turn(mixed, cosine[...], sine[...], -1.0)
        mixed_out[0, :, kind * width : (kind + 1) * width] = mixed.astype(jnp.bfloat16)
    grads = _dot_nt(mixed_out[0], _stack(w))
    _split(grads, [blocks.at[own ^ k] for k in range(4)])
    grad = jnp.concatenate([blocks[b] for b in range(4)], axis=1)
    back, grad_gain = _norm_back(x[...], gain[...], grad)
    resid_out[...] = resid[...] + back
    gain_out[...] = grad_gain


def pre_back(meta, x, gain, tables, resid, qkv, shards):
    rows, width = x.shape
    shards, specs = operands(shards)
    inputs = (x, gain, *tables, resid, *qkv)
    return call(
        _pre_back_kernel,
        meta,
        (*inputs, *shards),
        [
            _shape((1, rows, 3 * width)),
            _shape((rows, width), jnp.float32),
            _shape((1, width), jnp.float32),
        ],
        [
            pltpu.VMEM((4, 2, 3, width // 4, rows // 2), jnp.bfloat16),
            pltpu.VMEM((4, rows, width // 4), jnp.float32),
        ],
        flops=6 * rows * width * width,
        in_specs=[_whole(a.shape) for a in inputs] + specs,
    )


def _post_kernel(meta, x, gain, o0, o1, o2, o3, w0, w1, w2, w3, *rest):
    after, plain, blocks_out, keep, send, att_keep, att_send, att = rest
    own, line = meta[0], meta[1]
    piece = x.shape[0] // 2
    for k, o in enumerate((o0, o1, o2, o3)):
        for p in range(2):
            att[line ^ k, p * piece : (p + 1) * piece, :] = _flip(o[p])
    for j in range(2):
        att_keep[j] = att[own ^ (2 * j)]
        att_send[j] = att[own ^ (2 * j + 1)]
    rows = x[...] + _dot(_mine(att, own), _stack((w0, w1, w2, w3)))
    after[...] = rows
    normed = _norm(rows, gain[...]).astype(jnp.bfloat16)
    plain[...] = normed
    _split(normed, [att.at[b] for b in range(4)])
    blocks_out[...] = att[...]
    for j in range(2):
        keep[j] = att[own ^ (2 * j)]
        send[j] = att[own ^ (2 * j + 1)]


def post(meta, x, gain, heads, shards):
    rows, width = x.shape
    block = width // 4
    shards, specs = operands(shards)
    inputs = (x, gain, *heads)
    return call(
        _post_kernel,
        meta,
        (*inputs, *shards),
        [_shape((rows, width), jnp.float32), _shape((rows, width)), _shape((4, rows, block))]
        + [_shape((2, rows, block))] * 4,
        [pltpu.VMEM((4, rows, block), jnp.bfloat16)],
        flops=2 * rows * width * width,
        in_specs=[_whole(a.shape) for a in inputs] + specs,
    )


def _post_back_kernel(meta, x, gain, resid, grad, w0, w1, w2, w3, *rest):
    heads, (resid_out, branch, gain_out, att) = rest[:4], rest[4:]
    own, line = meta[0], meta[1]
    back, grad_gain = _norm_back(x[...], gain[...], grad[...])
    gain_out[...] = grad_gain
    rows = resid[...] + back
    resid_out[...] = rows
    rows = rows.astype(jnp.bfloat16)
    branch[0] = rows
    grads = _dot_nt(rows, _stack((w0, w1, w2, w3))).astype(jnp.bfloat16)
    _split(grads, [att.at[own ^ k] for k in range(4)])
    piece = x.shape[0] // 2
    for k in range(4):
        for p in range(2):
            heads[k][p] = _flip(att[line ^ k, p * piece : (p + 1) * piece, :])


def post_back(meta, x, gain, resid, grad, shards):
    rows, width = x.shape
    block = width // 4
    shards, specs = operands(shards)
    inputs = (x, gain, resid, grad)
    got = call(
        _post_back_kernel,
        meta,
        (*inputs, *shards),
        [_shape((2, block, rows // 2))] * 4
        + [
            _shape((rows, width), jnp.float32),
            _shape((1, rows, width)),
            _shape((1, width), jnp.float32),
        ],
        [pltpu.VMEM((4, rows, block), jnp.bfloat16)],
        flops=2 * rows * width * width,
        in_specs=[_whole(a.shape) for a in inputs] + specs,
    )
    return got[:4], got[4], got[5], got[6]


def _mlp_kernel(meta, x, blocks, *rest):
    gates, ups, downs = rest[:4], rest[4:8], rest[8:12]
    out, mixed, keep, send, acc = rest[12:]
    own, step = meta[0], pl.program_id(0)
    rows = _mine(blocks, own)
    gate = _dot(rows, _stack(gates))
    up = _dot(rows, _stack(ups))
    mixed[0], mixed[1] = gate, up
    hidden = (gate * jax.nn.sigmoid(gate) * up).astype(jnp.bfloat16)
    for k in range(4):

        @pl.when(step == k)
        def _(k=k):
            (send if k % 2 else keep)[k // 2] = hidden
            part = _dot(hidden, downs[k][...])
            if k == 0:
                acc[...] = x[...] + part
            elif k < 3:
                acc[...] += part
            else:
                out[...] = acc[...] + part


def mlp_width(shards):
    first = shards[0] if isinstance(shards, (tuple, list)) else shards
    return first.shape[1] // 2


def mlp(meta, x, blocks, shards_in, shards_out):
    rows, width = x.shape
    hidden = mlp_width(shards_in)
    part = hidden // 4
    gates, gate_specs = operands(shards_in, (part, 0))
    ups, up_specs = operands(shards_in, (part, 4))
    downs, down_specs = operands(shards_out)
    return call(
        _mlp_kernel,
        meta,
        (x, blocks, *gates, *ups, *downs),
        [
            _shape((rows, width), jnp.float32),
            _shape((2, rows, hidden), jnp.float32),
            _shape((2, rows, part)),
            _shape((2, rows, part)),
        ],
        [pltpu.VMEM((rows, width), jnp.float32)],
        flops=6 * rows * width * hidden,
        in_specs=[_whole(x.shape), _whole(blocks.shape), *gate_specs, *up_specs, *down_specs],
        out_specs=[
            _whole((rows, width)),
            pl.BlockSpec((2, rows, part), lambda i, m: (0, 0, m[0] ^ i)),
            _whole((2, rows, part)),
            _whole((2, rows, part)),
        ],
        grid=(4,),
    )


def _mlp_back_kernel(meta, branch, mixed, *rest):
    gates, ups, downs = rest[:4], rest[4:8], rest[8:12]
    grad_mixed, grad_out, grad_hidden, acc, turned = rest[12:]
    own, step = meta[0], pl.program_id(0)
    for k in range(4):

        @pl.when(step == k)
        def _(k=k):
            grad_hidden[...] = _dot_nt(branch[0], downs[k][...]).astype(jnp.bfloat16)

    grad_h = grad_hidden[...].astype(jnp.float32)
    gate, up = mixed[0], mixed[1]
    sigmoid = jax.nn.sigmoid(gate)
    grad_gate = (grad_h * up * sigmoid * (1.0 + gate * (1.0 - sigmoid))).astype(jnp.bfloat16)
    grad_up = (grad_h * gate * sigmoid).astype(jnp.bfloat16)
    grad_mixed[0], grad_mixed[1] = grad_gate, grad_up
    part = _dot_nt(grad_gate, _stack(gates)) + _dot_nt(grad_up, _stack(ups))

    @pl.when(step == 0)
    def _():
        acc[...] = part

    @pl.when((step > 0) & (step < 3))
    def _():
        acc[...] += part

    @pl.when(step == 3)
    def _():
        _split(acc[...] + part, [turned.at[own ^ k] for k in range(4)])
        grad_out[...] = jnp.concatenate([turned[b] for b in range(4)], axis=1)


def mlp_back(meta, branch, mixed, shards_in, shards_out):
    _, rows, width = branch.shape
    hidden = mixed.shape[2]
    part = hidden // 4
    block = width // 4
    gates, gate_specs = operands(shards_in, (part, 0))
    ups, up_specs = operands(shards_in, (part, 4))
    downs, down_specs = operands(shards_out)
    return call(
        _mlp_back_kernel,
        meta,
        (branch, mixed, *gates, *ups, *downs),
        [_shape((2, rows, hidden)), _shape((rows, width), jnp.float32)],
        [
            pltpu.VMEM((rows, part), jnp.bfloat16),
            pltpu.VMEM((rows, width), jnp.float32),
            pltpu.VMEM((4, rows, block), jnp.float32),
        ],
        flops=6 * rows * width * hidden,
        in_specs=[
            _whole(branch.shape),
            pl.BlockSpec((2, rows, part), lambda i, m: (0, 0, m[0] ^ i)),
            *gate_specs,
            *up_specs,
            *down_specs,
        ],
        out_specs=[
            pl.BlockSpec((2, rows, part), lambda i, m: (0, 0, m[0] ^ i)),
            _whole((rows, width)),
        ],
        grid=(4,),
    )


def _grad_kernel(meta, left, left_near, right, right_near, own, send, flipped):
    rows, depth = left.shape[1:]

    @pl.when((pl.program_id(0) == 0) & (pl.program_id(1) == 0))
    def _():
        for j in range(2):
            flipped[j * depth : (j + 1) * depth, :rows] = _flip(left[j])
            flipped[j * depth : (j + 1) * depth, rows:] = _flip(left_near[j])

    both = jnp.concatenate([right[0], right_near[0]], axis=0)
    grads = _dot(flipped[...], both).astype(jnp.bfloat16)
    own[...] = grads[:depth]
    send[...] = grads[depth:]


def weight_grad(meta, left, left_near, right, right_near):
    groups, rows, width = right.shape
    depth = left.shape[2]
    chunk = 512 if width % 768 else 768
    steps = width // chunk
    right_spec = pl.BlockSpec((1, rows, chunk), lambda g, i, m: (g, 0, i))
    out_spec = pl.BlockSpec((depth, chunk), lambda g, i, m: (0, g * steps + i))
    return call(
        _grad_kernel,
        meta,
        (left, left_near, right, right_near),
        [_shape((depth, groups * width))] * 2,
        [pltpu.VMEM((2 * depth, 2 * rows), jnp.bfloat16)],
        flops=8 * rows * depth * groups * width,
        in_specs=[_whole(left.shape), _whole(left.shape), right_spec, right_spec],
        out_specs=[out_spec, out_spec],
        grid=(groups, steps),
    )


def _mask(first_key, keys, query_pos, query_start, copies):
    key_pos = first_key + lax.broadcasted_iota(jnp.int32, (keys, query_pos.shape[1]), 0)
    allowed = (key_pos <= query_pos) & (key_pos >= query_start)
    return jnp.concatenate([allowed] * copies, axis=1)


def _tables(meta, parts):
    return (lambda s: meta[2 + s], lambda k: meta[2 + 8 * parts + k])


def _query_geometry(place, ends, count, piece, key_span):
    query_pos = place * piece + lax.broadcasted_iota(jnp.int32, (1, piece), 1)
    query_start = jnp.zeros_like(query_pos)
    first = place * piece
    least = jnp.int32(0)
    for k in range(count):
        last = k == count - 1
        query_start = jnp.where(query_pos >= ends(k), query_pos if last else ends(k), query_start)
        least = jnp.where(first >= ends(k), first if last else ends(k), least)
    return (query_pos, query_start, least // key_span, (first + piece - 1) // key_span + 1)


def _stack_heads(rows, heads):
    head_dim = rows.shape[0] // heads
    head = lax.broadcasted_iota(jnp.int32, rows.shape, 0) // head_dim
    zero = jnp.zeros_like(rows)
    return jnp.concatenate([jnp.where(head == h, rows, zero) for h in range(heads)], axis=1)


def _own_heads(acc, heads, piece):
    head_dim = acc.shape[0] // heads
    return jnp.concatenate(
        [
            acc[h * head_dim : (h + 1) * head_dim, h * piece : (h + 1) * piece]
            for h in range(heads)
        ],
        axis=0,
    )


def _attend_kernel(heads, count, key_span, parts, meta, *refs):
    inputs, o, (keep, lse, keys, values_t) = (
        refs[: 4 * parts],
        refs[4 * parts : 4 * parts + 4],
        refs[4 * parts + 4 :],
    )
    width, piece = inputs[0].shape[2:]
    place, ends = _tables(meta, parts)
    for s in range(8 * parts):
        at = pl.ds(pl.multiple_of(place(s) * piece, piece), piece)
        keys[at, :] = _flip(inputs[s // 2][s % 2, 1])
        values_t[:, at] = inputs[s // 2][s % 2, 2]
    cols = heads * piece
    for s in range(8):
        query_pos, query_start, begin, end = _query_geometry(
            place(s), ends, count, piece, key_span
        )
        stacked = _stack_heads(inputs[s // 2][s % 2, 0], heads)

        def advance(block, carried):
            run_max, run_sum, acc = carried
            first = pl.multiple_of(block * key_span, key_span)
            scores = _dot(keys[pl.ds(first, key_span), :], stacked)
            allowed = _mask(first, key_span, query_pos, query_start, heads)
            scores = jnp.where(allowed, scores, NEGATIVE)
            new_max = jnp.maximum(run_max, jnp.max(scores, axis=0, keepdims=True))
            weights = jnp.exp(scores - new_max)
            factor = jnp.exp(run_max - new_max)
            run_sum = run_sum * factor + jnp.sum(weights, axis=0, keepdims=True)
            part = _dot(values_t[:, pl.ds(first, key_span)], weights.astype(jnp.bfloat16))
            return (new_max, run_sum, acc * factor + part)

        run_max, run_sum, acc = lax.fori_loop(
            begin,
            end,
            advance,
            (
                jnp.full((1, cols), NEGATIVE, jnp.float32),
                jnp.zeros((1, cols), jnp.float32),
                jnp.zeros((width, cols), jnp.float32),
            ),
        )
        kept = _own_heads(acc / run_sum, heads, piece)
        keep[s] = kept
        o[s // 2][s % 2] = kept.astype(jnp.bfloat16)
        lse[s] = run_max + jnp.log(run_sum)


def attend(meta, inputs, count):
    _, _, width, piece = inputs[0].shape
    heads = width // HD
    parts = len(inputs) // 4
    slots = parts * 8 * piece
    got = call(
        functools.partial(_attend_kernel, heads, count, KEY_SPAN, parts),
        meta,
        inputs,
        [_shape((2, width, piece))] * 4
        + [_shape((8, width, piece), jnp.float32), _shape((8, 1, heads * piece), jnp.float32)],
        [
            pltpu.VMEM((slots, width), jnp.bfloat16),
            pltpu.VMEM((width, slots), jnp.bfloat16),
        ],
        flops=32 * piece * slots * width,
    )
    return got[:4], got[4], got[5]


def _attend_back_kernel(heads, count, key_span, parts, meta, *refs):
    inputs, grads, (keep, lse), rest = (
        refs[: 4 * parts],
        refs[4 * parts : 4 * parts + 4],
        refs[4 * parts + 4 : 4 * parts + 6],
        refs[4 * parts + 6 :],
    )
    gq, gkv = rest[0], rest[1 : 1 + parts]
    keys, keys_t, values, gkeys, gvalues = rest[1 + parts :]
    width, piece = inputs[0].shape[2:]
    head_dim = width // heads
    place, ends = _tables(meta, parts)
    for s in range(8 * parts):
        at = pl.ds(pl.multiple_of(place(s) * piece, piece), piece)
        key_rows = inputs[s // 2][s % 2, 1]
        keys_t[:, at] = key_rows
        keys[at, :] = _flip(key_rows)
        values[at, :] = _flip(inputs[s // 2][s % 2, 2])
    gkeys[...] = jnp.zeros_like(gkeys)
    gvalues[...] = jnp.zeros_like(gvalues)
    for s in range(8):
        query_pos, query_start, begin, end = _query_geometry(
            place(s), ends, count, piece, key_span
        )
        stacked = _stack_heads(inputs[s // 2][s % 2, 0], heads)
        grad = grads[s // 2][s % 2]
        grad_stacked = _stack_heads(grad, heads)
        product = grad.astype(jnp.float32) * keep[s]
        delta = jnp.concatenate(
            [
                jnp.sum(product[h * head_dim : (h + 1) * head_dim, :], axis=0, keepdims=True)
                for h in range(heads)
            ],
            axis=1,
        )
        log_sum = lse[s]

        def retreat(block, acc):
            first = pl.multiple_of(block * key_span, key_span)
            at = pl.ds(first, key_span)
            scores = _dot(keys[at, :], stacked)
            allowed = _mask(first, key_span, query_pos, query_start, heads)
            probs = jnp.where(allowed, jnp.exp(scores - log_sum), 0.0)
            grad_probs = _dot(values[at, :], grad_stacked)
            grad_scores = (probs * (grad_probs - delta)).astype(jnp.bfloat16)
            gvalues[:, at] += _dot_nt(grad_stacked, probs.astype(jnp.bfloat16))
            gkeys[:, at] += _dot_nt(stacked, grad_scores)
            return acc + _dot(keys_t[:, at], grad_scores)

        acc = lax.fori_loop(begin, end, retreat, jnp.zeros((width, heads * piece), jnp.float32))
        gq[s] = _own_heads(acc, heads, piece).astype(jnp.bfloat16)
    for s in range(8 * parts):
        at = pl.ds(pl.multiple_of(place(s) * piece, piece), piece)
        out = gkv[s // 8]
        out[s % 8, 0] = gkeys[:, at].astype(out.dtype)
        out[s % 8, 1] = gvalues[:, at].astype(out.dtype)


def attend_back(meta, inputs, grads, keep, lse, count):
    _, _, width, piece = inputs[0].shape
    heads = width // HD
    parts = len(inputs) // 4
    slots = parts * 8 * piece
    got = call(
        functools.partial(_attend_back_kernel, heads, count, KEY_SPAN, parts),
        meta,
        (*inputs, *grads, keep, lse),
        [_shape((8, width, piece)), _shape((8, 2, width, piece), jnp.float32)]
        + [_shape((8, 2, width, piece))] * (parts - 1),
        [
            pltpu.VMEM((slots, width), jnp.bfloat16),
            pltpu.VMEM((width, slots), jnp.bfloat16),
            pltpu.VMEM((slots, width), jnp.bfloat16),
            pltpu.VMEM((width, slots), jnp.float32),
            pltpu.VMEM((width, slots), jnp.float32),
        ],
        flops=80 * piece * slots * width,
    )
    return got[0], got[1], got[2:]


def _merge_kernel(meta, gq, own, *rest):
    arrived, out = rest[:-4], rest[-4:]
    for s in range(8):
        total = own[s]
        for other in arrived:
            total = total + other[s].astype(jnp.float32)
        out[s // 2][s % 2, 0] = gq[s]
        out[s // 2][s % 2, 1:3] = total.astype(jnp.bfloat16)


def merge(meta, gq, own, arrived):
    _, width, piece = gq.shape
    return call(
        _merge_kernel, meta, (gq, own, *arrived), [_shape((2, 3, width, piece))] * 4
    )


def _halve_kernel(meta, first, second, sent, kept):
    summed = (first[...].astype(jnp.float32) + second[...].astype(jnp.float32)).astype(jnp.bfloat16)
    half = sent.shape[1]
    left, right = summed[:, :half], summed[:, half:]
    side = meta[0] == 0
    sent[...] = jnp.where(side, right, left)
    kept[...] = jnp.where(side, left, right)


def _quarter_kernel(meta, first, second, *rest):
    parts, summed = rest[:-1], rest[-1]
    summed[...] = (first[...].astype(jnp.float32) + second[...].astype(jnp.float32)).astype(
        jnp.bfloat16
    )
    chunk = parts[0].shape[0]
    for k, part in enumerate(parts):
        at = pl.multiple_of((meta[1] ^ k) * chunk, chunk)
        part[...] = summed[pl.ds(at, chunk), :]


def _place_kernel(meta, other, *refs):
    out, parts = refs[-1], refs[:-1]
    _, rows, width = out.shape
    lines = len(parts) // 2
    chunk, half = rows // lines, width // 2
    side = meta[0] == 0
    for k in range(lines):
        at = pl.multiple_of((meta[1] ^ k) * chunk, chunk)
        own = parts[k][...].astype(jnp.float32)
        near = parts[lines + k][...].astype(jnp.float32)
        out[0, pl.ds(at, chunk), :half] = jnp.where(side, own, near)
        out[0, pl.ds(at, chunk), half:] = jnp.where(side, near, own)
    out[1] = other[...].astype(jnp.float32)


def reduce_last(place, grads, held, small):
    lines = lax.axis_size("ctx") // 2
    if any(own.shape[0] // lines % 16 for own, _, _ in grads):
        outs = [
            jnp.stack([lax.psum(own + arrived, "ctx"), other]).astype(jnp.float32)
            for own, arrived, other in grads
        ]
        return outs, held, total_small(small)
    columns = []
    for i, (own, arrived, other) in enumerate(grads):
        rows, width = own.shape
        chunk, half = rows // lines, width // 2
        sent, kept = call(_halve_kernel, place, (own, arrived), [_shape((rows, half))] * 2)
        if i == 0:
            kept, small = lax.optimization_barrier((kept, small))
            small = total_small(small)
        parts = call(
            _quarter_kernel,
            place,
            (kept, swap(sent, "ctx", 1)),
            [_shape((chunk, half))] * lines,
            [pltpu.VMEM((rows, half), jnp.bfloat16)],
        )
        summed = parts[0].astype(jnp.float32)
        for k in range(1, lines):
            summed = summed + swap(parts[k], "ctx", 2 * k).astype(jnp.float32)
        summed = summed.astype(jnp.bfloat16)
        column = [swap(summed, "ctx", 2 * k) if k else summed for k in range(lines)]
        columns.append(column + [swap(c, "ctx", 1) for c in column])
    columns, held = lax.optimization_barrier((columns, held))
    outs = [
        call(
            _place_kernel,
            place,
            (other, *parts),
            [_shape((2, *own.shape), jnp.float32)],
        )[0]
        for (own, _, other), parts in zip(grads, columns)
    ]
    return outs, held, small


def _expert_kernel(units, meta, *refs):
    xs, cs = refs[:units], refs[units : 2 * units]
    router, ids, w = refs[2 * units : 2 * units + 3]
    outs = refs[2 * units + 3 :]
    parts, backs = outs[:units], outs[units : 2 * units]
    rows_out, grads_out, hidden_out, gate_out, up_out, dots_out = outs[2 * units : 2 * units + 6]
    gates, ups, downs, x, c = outs[2 * units + 6 :]
    step = pl.program_id(0)
    tiles = pl.num_programs(0) // units

    @pl.when(step == 0)
    def _():
        width = w.shape[2]
        for f in range(4):
            part = slice(f * width, (f + 1) * width)
            gates[part, :] = w[f, 0]
            ups[part, :] = w[f, 1]
            downs[part, :] = w[f, 2]

    for u in range(units):

        @pl.when(step // tiles == u)
        def _(u=u):
            x[...] = xs[u][...]
            c[...] = cs[u][...]

    rows = x[...]
    rows_out[...] = rows
    incoming = c[...].astype(jnp.float32)
    logits = _dot(rows, router[...])
    lane = lax.broadcasted_iota(jnp.int32, logits.shape, 1)
    gap = jnp.sum(
        jnp.where(lane == meta[0], logits, 0.0)
        - jnp.where(lane.astype(jnp.float32) == ids[...], logits, 0.0),
        axis=1,
        keepdims=True,
    )
    grads = (jax.nn.sigmoid(gap) * incoming).astype(jnp.bfloat16)
    grads_out[...] = grads
    gate = _dot(rows, gates[...])
    up = _dot(rows, ups[...])
    sigmoid = jax.nn.sigmoid(gate)
    silu = gate * sigmoid
    hidden = (silu * up).astype(jnp.bfloat16)
    hidden_out[...] = hidden
    part = _dot_nt(hidden, downs[...])
    dots_out[...] = jnp.sum(part * incoming, axis=1, keepdims=True)
    grad_h = _dot(grads, downs[...]).astype(jnp.bfloat16).astype(jnp.float32)
    grad_gate = (grad_h * up * sigmoid * (1.0 + gate * (1.0 - sigmoid))).astype(jnp.bfloat16)
    grad_up = (grad_h * silu).astype(jnp.bfloat16)
    gate_out[...] = grad_gate
    up_out[...] = grad_up
    back = _dot_nt(grad_gate, gates[...]) + _dot_nt(grad_up, ups[...])
    for u in range(units):

        @pl.when(step // tiles == u)
        def _(u=u):
            parts[u][...] = part.astype(jnp.bfloat16)
            backs[u][...] = back.astype(jnp.bfloat16)


def experts(meta, xs, cs, router, ids, w):
    units, (rows, width), tile = len(xs), xs[0].shape, 1024 // len(xs)
    tiles, hidden = rows // tile, w.shape[3]
    total_rows = units * rows
    slabs = [
        pl.BlockSpec((tile, width), lambda i, m, u=u: (jnp.clip(i - u * tiles, 0, tiles - 1), 0))
        for u in range(units)
    ]

    def rowed(columns):
        return pl.BlockSpec((tile, columns), lambda i, m: (i, 0))

    got = call(
        functools.partial(_expert_kernel, units),
        meta,
        (*xs, *cs, router, ids, w),
        [_shape((rows, width))] * (2 * units)
        + [_shape((total_rows, width))] * 2
        + [_shape((total_rows, hidden))] * 3
        + [_shape((total_rows, 1), jnp.float32)],
        [pltpu.VMEM((width, hidden), jnp.bfloat16)] * 3
        + [pltpu.VMEM((tile, width), jnp.bfloat16)] * 2,
        flops=12 * total_rows * width * hidden,
        in_specs=slabs
        + slabs
        + [_whole(router.shape), rowed(1), _whole(w.shape)],
        out_specs=slabs + slabs + [rowed(width)] * 2 + [rowed(hidden)] * 3 + [rowed(1)],
        grid=(units * tiles,),
    )
    return got[:units], got[units : 2 * units], got[2 * units :]


def layout(lengths_row, order_row, piece_len):
    all_slots = order_row.shape[0] * piece_len
    position = (
        order_row[:, None] * piece_len + jnp.arange(piece_len, dtype=jnp.int32)[None, :]
    ).reshape(all_slots)
    count = jnp.arange(lengths_row.shape[0], dtype=jnp.int32)
    seq_ends = jnp.sum(
        jnp.where(count[:, None] <= count[None, :], lengths_row[:, None], 0), axis=0, dtype=jnp.int32
    )
    segment = jnp.sum(
        (position[:, None] >= seq_ends[None, :]).astype(jnp.int32), axis=1, dtype=jnp.int32
    )
    seq_start = jnp.sum(
        jnp.where(segment[:, None] > count[None, :], lengths_row[None, :], 0),
        axis=1,
        dtype=jnp.int32,
    )
    return (seq_ends, position - seq_start)


def angles(offset):
    freq_table = jnp.exp(
        jnp.arange(HD // 2, dtype=jnp.float32) * (-2.0 * math.log(10000.0) / HD)
    )
    theta = offset.astype(jnp.float32)[..., None] * freq_table
    cosine, sine = jnp.cos(theta), jnp.sin(theta)
    return (
        jnp.tile(cosine, (1, 256 // HD)),
        jnp.tile(jnp.concatenate([-sine, sine], axis=1), (1, 128 // HD)),
    )


def hidden_back(gate_pre, up_pre, grad_hidden):
    sigmoid_gate = jax.nn.sigmoid(gate_pre)
    grad_gate = grad_hidden * up_pre * sigmoid_gate * (1.0 + gate_pre * (1.0 - sigmoid_gate))
    grad_up = grad_hidden * gate_pre * sigmoid_gate
    return (grad_gate.astype(jnp.bfloat16), grad_up.astype(jnp.bfloat16))


def head_parts():
    return lax.axis_size("ctx") // HEAD_GROUPS


def exchange(values):
    return [values[0]] + [swap(values[k], "ctx", k * head_parts()) for k in range(1, 4)]


def attend_forward(meta, count, resid, gain, tables, w_in, early):
    keep, send, qkv = pre(meta, resid, gain, tables, w_in)
    qkv = exchange(qkv)
    inputs = list(qkv)
    for part in range(1, head_parts()):
        inputs += [swap(values, "ctx", part) for values in qkv]
    inputs, early = lax.optimization_barrier((inputs, early))
    heads, acc, lse = attend(meta, inputs, count)
    return heads, (keep, send, inputs, acc, lse), early


def near(*values):
    return [swap(v, "fsdp", 1) for v in values]


def add_arrived(grads):
    return grads[0] + swap(grads[1], "fsdp", 2)


def total(bucket, grads):
    count = lax.axis_size("ctx")
    ring = [[(i + bucket) % count for i in range(count)]]
    return lax.psum(tuple(grads), "ctx", axis_index_groups=ring)


def total_small(values):
    for axis in BOTH:
        step = 1
        while step < lax.axis_size(axis):
            values = values + swap(values, axis, step)
            step *= 2
    return values


def per_device(
    tokens,
    cotangent,
    lengths,
    piece_order,
    routes,
    attn_in,
    attn_out,
    norm_gain,
    mlp_in,
    mlp_out,
    router,
    expert_in,
    expert_out,
):
    tok_rows, model_width = tokens.shape[1:]
    shard_width = router.shape[0]
    num_experts = router.shape[1]
    own_ctx, own_fsdp = lax.axis_index("ctx"), lax.axis_index("fsdp")
    ctx_count, fsdp_count = lax.axis_size("ctx"), lax.axis_size("fsdp")
    units = ctx_count * fsdp_count // num_experts
    hid_unit = expert_out.shape[0] // fsdp_count
    members = [
        [i for i in range(ctx_count * fsdp_count) if i % units == lane] for lane in range(units)
    ]

    def dispatch(values):
        return lax.all_to_all(values, BOTH, 0, 0, tiled=True, axis_index_groups=members)

    def to_units(values):
        return [values] + [swap(values, BOTH, k) for k in range(1, units)]

    def from_units(partial):
        summed = partial[0].astype(jnp.float32)
        for k in range(1, units):
            summed = summed + swap(partial[k], BOTH, k).astype(jnp.float32)
        return summed

    def gathered(shard):
        return lax.all_gather(shard, "fsdp", axis=0, tiled=True)

    seq_ends, offset = layout(lengths[0], piece_order[0], tok_rows // 2)
    tables = angles(lax.dynamic_slice_in_dim(offset, own_ctx * tok_rows, tok_rows, 0))
    parts = ctx_count // HEAD_GROUPS
    line, side = own_ctx // parts, own_ctx % parts
    order = piece_order[0].reshape(HEAD_GROUPS, parts, 2)
    place = [order[line ^ k, side ^ part] for part in range(parts) for k in range(HEAD_GROUPS)]
    meta = jnp.concatenate([jnp.stack([own_fsdp, line]), jnp.concatenate(place), seq_ends])
    at_ctx = jnp.stack([own_ctx % 2, own_ctx // 2])
    count = lengths.shape[1]

    item_count = tok_rows * TOP
    capacity = 2 * item_count // num_experts
    slot_count = num_experts * capacity
    expert_ids = jnp.arange(num_experts, dtype=jnp.int32)
    chosen = routes[0][:, :, None] == expert_ids[None, None, :]
    flat_chosen = chosen.reshape(item_count, num_experts).astype(jnp.bfloat16)
    items = jnp.arange(item_count, dtype=jnp.int32)
    earlier = jnp.dot(
        (items[None, :] < items[:, None]).astype(jnp.bfloat16),
        flat_chosen,
        preferred_element_type=jnp.float32,
    )
    slot_rank = jnp.sum(earlier * flat_chosen.astype(jnp.float32), axis=1).astype(jnp.int32)
    slot_target = (routes[0].reshape(item_count) * capacity + slot_rank).reshape(tok_rows, TOP)
    slots = jnp.arange(slot_count, dtype=jnp.int32)
    at_slot = [slots[:, None] == slot_target[None, :, k] for k in range(TOP)]
    of_token = [(slots[None, :] == slot_target[:, k, None]).astype(jnp.bfloat16) for k in range(TOP)]
    fill = (at_slot[0] | at_slot[1]).astype(jnp.bfloat16)

    def to_slots(rows):
        return jnp.dot(fill, rows, preferred_element_type=jnp.float32).astype(jnp.bfloat16)

    def send_rows(rows):
        return dispatch(to_slots(rows).reshape(num_experts, capacity, model_width))

    other_ids = sum(
        jnp.sum(
            jnp.where(at_slot[k], routes[0][None, :, 1 - k].astype(jnp.float32), 0.0), axis=1
        )
        for k in range(TOP)
    )

    def with_notes(rows, *notes):
        extra = jnp.stack(notes, axis=1).astype(jnp.bfloat16)
        extra = jnp.pad(extra, ((0, 0), (0, 8 - len(notes)), (0, model_width - capacity)))
        return jnp.concatenate([rows, extra], axis=1)

    shard = attn_in[0]
    near_shard, far_shard = swap(shard, "fsdp", 1), swap(shard, "fsdp", 2)
    small = gather_shards(jnp.concatenate([norm_gain.reshape(4, shard_width), router.T], axis=0))
    ordered = []
    for i in range(4):
        block = small[3]
        for j in range(3):
            block = jnp.where(own_fsdp ^ j == i, small[j], block)
        ordered.append(block)
    small = jnp.concatenate(ordered, axis=1)
    gains = [small[i : i + 1].astype(jnp.float32) for i in range(4)]
    router_full = small[4:].T
    grad_rows = to_slots(cotangent[0]).reshape(num_experts, capacity, model_width)
    grad_sent = with_notes(grad_rows, other_ids.reshape(num_experts, capacity))
    stored = jnp.concatenate(
        [jnp.swapaxes(expert_in, 1, 2), jnp.swapaxes(expert_out, 0, 1)[None]]
    )
    expert_part = jnp.stack(
        [stored[:, :, f * hid_unit : (f + 1) * hid_unit] for f in range(fsdp_count)]
    )
    near_out, far_out = swap(attn_out[0], "fsdp", 1), swap(attn_out[0], "fsdp", 2)
    far_shard, tables, meta, gains, expert_part = lax.optimization_barrier(
        (far_shard, tables, meta, gains, expert_part)
    )
    w_attn_in_one = (shard, near_shard, far_shard, swap(far_shard, "fsdp", 1))
    own_out = attn_out[0]
    far_shard, far_out, attn_in, attn_out, mlp_in, mlp_out = lax.optimization_barrier(
        (far_shard, far_out, attn_in, attn_out, mlp_in, mlp_out)
    )
    w_attn_out_one = (own_out, near_out, far_out, swap(far_out, "fsdp", 1))
    w_mlp_in_one, w_mlp_out_one = gathered(mlp_in[0]), gathered(mlp_out[0])
    w_mlp_in_two, w_mlp_out_two = gathered(mlp_in[1]), gathered(mlp_out[1])

    resid_in = tokens[0].astype(jnp.float32)
    heads_one, kept_one, (grad_sent, attn_in, attn_out) = attend_forward(
        meta, count, resid_in, gains[0], tables, w_attn_in_one, (grad_sent, attn_in, attn_out)
    )
    far_in, far_out = swap(attn_in[1], "fsdp", 2), swap(attn_out[1], "fsdp", 2)
    grad_sent = dispatch(grad_sent)
    heads_one = exchange(heads_one)
    heads_one, far_in, far_out = lax.optimization_barrier((heads_one, far_in, far_out))
    w_attn_in_two, w_attn_out_two = [
        (own, swap(own, "fsdp", 1), far, swap(far, "fsdp", 1))
        for own, far in ((attn_in[1], far_in), (attn_out[1], far_out))
    ]
    after_one, _, blocks_one, keep_one, send_one, att_keep_one, att_send_one = post(
        meta, resid_in, gains[1], heads_one, w_attn_out_one
    )
    after_one, grad_sent, expert_part = lax.optimization_barrier(
        (after_one, grad_sent, expert_part)
    )
    expert_w = lax.all_to_all(expert_part, "fsdp", 0, 0, tiled=True)
    middle, mixed_one, hid_keep_one, hid_send_one = mlp(
        meta, after_one, blocks_one, w_mlp_in_one, w_mlp_out_one
    )
    near_one = near(send_one, att_send_one, hid_send_one)
    heads_two, kept_two, grad_sent = attend_forward(
        meta, count, middle, gains[2], tables, w_attn_in_two, grad_sent
    )
    grad_arrived = to_units(grad_sent[:, :capacity].reshape(slot_count, model_width))
    arrived_ids = jnp.concatenate(
        to_units(grad_sent[:, capacity, :capacity].astype(jnp.float32))
    ).reshape(-1, 1)
    heads_two, grad_arrived, arrived_ids = lax.optimization_barrier(
        (heads_two, grad_arrived, arrived_ids)
    )
    heads_two = exchange(heads_two)
    heads_two, w_attn_out_two, expert_w = lax.optimization_barrier(
        (heads_two, w_attn_out_two, expert_w)
    )
    after_two, normed_three, blocks_two, keep_two, send_two, att_keep_two, att_send_two = post(
        meta, middle, gains[3], heads_two, w_attn_out_two
    )

    rows_sent = send_rows(normed_three)
    shared, mixed_two, hid_keep_two, hid_send_two = mlp(
        meta, after_two, blocks_two, w_mlp_in_two, w_mlp_out_two
    )
    grad_mixed_two, grad_shared_in = mlp_back(
        meta, cotangent, mixed_two, w_mlp_in_two, w_mlp_out_two
    )
    grad_mlp_out_two = weight_grad(
        meta, hid_keep_two, *near(hid_send_two), cotangent, *near(cotangent)
    )
    logits = jnp.dot(normed_three, router_full, preferred_element_type=jnp.float32)
    picked = jnp.sum(jnp.where(chosen, logits[:, None, :], 0.0), axis=-1)
    gate_probs = jax.nn.softmax(picked, axis=-1)
    rows_sent, grad_shared_in, grad_mlp_out_two, gate_probs = lax.optimization_barrier(
        (rows_sent, grad_shared_in, grad_mlp_out_two, gate_probs)
    )
    sum_mlp_out_two = add_arrived(grad_mlp_out_two)
    router_wide = jnp.pad(router_full, ((0, 0), (0, 128 - num_experts)))
    own_expert = ((own_ctx * fsdp_count + own_fsdp) // units).reshape(1)
    partial_rows, partial_back, kept_rows = experts(
        own_expert,
        to_units(rows_sent.reshape(slot_count, model_width)),
        grad_arrived,
        router_wide,
        arrived_ids,
        expert_w,
    )
    arrived, grad_rows, hidden_rows, grad_gate, grad_up, dots = kept_rows
    dots = from_units(dots.reshape(units, num_experts, capacity))
    coarse = lax.optimization_barrier(dots.astype(jnp.bfloat16))
    payload = with_notes(
        from_units(partial_back).astype(jnp.bfloat16).reshape(num_experts, capacity, model_width),
        coarse,
        dots - coarse.astype(jnp.float32),
    )
    payload, kept_rows, partial_rows = lax.optimization_barrier((payload, kept_rows, partial_rows))
    arrived, grad_rows, hidden_rows, grad_gate, grad_up, _ = kept_rows
    back = dispatch(payload)
    grad_experts = jnp.stack(
        [
            jnp.einsum("rd,rf->df", left, right, preferred_element_type=jnp.float32)
            .astype(jnp.bfloat16)
            .reshape(fsdp_count, shard_width, hid_unit)
            for left, right in ((arrived, grad_gate), (arrived, grad_up), (grad_rows, hidden_rows))
        ],
        axis=1,
    )
    grad_mlp_in_two = weight_grad(
        meta, keep_two, *near(send_two), grad_mixed_two, *near(grad_mixed_two)
    )
    back, grad_experts, grad_mlp_in_two, sum_mlp_out_two = lax.optimization_barrier(
        (back, grad_experts, grad_mlp_in_two, sum_mlp_out_two)
    )
    grad_out = cotangent[0].astype(jnp.float32)
    stride = back.shape[1]
    notes = back[:, capacity : capacity + 2, :capacity].astype(jnp.float32)
    slot_dots = jnp.sum(notes, axis=1).reshape(1, slot_count)
    grad_gates = jnp.stack(
        [
            jnp.sum(
                jnp.where(slots[None, :] == slot_target[:, k, None], slot_dots, 0.0), axis=-1
            )
            for k in range(TOP)
        ],
        axis=1,
    )
    grad_picked = gate_probs * (
        grad_gates - jnp.sum(gate_probs * grad_gates, axis=-1, keepdims=True)
    )
    grad_logits = jnp.sum(jnp.where(chosen, grad_picked[..., None], 0.0), axis=1)
    grad_router = jnp.einsum(
        "te,td->ed", grad_logits, normed_three.astype(jnp.float32), precision=HIGHEST
    )
    wide = jnp.arange(num_experts * stride, dtype=jnp.int32)[None, :]
    wide_target = slot_target + (stride - capacity) * routes[0]
    spread = (wide == wide_target[:, 0, None]) | (wide == wide_target[:, 1, None])
    grad_normed = (
        grad_shared_in
        + jnp.dot(
            spread.astype(jnp.bfloat16),
            back.reshape(num_experts * stride, model_width),
            preferred_element_type=jnp.float32,
        )
        + jnp.einsum(
            "te,de->td", grad_logits, router_full.astype(jnp.float32), precision=HIGHEST
        )
    )
    grad_heads, grad_resid, branch, gain_three = post_back(
        meta, after_two, gains[3], grad_out, grad_normed, w_attn_out_two
    )
    grad_heads = exchange(grad_heads)
    grad_attn_out_two = weight_grad(
        meta, att_keep_two, *near(att_send_two), branch, *near(branch)
    )
    sum_mlp_in_two = add_arrived(grad_mlp_in_two)
    grad_heads, grad_attn_out_two, grad_experts, sum_mlp_in_two, sum_mlp_out_two = (
        lax.optimization_barrier(
            (grad_heads, grad_attn_out_two, grad_experts, sum_mlp_in_two, sum_mlp_out_two)
        )
    )
    grad_experts = lax.all_to_all(grad_experts, "fsdp", 0, 0, tiled=True)
    grad_q, own, others = attend_back(
        meta, kept_two[2], grad_heads, kept_two[3], kept_two[4], count
    )
    arrived_kv = [swap(values, "ctx", part + 1) for part, values in enumerate(others)]
    sum_attn_out_two = add_arrived(grad_attn_out_two)
    grad_qkv = exchange(merge(meta, grad_q, own, arrived_kv))
    expert_rows = from_units(partial_rows).astype(jnp.bfloat16)
    sums_two = jnp.concatenate(
        [sum_mlp_in_two, sum_mlp_out_two.reshape(shard_width, -1)], axis=1
    ).reshape(ctx_count, shard_width // ctx_count, -1)
    grad_qkv, expert_rows, grad_experts, sums_two, sum_attn_out_two = lax.optimization_barrier(
        (grad_qkv, expert_rows, grad_experts, sums_two, sum_attn_out_two)
    )
    sums_two = lax.all_to_all(sums_two, "ctx", 0, 0, tiled=True)
    grad_mixed, grad_resid, gain_two = pre_back(
        meta, middle, gains[2], tables, grad_resid, grad_qkv, w_attn_in_two
    )
    near_qkv = near(kept_two[1], grad_mixed)
    branch = grad_resid.astype(jnp.bfloat16)[None]
    grad_mixed_one, grad_normed = mlp_back(
        meta, branch, mixed_one, w_mlp_in_one, w_mlp_out_one
    )
    grad_attn_in_two = weight_grad(meta, kept_two[0], near_qkv[0], grad_mixed, near_qkv[1])
    grad_normed, grad_attn_in_two = lax.optimization_barrier((grad_normed, grad_attn_in_two))
    near_mixed = [None] + near(branch, grad_mixed_one)
    grad_heads, grad_resid, att_branch, gain_one = post_back(
        meta, after_one, gains[1], grad_resid, grad_normed, w_attn_out_one
    )
    near_branch = near(att_branch)[0]
    grad_heads = exchange(grad_heads)
    grad_mlp_in_one = weight_grad(meta, keep_one, near_one[0], grad_mixed_one, near_mixed[2])
    first_sent = jnp.concatenate([grad_mlp_in_one[1], grad_attn_in_two[1]], axis=1)
    grad_heads, first_sent, expert_rows, sums_two = lax.optimization_barrier(
        (grad_heads, first_sent, expert_rows, sums_two)
    )
    sums_two = jnp.sum(sums_two.astype(jnp.float32), axis=0).astype(jnp.bfloat16)
    sums_two = lax.all_gather(sums_two, "ctx", axis=0, tiled=True)
    expert_rows = dispatch(expert_rows.reshape(num_experts, capacity, model_width))
    expert_rows = expert_rows.reshape(slot_count, model_width)
    first_arrived = swap(first_sent, "fsdp", 2)
    grad_q, own, others = attend_back(
        meta, kept_one[2], grad_heads, kept_one[3], kept_one[4], count
    )
    arrived_kv = [swap(values, "ctx", part + 1) for part, values in enumerate(others)]
    grad_mlp_out_one = weight_grad(meta, hid_keep_one, near_one[2], branch, near_mixed[1])
    grad_attn_out_one = weight_grad(meta, att_keep_one, near_one[1], att_branch, near_branch)
    second_sent = jnp.concatenate([grad_mlp_out_one[1], grad_attn_out_one[1]], axis=0)
    wide = grad_mlp_in_one[0].shape[1]
    first_sums = (
        grad_attn_in_two[0] + first_arrived[:, wide:],
        grad_mlp_in_one[0] + first_arrived[:, :wide],
    )
    arrived_kv, second_sent, first_sums = lax.optimization_barrier(
        (arrived_kv, second_sent, first_sums)
    )
    grad_qkv = exchange(merge(meta, grad_q, own, arrived_kv))
    second_arrived = swap(second_sent, "fsdp", 2)
    tall = grad_mlp_out_one[0].shape[0]
    sums_one = total(1, (*first_sums, sum_attn_out_two))
    grad_qkv, expert_rows, sums_two = lax.optimization_barrier((grad_qkv, expert_rows, sums_two))
    grad_mixed, grad_resid, gain_zero = pre_back(
        meta, resid_in, gains[0], tables, grad_resid, grad_qkv, w_attn_in_one
    )
    near_qkv = near(kept_one[1], grad_mixed)
    grad_attn_in_one = weight_grad(meta, kept_one[0], near_qkv[0], grad_mixed, near_qkv[1])
    grad_attn_in_one, expert_rows, grad_experts = lax.optimization_barrier(
        (grad_attn_in_one, expert_rows, grad_experts)
    )
    grad_experts = jnp.transpose(grad_experts, (1, 2, 0, 3)).astype(jnp.float32)
    grad_experts = grad_experts.reshape(3, shard_width, hid_unit * fsdp_count)
    back_rows = [jnp.dot(p, expert_rows, preferred_element_type=jnp.float32) for p in of_token]
    output = shared + sum(gate_probs[:, k, None] * back_rows[k] for k in range(TOP))
    small_grads = jnp.concatenate([gain_zero, gain_one, gain_two, gain_three, grad_router])
    wide = sums_one[1].shape[1]
    (attn_grad, mlp_out_grad), sums_one, small_grads = reduce_last(
        at_ctx,
        [
            tuple(
                jnp.concatenate(pair, axis=1)
                for pair in (
                    (grad_attn_in_one[0], grad_attn_out_one[0]),
                    (swap(grad_attn_in_one[1], "fsdp", 2), second_arrived[tall:]),
                    (sums_one[0], sums_one[2]),
                )
            ),
            (
                grad_mlp_out_one[0],
                second_arrived[:tall],
                sums_two[:, wide:].reshape(tall, model_width),
            ),
        ],
        sums_one,
        small_grads,
    )
    small_grads = lax.dynamic_slice_in_dim(small_grads, own_fsdp * shard_width, shard_width, 1)
    attn_in_grad, attn_out_grad = attn_grad[:, :, :-model_width], attn_grad[:, :, -model_width:]
    mlp_in_grad = jnp.stack([sums_one[1], sums_two[:, :wide]]).astype(jnp.float32)
    return (
        output[None],
        grad_resid[None],
        attn_in_grad,
        attn_out_grad,
        small_grads[:4].reshape(2, 2, shard_width),
        mlp_in_grad,
        mlp_out_grad,
        small_grads[4:].T,
        jnp.swapaxes(grad_experts[:2], 1, 2),
        grad_experts[2].T,
    )


def solution(mesh):
    placed = (
        P("fsdp", "ctx", None),
        P("fsdp", "ctx", None),
        P("fsdp", None),
        P("fsdp", None),
        P("fsdp", "ctx", None),
        P(None, "fsdp", None),
        P(None, "fsdp", None),
        P(None, None, "fsdp"),
        P(None, "fsdp", None),
        P(None, "fsdp", None),
        P("fsdp", None),
        P(None, "ctx", "fsdp"),
        P("ctx", "fsdp"),
    )
    return jax.shard_map(
        per_device,
        mesh=mesh,
        in_specs=placed,
        out_specs=(
            P("fsdp", "ctx", None),
            P("fsdp", "ctx", None),
            P(None, "fsdp", None),
            P(None, "fsdp", None),
            P(None, None, "fsdp"),
            P(None, "fsdp", None),
            P(None, "fsdp", None),
            P("fsdp", None),
            P(None, "ctx", "fsdp"),
            P("ctx", "fsdp"),
        ),
        check_vma=False,
    )
```

```python
import functools
import math

import jax
import jax.numpy as jnp
from jax import lax
from jax.experimental import pallas as pl
from jax.experimental.pallas import tpu as pltpu
from jax.sharding import PartitionSpec as P

HEADS = 12
HD = 64
FF = 2048
TOP = 2
HEAD_GROUPS = 4
KEY_SPAN = 512
VMEM_LIMIT = 60 * 1024 * 1024


HIGHEST = lax.Precision.HIGHEST
EPSILON = 1e-06
NEGATIVE = -1e30


BOTH = ("ctx", "fsdp")


def swap(values, axis, mask):
    count = lax.axis_size(axis)
    return lax.ppermute(values, axis, [(i, i ^ mask) for i in range(count)])


def gather_shards(shard):
    near = swap(shard, "fsdp", 1)
    far = swap(shard, "fsdp", 2)
    return (shard, near, far, swap(far, "fsdp", 1))


def in_order(shards):
    own = lax.axis_index("fsdp")
    buffer = jnp.zeros((len(shards),) + shards[0].shape, shards[0].dtype)
    for k, shard in enumerate(shards):
        buffer = lax.dynamic_update_index_in_dim(buffer, shard, own ^ k, 0)
    return buffer


NT = (((1,), (1,)), ((), ()))


def _dot(a, b):
    return jnp.dot(a, b, preferred_element_type=jnp.float32)


def _dot_nt(a, b):
    return lax.dot_general(a, b, NT, preferred_element_type=jnp.float32)


def _flip(values):
    return values.astype(jnp.float32).T.astype(values.dtype)


def _shape(shape, dtype=jnp.bfloat16):
    return jax.ShapeDtypeStruct(shape, dtype)


def _whole(shape):
    return pl.BlockSpec(tuple(shape), lambda *_: (0,) * len(shape))


def operands(shards, part=None):
    if isinstance(shards, (tuple, list)):
        arrays, rows, place = shards, shards[0].shape[0], lambda m, k: 0
    else:
        arrays, rows, place = (shards,) * 4, shards.shape[0] // 4, lambda m, k: m[0] ^ k
    width = arrays[0].shape[1]
    if part is None:
        specs = [
            pl.BlockSpec((rows, width), lambda i, m, k=k: (place(m, k), 0)) for k in range(4)
        ]
    else:
        size, first = part
        specs = [
            pl.BlockSpec((rows, size), lambda i, m, k=k: (place(m, k), first + (m[0] ^ i)))
            for k in range(4)
        ]
    return list(arrays), specs


def call(body, meta, inputs, outputs, scratch=(), flops=0, in_specs=None, out_specs=None, grid=(1,)):
    moved = sum(math.prod(a.shape) * a.dtype.itemsize for a in (*inputs, *outputs))
    return pl.pallas_call(
        body,
        grid_spec=pltpu.PrefetchScalarGridSpec(
            num_scalar_prefetch=1,
            grid=grid,
            in_specs=in_specs or [_whole(a.shape) for a in inputs],
            out_specs=out_specs or [_whole(a.shape) for a in outputs],
            scratch_shapes=list(scratch),
        ),
        out_shape=list(outputs),
        compiler_params=pltpu.CompilerParams(vmem_limit_bytes=VMEM_LIMIT),
        cost_estimate=pl.CostEstimate(flops=flops, bytes_accessed=moved, transcendentals=0),
    )(meta, *inputs)


def _stack(refs, cols=slice(None)):
    return jnp.concatenate([w[:, cols] for w in refs], axis=0)


def _mine(blocks, own):
    return jnp.concatenate([blocks[own ^ k] for k in range(4)], axis=1)


def _norm(rows, gain):
    inverse = lax.rsqrt(jnp.mean(rows * rows, axis=-1, keepdims=True) + EPSILON)
    return rows * inverse * gain


def _norm_back(rows, gain, grad):
    inverse = lax.rsqrt(jnp.mean(rows * rows, axis=-1, keepdims=True) + EPSILON)
    weighted = grad * gain
    scaled = rows * inverse
    back = inverse * (weighted - scaled * jnp.mean(weighted * scaled, axis=-1, keepdims=True))
    return back, jnp.sum(grad * scaled, axis=0, keepdims=True)


def _split(rows, blocks):
    width = rows.shape[1] // len(blocks)
    for b, ref in enumerate(blocks):
        ref[...] = rows[:, b * width : (b + 1) * width]


def _turn(rows, cosine, sine, sign):
    lane = lax.broadcasted_iota(jnp.int32, cosine.shape, 1)
    low = lane % HD < HD // 2
    turned = []
    for b in range(rows.shape[1] // 128):
        part = rows[:, b * 128 : (b + 1) * 128]
        other = jnp.where(low, pltpu.roll(part, 128 - HD // 2, 1), pltpu.roll(part, HD // 2, 1))
        turned.append(part * cosine + sign * (other * sine))
    return jnp.concatenate(turned, axis=1)


def _pre_kernel(meta, x, gain, cosine, sine, w0, w1, w2, w3, keep, send, *rest):
    qkv, (blocks, heads) = rest[:4], rest[4:]
    own, line = meta[0], meta[1]
    width = x.shape[1]
    normed = _norm(x[...], gain[...]).astype(jnp.bfloat16)
    _split(normed, [blocks.at[b] for b in range(4)])
    for j in range(2):
        keep[j] = blocks[own ^ (2 * j)]
        send[j] = blocks[own ^ (2 * j + 1)]
    piece = x.shape[0] // 2
    mine = _mine(blocks, own)
    for kind in range(3):
        mixed = _dot(mine, _stack((w0, w1, w2, w3), slice(kind * width, (kind + 1) * width)))
        if kind < 2:
            mixed = _turn(mixed, cosine[...], sine[...], 1.0)
        if kind == 0:
            mixed = mixed * 0.125
        turned = mixed.T.astype(jnp.bfloat16)
        block = width // 4
        for b in range(4):
            for p in range(2):
                heads[b, p, kind] = turned[
                    b * block : (b + 1) * block, p * piece : (p + 1) * piece
                ]
    for k in range(4):
        qkv[k][...] = heads[line ^ k]


def pre(meta, x, gain, tables, shards):
    rows, width = x.shape
    block = width // 4
    outs = [_shape((2, rows, block))] * 2 + [_shape((2, 3, block, rows // 2))] * 4
    shards, specs = operands(shards)
    inputs = (x, gain, *tables)
    got = call(
        _pre_kernel,
        meta,
        (*inputs, *shards),
        outs,
        [
            pltpu.VMEM((4, rows, block), jnp.bfloat16),
            pltpu.VMEM((4, 2, 3, block, rows // 2), jnp.bfloat16),
        ],
        flops=6 * rows * width * width,
        in_specs=[_whole(a.shape) for a in inputs] + specs,
    )
    return got[0], got[1], got[2:6]


def _pre_back_kernel(meta, x, gain, cosine, sine, resid, *rest):
    qkv, w = rest[:4], rest[4:8]
    mixed_out, resid_out, gain_out, heads, blocks = rest[8:]
    own, line = meta[0], meta[1]
    width = x.shape[1]
    for k in range(4):
        heads[line ^ k] = qkv[k][...]
    for kind in range(3):
        mixed = jnp.concatenate(
            [
                jnp.concatenate([heads[b, p, kind] for b in range(4)], axis=0)
                for p in range(2)
            ],
            axis=1,
        )
        mixed = mixed.astype(jnp.float32).T
        if kind < 2:
            mixed = mixed * (0.125 if kind == 0 else 1.0)
            mixed = _turn(mixed, cosine[...], sine[...], -1.0)
        mixed_out[0, :, kind * width : (kind + 1) * width] = mixed.astype(jnp.bfloat16)
    grads = _dot_nt(mixed_out[0], _stack(w))
    _split(grads, [blocks.at[own ^ k] for k in range(4)])
    grad = jnp.concatenate([blocks[b] for b in range(4)], axis=1)
    back, grad_gain = _norm_back(x[...], gain[...], grad)
    resid_out[...] = resid[...] + back
    gain_out[...] = grad_gain


def pre_back(meta, x, gain, tables, resid, qkv, shards):
    rows, width = x.shape
    shards, specs = operands(shards)
    inputs = (x, gain, *tables, resid, *qkv)
    return call(
        _pre_back_kernel,
        meta,
        (*inputs, *shards),
        [
            _shape((1, rows, 3 * width)),
            _shape((rows, width), jnp.float32),
            _shape((1, width), jnp.float32),
        ],
        [
            pltpu.VMEM((4, 2, 3, width // 4, rows // 2), jnp.bfloat16),
            pltpu.VMEM((4, rows, width // 4), jnp.float32),
        ],
        flops=6 * rows * width * width,
        in_specs=[_whole(a.shape) for a in inputs] + specs,
    )


def _post_kernel(meta, x, gain, o0, o1, o2, o3, w0, w1, w2, w3, *rest):
    after, plain, blocks_out, keep, send, att_keep, att_send, att = rest
    own, line = meta[0], meta[1]
    piece = x.shape[0] // 2
    for k, o in enumerate((o0, o1, o2, o3)):
        for p in range(2):
            att[line ^ k, p * piece : (p + 1) * piece, :] = _flip(o[p])
    for j in range(2):
        att_keep[j] = att[own ^ (2 * j)]
        att_send[j] = att[own ^ (2 * j + 1)]
    rows = x[...] + _dot(_mine(att, own), _stack((w0, w1, w2, w3)))
    after[...] = rows
    normed = _norm(rows, gain[...]).astype(jnp.bfloat16)
    plain[...] = normed
    _split(normed, [att.at[b] for b in range(4)])
    blocks_out[...] = att[...]
    for j in range(2):
        keep[j] = att[own ^ (2 * j)]
        send[j] = att[own ^ (2 * j + 1)]


def post(meta, x, gain, heads, shards):
    rows, width = x.shape
    block = width // 4
    shards, specs = operands(shards)
    inputs = (x, gain, *heads)
    return call(
        _post_kernel,
        meta,
        (*inputs, *shards),
        [_shape((rows, width), jnp.float32), _shape((rows, width)), _shape((4, rows, block))]
        + [_shape((2, rows, block))] * 4,
        [pltpu.VMEM((4, rows, block), jnp.bfloat16)],
        flops=2 * rows * width * width,
        in_specs=[_whole(a.shape) for a in inputs] + specs,
    )


def _post_back_kernel(meta, x, gain, resid, grad, w0, w1, w2, w3, *rest):
    heads, (resid_out, branch, gain_out, att) = rest[:4], rest[4:]
    own, line = meta[0], meta[1]
    back, grad_gain = _norm_back(x[...], gain[...], grad[...])
    gain_out[...] = grad_gain
    rows = resid[...] + back
    resid_out[...] = rows
    rows = rows.astype(jnp.bfloat16)
    branch[0] = rows
    grads = _dot_nt(rows, _stack((w0, w1, w2, w3))).astype(jnp.bfloat16)
    _split(grads, [att.at[own ^ k] for k in range(4)])
    piece = x.shape[0] // 2
    for k in range(4):
        for p in range(2):
            heads[k][p] = _flip(att[line ^ k, p * piece : (p + 1) * piece, :])


def post_back(meta, x, gain, resid, grad, shards):
    rows, width = x.shape
    block = width // 4
    shards, specs = operands(shards)
    inputs = (x, gain, resid, grad)
    got = call(
        _post_back_kernel,
        meta,
        (*inputs, *shards),
        [_shape((2, block, rows // 2))] * 4
        + [
            _shape((rows, width), jnp.float32),
            _shape((1, rows, width)),
            _shape((1, width), jnp.float32),
        ],
        [pltpu.VMEM((4, rows, block), jnp.bfloat16)],
        flops=2 * rows * width * width,
        in_specs=[_whole(a.shape) for a in inputs] + specs,
    )
    return got[:4], got[4], got[5], got[6]


def _mlp_kernel(meta, x, blocks, *rest):
    gates, ups, downs = rest[:4], rest[4:8], rest[8:12]
    out, mixed, keep, send, acc = rest[12:]
    own, step = meta[0], pl.program_id(0)
    rows = _mine(blocks, own)
    gate = _dot(rows, _stack(gates))
    up = _dot(rows, _stack(ups))
    mixed[0], mixed[1] = gate, up
    hidden = (gate * jax.nn.sigmoid(gate) * up).astype(jnp.bfloat16)
    for k in range(4):

        @pl.when(step == k)
        def _(k=k):
            (send if k % 2 else keep)[k // 2] = hidden
            part = _dot(hidden, downs[k][...])
            if k == 0:
                acc[...] = x[...] + part
            elif k < 3:
                acc[...] += part
            else:
                out[...] = acc[...] + part


def mlp_width(shards):
    first = shards[0] if isinstance(shards, (tuple, list)) else shards
    return first.shape[1] // 2


def mlp(meta, x, blocks, shards_in, shards_out):
    rows, width = x.shape
    hidden = mlp_width(shards_in)
    part = hidden // 4
    gates, gate_specs = operands(shards_in, (part, 0))
    ups, up_specs = operands(shards_in, (part, 4))
    downs, down_specs = operands(shards_out)
    return call(
        _mlp_kernel,
        meta,
        (x, blocks, *gates, *ups, *downs),
        [
            _shape((rows, width), jnp.float32),
            _shape((2, rows, hidden), jnp.float32),
            _shape((2, rows, part)),
            _shape((2, rows, part)),
        ],
        [pltpu.VMEM((rows, width), jnp.float32)],
        flops=6 * rows * width * hidden,
        in_specs=[_whole(x.shape), _whole(blocks.shape), *gate_specs, *up_specs, *down_specs],
        out_specs=[
            _whole((rows, width)),
            pl.BlockSpec((2, rows, part), lambda i, m: (0, 0, m[0] ^ i)),
            _whole((2, rows, part)),
            _whole((2, rows, part)),
        ],
        grid=(4,),
    )


def _mlp_back_kernel(meta, branch, mixed, *rest):
    gates, ups, downs = rest[:4], rest[4:8], rest[8:12]
    grad_mixed, grad_out, grad_hidden, acc, turned = rest[12:]
    own, step = meta[0], pl.program_id(0)
    for k in range(4):

        @pl.when(step == k)
        def _(k=k):
            grad_hidden[...] = _dot_nt(branch[0], downs[k][...]).astype(jnp.bfloat16)

    grad_h = grad_hidden[...].astype(jnp.float32)
    gate, up = mixed[0], mixed[1]
    sigmoid = jax.nn.sigmoid(gate)
    grad_gate = (grad_h * up * sigmoid * (1.0 + gate * (1.0 - sigmoid))).astype(jnp.bfloat16)
    grad_up = (grad_h * gate * sigmoid).astype(jnp.bfloat16)
    grad_mixed[0], grad_mixed[1] = grad_gate, grad_up
    part = _dot_nt(grad_gate, _stack(gates)) + _dot_nt(grad_up, _stack(ups))

    @pl.when(step == 0)
    def _():
        acc[...] = part

    @pl.when((step > 0) & (step < 3))
    def _():
        acc[...] += part

    @pl.when(step == 3)
    def _():
        _split(acc[...] + part, [turned.at[own ^ k] for k in range(4)])
        grad_out[...] = jnp.concatenate([turned[b] for b in range(4)], axis=1)


def mlp_back(meta, branch, mixed, shards_in, shards_out):
    _, rows, width = branch.shape
    hidden = mixed.shape[2]
    part = hidden // 4
    block = width // 4
    gates, gate_specs = operands(shards_in, (part, 0))
    ups, up_specs = operands(shards_in, (part, 4))
    downs, down_specs = operands(shards_out)
    return call(
        _mlp_back_kernel,
        meta,
        (branch, mixed, *gates, *ups, *downs),
        [_shape((2, rows, hidden)), _shape((rows, width), jnp.float32)],
        [
            pltpu.VMEM((rows, part), jnp.bfloat16),
            pltpu.VMEM((rows, width), jnp.float32),
            pltpu.VMEM((4, rows, block), jnp.float32),
        ],
        flops=6 * rows * width * hidden,
        in_specs=[
            _whole(branch.shape),
            pl.BlockSpec((2, rows, part), lambda i, m: (0, 0, m[0] ^ i)),
            *gate_specs,
            *up_specs,
            *down_specs,
        ],
        out_specs=[
            pl.BlockSpec((2, rows, part), lambda i, m: (0, 0, m[0] ^ i)),
            _whole((rows, width)),
        ],
        grid=(4,),
    )


def _grad_kernel(meta, left, left_near, right, right_near, own, send, flipped):
    rows, depth = left.shape[1:]

    @pl.when((pl.program_id(0) == 0) & (pl.program_id(1) == 0))
    def _():
        for j in range(2):
            flipped[j * depth : (j + 1) * depth, :rows] = _flip(left[j])
            flipped[j * depth : (j + 1) * depth, rows:] = _flip(left_near[j])

    both = jnp.concatenate([right[0], right_near[0]], axis=0)
    grads = _dot(flipped[...], both).astype(jnp.bfloat16)
    own[...] = grads[:depth]
    send[...] = grads[depth:]


def weight_grad(meta, left, left_near, right, right_near):
    groups, rows, width = right.shape
    depth = left.shape[2]
    chunk = 512 if width % 768 else 768
    steps = width // chunk
    right_spec = pl.BlockSpec((1, rows, chunk), lambda g, i, m: (g, 0, i))
    out_spec = pl.BlockSpec((depth, chunk), lambda g, i, m: (0, g * steps + i))
    return call(
        _grad_kernel,
        meta,
        (left, left_near, right, right_near),
        [_shape((depth, groups * width))] * 2,
        [pltpu.VMEM((2 * depth, 2 * rows), jnp.bfloat16)],
        flops=8 * rows * depth * groups * width,
        in_specs=[_whole(left.shape), _whole(left.shape), right_spec, right_spec],
        out_specs=[out_spec, out_spec],
        grid=(groups, steps),
    )


def _mask(first_key, keys, query_pos, query_start, copies):
    key_pos = first_key + lax.broadcasted_iota(jnp.int32, (keys, query_pos.shape[1]), 0)
    allowed = (key_pos <= query_pos) & (key_pos >= query_start)
    return jnp.concatenate([allowed] * copies, axis=1)


def _tables(meta, parts):
    return (lambda s: meta[2 + s], lambda k: meta[2 + 8 * parts + k])


def _query_geometry(place, ends, count, piece, key_span):
    query_pos = place * piece + lax.broadcasted_iota(jnp.int32, (1, piece), 1)
    query_start = jnp.zeros_like(query_pos)
    first = place * piece
    least = jnp.int32(0)
    for k in range(count):
        last = k == count - 1
        query_start = jnp.where(query_pos >= ends(k), query_pos if last else ends(k), query_start)
        least = jnp.where(first >= ends(k), first if last else ends(k), least)
    return (query_pos, query_start, least // key_span, (first + piece - 1) // key_span + 1)


def _stack_heads(rows, heads):
    head_dim = rows.shape[0] // heads
    head = lax.broadcasted_iota(jnp.int32, rows.shape, 0) // head_dim
    zero = jnp.zeros_like(rows)
    return jnp.concatenate([jnp.where(head == h, rows, zero) for h in range(heads)], axis=1)


def _own_heads(acc, heads, piece):
    head_dim = acc.shape[0] // heads
    return jnp.concatenate(
        [
            acc[h * head_dim : (h + 1) * head_dim, h * piece : (h + 1) * piece]
            for h in range(heads)
        ],
        axis=0,
    )


def _attend_kernel(heads, count, key_span, parts, meta, *refs):
    inputs, o, (keep, lse, keys, values_t) = (
        refs[: 4 * parts],
        refs[4 * parts : 4 * parts + 4],
        refs[4 * parts + 4 :],
    )
    width, piece = inputs[0].shape[2:]
    place, ends = _tables(meta, parts)
    for s in range(8 * parts):
        at = pl.ds(pl.multiple_of(place(s) * piece, piece), piece)
        keys[at, :] = _flip(inputs[s // 2][s % 2, 1])
        values_t[:, at] = inputs[s // 2][s % 2, 2]
    cols = heads * piece
    for s in range(8):
        query_pos, query_start, begin, end = _query_geometry(
            place(s), ends, count, piece, key_span
        )
        stacked = _stack_heads(inputs[s // 2][s % 2, 0], heads)

        def advance(block, carried):
            run_max, run_sum, acc = carried
            first = pl.multiple_of(block * key_span, key_span)
            scores = _dot(keys[pl.ds(first, key_span), :], stacked)
            allowed = _mask(first, key_span, query_pos, query_start, heads)
            scores = jnp.where(allowed, scores, NEGATIVE)
            new_max = jnp.maximum(run_max, jnp.max(scores, axis=0, keepdims=True))
            weights = jnp.exp(scores - new_max)
            factor = jnp.exp(run_max - new_max)
            run_sum = run_sum * factor + jnp.sum(weights, axis=0, keepdims=True)
            part = _dot(values_t[:, pl.ds(first, key_span)], weights.astype(jnp.bfloat16))
            return (new_max, run_sum, acc * factor + part)

        run_max, run_sum, acc = lax.fori_loop(
            begin,
            end,
            advance,
            (
                jnp.full((1, cols), NEGATIVE, jnp.float32),
                jnp.zeros((1, cols), jnp.float32),
                jnp.zeros((width, cols), jnp.float32),
            ),
        )
        kept = _own_heads(acc / run_sum, heads, piece)
        keep[s] = kept
        o[s // 2][s % 2] = kept.astype(jnp.bfloat16)
        lse[s] = run_max + jnp.log(run_sum)


def attend(meta, inputs, count):
    _, _, width, piece = inputs[0].shape
    heads = width // HD
    parts = len(inputs) // 4
    slots = parts * 8 * piece
    got = call(
        functools.partial(_attend_kernel, heads, count, KEY_SPAN, parts),
        meta,
        inputs,
        [_shape((2, width, piece))] * 4
        + [_shape((8, width, piece), jnp.float32), _shape((8, 1, heads * piece), jnp.float32)],
        [
            pltpu.VMEM((slots, width), jnp.bfloat16),
            pltpu.VMEM((width, slots), jnp.bfloat16),
        ],
        flops=32 * piece * slots * width,
    )
    return got[:4], got[4], got[5]


def _attend_back_kernel(heads, count, key_span, parts, meta, *refs):
    inputs, grads, (keep, lse), rest = (
        refs[: 4 * parts],
        refs[4 * parts : 4 * parts + 4],
        refs[4 * parts + 4 : 4 * parts + 6],
        refs[4 * parts + 6 :],
    )
    gq, gkv = rest[0], rest[1 : 1 + parts]
    keys, keys_t, values, gkeys, gvalues = rest[1 + parts :]
    width, piece = inputs[0].shape[2:]
    head_dim = width // heads
    place, ends = _tables(meta, parts)
    for s in range(8 * parts):
        at = pl.ds(pl.multiple_of(place(s) * piece, piece), piece)
        key_rows = inputs[s // 2][s % 2, 1]
        keys_t[:, at] = key_rows
        keys[at, :] = _flip(key_rows)
        values[at, :] = _flip(inputs[s // 2][s % 2, 2])
    gkeys[...] = jnp.zeros_like(gkeys)
    gvalues[...] = jnp.zeros_like(gvalues)
    for s in range(8):
        query_pos, query_start, begin, end = _query_geometry(
            place(s), ends, count, piece, key_span
        )
        stacked = _stack_heads(inputs[s // 2][s % 2, 0], heads)
        grad = grads[s // 2][s % 2]
        grad_stacked = _stack_heads(grad, heads)
        product = grad.astype(jnp.float32) * keep[s]
        delta = jnp.concatenate(
            [
                jnp.sum(product[h * head_dim : (h + 1) * head_dim, :], axis=0, keepdims=True)
                for h in range(heads)
            ],
            axis=1,
        )
        log_sum = lse[s]

        def retreat(block, acc):
            first = pl.multiple_of(block * key_span, key_span)
            at = pl.ds(first, key_span)
            scores = _dot(keys[at, :], stacked)
            allowed = _mask(first, key_span, query_pos, query_start, heads)
            probs = jnp.where(allowed, jnp.exp(scores - log_sum), 0.0)
            grad_probs = _dot(values[at, :], grad_stacked)
            grad_scores = (probs * (grad_probs - delta)).astype(jnp.bfloat16)
            gvalues[:, at] += _dot_nt(grad_stacked, probs.astype(jnp.bfloat16))
            gkeys[:, at] += _dot_nt(stacked, grad_scores)
            return acc + _dot(keys_t[:, at], grad_scores)

        acc = lax.fori_loop(begin, end, retreat, jnp.zeros((width, heads * piece), jnp.float32))
        gq[s] = _own_heads(acc, heads, piece).astype(jnp.bfloat16)
    for s in range(8 * parts):
        at = pl.ds(pl.multiple_of(place(s) * piece, piece), piece)
        out = gkv[s // 8]
        out[s % 8, 0] = gkeys[:, at].astype(out.dtype)
        out[s % 8, 1] = gvalues[:, at].astype(out.dtype)


def attend_back(meta, inputs, grads, keep, lse, count):
    _, _, width, piece = inputs[0].shape
    heads = width // HD
    parts = len(inputs) // 4
    slots = parts * 8 * piece
    got = call(
        functools.partial(_attend_back_kernel, heads, count, KEY_SPAN, parts),
        meta,
        (*inputs, *grads, keep, lse),
        [_shape((8, width, piece)), _shape((8, 2, width, piece), jnp.float32)]
        + [_shape((8, 2, width, piece))] * (parts - 1),
        [
            pltpu.VMEM((slots, width), jnp.bfloat16),
            pltpu.VMEM((width, slots), jnp.bfloat16),
            pltpu.VMEM((slots, width), jnp.bfloat16),
            pltpu.VMEM((width, slots), jnp.float32),
            pltpu.VMEM((width, slots), jnp.float32),
        ],
        flops=80 * piece * slots * width,
    )
    return got[0], got[1], got[2:]


def _merge_kernel(meta, gq, own, *rest):
    arrived, out = rest[:-4], rest[-4:]
    for s in range(8):
        total = own[s]
        for other in arrived:
            total = total + other[s].astype(jnp.float32)
        out[s // 2][s % 2, 0] = gq[s]
        out[s // 2][s % 2, 1:3] = total.astype(jnp.bfloat16)


def merge(meta, gq, own, arrived):
    _, width, piece = gq.shape
    return call(
        _merge_kernel, meta, (gq, own, *arrived), [_shape((2, 3, width, piece))] * 4
    )


def _halve_kernel(meta, first, second, sent, kept):
    summed = (first[...].astype(jnp.float32) + second[...].astype(jnp.float32)).astype(jnp.bfloat16)
    half = sent.shape[1]
    left, right = summed[:, :half], summed[:, half:]
    side = meta[0] == 0
    sent[...] = jnp.where(side, right, left)
    kept[...] = jnp.where(side, left, right)


def _quarter_kernel(meta, first, second, *rest):
    parts, summed = rest[:-1], rest[-1]
    summed[...] = (first[...].astype(jnp.float32) + second[...].astype(jnp.float32)).astype(
        jnp.bfloat16
    )
    chunk = parts[0].shape[0]
    for k, part in enumerate(parts):
        at = pl.multiple_of((meta[1] ^ k) * chunk, chunk)
        part[...] = summed[pl.ds(at, chunk), :]


def _place_kernel(meta, other, *refs):
    out, parts = refs[-1], refs[:-1]
    _, rows, width = out.shape
    lines = len(parts) // 2
    chunk, half = rows // lines, width // 2
    side = meta[0] == 0
    for k in range(lines):
        at = pl.multiple_of((meta[1] ^ k) * chunk, chunk)
        own = parts[k][...].astype(jnp.float32)
        near = parts[lines + k][...].astype(jnp.float32)
        out[0, pl.ds(at, chunk), :half] = jnp.where(side, own, near)
        out[0, pl.ds(at, chunk), half:] = jnp.where(side, near, own)
    out[1] = other[...].astype(jnp.float32)


def reduce_last(place, grads, held, small):
    lines = lax.axis_size("ctx") // 2
    if any(own.shape[0] // lines % 16 for own, _, _ in grads):
        outs = [
            jnp.stack([lax.psum(own + arrived, "ctx"), other]).astype(jnp.float32)
            for own, arrived, other in grads
        ]
        return outs, held, total_small(small)
    columns = []
    for i, (own, arrived, other) in enumerate(grads):
        rows, width = own.shape
        chunk, half = rows // lines, width // 2
        sent, kept = call(_halve_kernel, place, (own, arrived), [_shape((rows, half))] * 2)
        if i == 0:
            kept, small = lax.optimization_barrier((kept, small))
            small = total_small(small)
        parts = call(
            _quarter_kernel,
            place,
            (kept, swap(sent, "ctx", 1)),
            [_shape((chunk, half))] * lines,
            [pltpu.VMEM((rows, half), jnp.bfloat16)],
        )
        summed = parts[0].astype(jnp.float32)
        for k in range(1, lines):
            summed = summed + swap(parts[k], "ctx", 2 * k).astype(jnp.float32)
        summed = summed.astype(jnp.bfloat16)
        column = [swap(summed, "ctx", 2 * k) if k else summed for k in range(lines)]
        columns.append(column + [swap(c, "ctx", 1) for c in column])
    columns, held = lax.optimization_barrier((columns, held))
    outs = [
        call(
            _place_kernel,
            place,
            (other, *parts),
            [_shape((2, *own.shape), jnp.float32)],
        )[0]
        for (own, _, other), parts in zip(grads, columns)
    ]
    return outs, held, small


def _expert_kernel(units, meta, *refs):
    xs, cs = refs[:units], refs[units : 2 * units]
    router, ids, w = refs[2 * units : 2 * units + 3]
    outs = refs[2 * units + 3 :]
    parts, backs = outs[:units], outs[units : 2 * units]
    rows_out, grads_out, hidden_out, gate_out, up_out, dots_out = outs[2 * units : 2 * units + 6]
    gates, ups, downs, x, c = outs[2 * units + 6 :]
    step = pl.program_id(0)
    tiles = pl.num_programs(0) // units

    @pl.when(step == 0)
    def _():
        width = w.shape[2]
        for f in range(4):
            part = slice(f * width, (f + 1) * width)
            gates[part, :] = w[f, 0]
            ups[part, :] = w[f, 1]
            downs[part, :] = w[f, 2]

    for u in range(units):

        @pl.when(step // tiles == u)
        def _(u=u):
            x[...] = xs[u][...]
            c[...] = cs[u][...]

    rows = x[...]
    rows_out[...] = rows
    incoming = c[...].astype(jnp.float32)
    logits = _dot(rows, router[...])
    lane = lax.broadcasted_iota(jnp.int32, logits.shape, 1)
    gap = jnp.sum(
        jnp.where(lane == meta[0], logits, 0.0)
        - jnp.where(lane.astype(jnp.float32) == ids[...], logits, 0.0),
        axis=1,
        keepdims=True,
    )
    grads = (jax.nn.sigmoid(gap) * incoming).astype(jnp.bfloat16)
    grads_out[...] = grads
    gate = _dot(rows, gates[...])
    up = _dot(rows, ups[...])
    sigmoid = jax.nn.sigmoid(gate)
    silu = gate * sigmoid
    hidden = (silu * up).astype(jnp.bfloat16)
    hidden_out[...] = hidden
    part = _dot_nt(hidden, downs[...])
    dots_out[...] = jnp.sum(part * incoming, axis=1, keepdims=True)
    grad_h = _dot(grads, downs[...]).astype(jnp.bfloat16).astype(jnp.float32)
    grad_gate = (grad_h * up * sigmoid * (1.0 + gate * (1.0 - sigmoid))).astype(jnp.bfloat16)
    grad_up = (grad_h * silu).astype(jnp.bfloat16)
    gate_out[...] = grad_gate
    up_out[...] = grad_up
    back = _dot_nt(grad_gate, gates[...]) + _dot_nt(grad_up, ups[...])
    for u in range(units):

        @pl.when(step // tiles == u)
        def _(u=u):
            parts[u][...] = part.astype(jnp.bfloat16)
            backs[u][...] = back.astype(jnp.bfloat16)


def experts(meta, xs, cs, router, ids, w):
    units, (rows, width), tile = len(xs), xs[0].shape, 1024 // len(xs)
    tiles, hidden = rows // tile, w.shape[3]
    total_rows = units * rows
    slabs = [
        pl.BlockSpec((tile, width), lambda i, m, u=u: (jnp.clip(i - u * tiles, 0, tiles - 1), 0))
        for u in range(units)
    ]

    def rowed(columns):
        return pl.BlockSpec((tile, columns), lambda i, m: (i, 0))

    got = call(
        functools.partial(_expert_kernel, units),
        meta,
        (*xs, *cs, router, ids, w),
        [_shape((rows, width))] * (2 * units)
        + [_shape((total_rows, width))] * 2
        + [_shape((total_rows, hidden))] * 3
        + [_shape((total_rows, 1), jnp.float32)],
        [pltpu.VMEM((width, hidden), jnp.bfloat16)] * 3
        + [pltpu.VMEM((tile, width), jnp.bfloat16)] * 2,
        flops=12 * total_rows * width * hidden,
        in_specs=slabs
        + slabs
        + [_whole(router.shape), rowed(1), _whole(w.shape)],
        out_specs=slabs + slabs + [rowed(width)] * 2 + [rowed(hidden)] * 3 + [rowed(1)],
        grid=(units * tiles,),
    )
    return got[:units], got[units : 2 * units], got[2 * units :]


def layout(lengths_row, order_row, piece_len):
    all_slots = order_row.shape[0] * piece_len
    position = (
        order_row[:, None] * piece_len + jnp.arange(piece_len, dtype=jnp.int32)[None, :]
    ).reshape(all_slots)
    count = jnp.arange(lengths_row.shape[0], dtype=jnp.int32)
    seq_ends = jnp.sum(
        jnp.where(count[:, None] <= count[None, :], lengths_row[:, None], 0), axis=0, dtype=jnp.int32
    )
    segment = jnp.sum(
        (position[:, None] >= seq_ends[None, :]).astype(jnp.int32), axis=1, dtype=jnp.int32
    )
    seq_start = jnp.sum(
        jnp.where(segment[:, None] > count[None, :], lengths_row[None, :], 0),
        axis=1,
        dtype=jnp.int32,
    )
    return (seq_ends, position - seq_start)


def angles(offset):
    freq_table = jnp.exp(
        jnp.arange(HD // 2, dtype=jnp.float32) * (-2.0 * math.log(10000.0) / HD)
    )
    theta = offset.astype(jnp.float32)[..., None] * freq_table
    cosine, sine = jnp.cos(theta), jnp.sin(theta)
    return (
        jnp.tile(cosine, (1, 256 // HD)),
        jnp.tile(jnp.concatenate([-sine, sine], axis=1), (1, 128 // HD)),
    )


def hidden_back(gate_pre, up_pre, grad_hidden):
    sigmoid_gate = jax.nn.sigmoid(gate_pre)
    grad_gate = grad_hidden * up_pre * sigmoid_gate * (1.0 + gate_pre * (1.0 - sigmoid_gate))
    grad_up = grad_hidden * gate_pre * sigmoid_gate
    return (grad_gate.astype(jnp.bfloat16), grad_up.astype(jnp.bfloat16))


def head_parts():
    return lax.axis_size("ctx") // HEAD_GROUPS


def exchange(values):
    return [values[0]] + [swap(values[k], "ctx", k * head_parts()) for k in range(1, 4)]


def attend_forward(meta, count, resid, gain, tables, w_in, early):
    keep, send, qkv = pre(meta, resid, gain, tables, w_in)
    qkv = exchange(qkv)
    inputs = list(qkv)
    for part in range(1, head_parts()):
        inputs += [swap(values, "ctx", part) for values in qkv]
    inputs, early = lax.optimization_barrier((inputs, early))
    heads, acc, lse = attend(meta, inputs, count)
    return heads, (keep, send, inputs, acc, lse), early


def near(*values):
    return [swap(v, "fsdp", 1) for v in values]


def add_arrived(grads):
    return grads[0] + swap(grads[1], "fsdp", 2)


def total(bucket, grads):
    count = lax.axis_size("ctx")
    ring = [[(i + bucket) % count for i in range(count)]]
    return lax.psum(tuple(grads), "ctx", axis_index_groups=ring)


def total_small(values):
    for axis in BOTH:
        step = 1
        while step < lax.axis_size(axis):
            values = values + swap(values, axis, step)
            step *= 2
    return values


def per_device(
    tokens,
    cotangent,
    lengths,
    piece_order,
    routes,
    attn_in,
    attn_out,
    norm_gain,
    mlp_in,
    mlp_out,
    router,
    expert_in,
    expert_out,
):
    tok_rows, model_width = tokens.shape[1:]
    shard_width = router.shape[0]
    num_experts = router.shape[1]
    own_ctx, own_fsdp = lax.axis_index("ctx"), lax.axis_index("fsdp")
    ctx_count, fsdp_count = lax.axis_size("ctx"), lax.axis_size("fsdp")
    units = ctx_count * fsdp_count // num_experts
    hid_unit = expert_out.shape[0] // fsdp_count
    members = [
        [i for i in range(ctx_count * fsdp_count) if i % units == lane] for lane in range(units)
    ]

    def dispatch(values):
        return lax.all_to_all(values, BOTH, 0, 0, tiled=True, axis_index_groups=members)

    def to_units(values):
        return [values] + [swap(values, BOTH, k) for k in range(1, units)]

    def from_units(partial):
        summed = partial[0].astype(jnp.float32)
        for k in range(1, units):
            summed = summed + swap(partial[k], BOTH, k).astype(jnp.float32)
        return summed

    def gathered(shard):
        return lax.all_gather(shard, "fsdp", axis=0, tiled=True)

    seq_ends, offset = layout(lengths[0], piece_order[0], tok_rows // 2)
    tables = angles(lax.dynamic_slice_in_dim(offset, own_ctx * tok_rows, tok_rows, 0))
    parts = ctx_count // HEAD_GROUPS
    line, side = own_ctx // parts, own_ctx % parts
    order = piece_order[0].reshape(HEAD_GROUPS, parts, 2)
    place = [order[line ^ k, side ^ part] for part in range(parts) for k in range(HEAD_GROUPS)]
    meta = jnp.concatenate([jnp.stack([own_fsdp, line]), jnp.concatenate(place), seq_ends])
    at_ctx = jnp.stack([own_ctx % 2, own_ctx // 2])
    count = lengths.shape[1]

    item_count = tok_rows * TOP
    capacity = 2 * item_count // num_experts
    slot_count = num_experts * capacity
    expert_ids = jnp.arange(num_experts, dtype=jnp.int32)
    chosen = routes[0][:, :, None] == expert_ids[None, None, :]
    flat_chosen = chosen.reshape(item_count, num_experts).astype(jnp.bfloat16)
    items = jnp.arange(item_count, dtype=jnp.int32)
    earlier = jnp.dot(
        (items[None, :] < items[:, None]).astype(jnp.bfloat16),
        flat_chosen,
        preferred_element_type=jnp.float32,
    )
    slot_rank = jnp.sum(earlier * flat_chosen.astype(jnp.float32), axis=1).astype(jnp.int32)
    slot_target = (routes[0].reshape(item_count) * capacity + slot_rank).reshape(tok_rows, TOP)
    slots = jnp.arange(slot_count, dtype=jnp.int32)
    at_slot = [slots[:, None] == slot_target[None, :, k] for k in range(TOP)]
    of_token = [(slots[None, :] == slot_target[:, k, None]).astype(jnp.bfloat16) for k in range(TOP)]
    fill = (at_slot[0] | at_slot[1]).astype(jnp.bfloat16)

    def to_slots(rows):
        return jnp.dot(fill, rows, preferred_element_type=jnp.float32).astype(jnp.bfloat16)

    def send_rows(rows):
        return dispatch(to_slots(rows).reshape(num_experts, capacity, model_width))

    other_ids = sum(
        jnp.sum(
            jnp.where(at_slot[k], routes[0][None, :, 1 - k].astype(jnp.float32), 0.0), axis=1
        )
        for k in range(TOP)
    )

    def with_notes(rows, *notes):
        extra = jnp.stack(notes, axis=1).astype(jnp.bfloat16)
        extra = jnp.pad(extra, ((0, 0), (0, 8 - len(notes)), (0, model_width - capacity)))
        return jnp.concatenate([rows, extra], axis=1)

    shard = attn_in[0]
    near_shard, far_shard = swap(shard, "fsdp", 1), swap(shard, "fsdp", 2)
    small = gather_shards(jnp.concatenate([norm_gain.reshape(4, shard_width), router.T], axis=0))
    ordered = []
    for i in range(4):
        block = small[3]
        for j in range(3):
            block = jnp.where(own_fsdp ^ j == i, small[j], block)
        ordered.append(block)
    small = jnp.concatenate(ordered, axis=1)
    gains = [small[i : i + 1].astype(jnp.float32) for i in range(4)]
    router_full = small[4:].T
    grad_rows = to_slots(cotangent[0]).reshape(num_experts, capacity, model_width)
    grad_sent = with_notes(grad_rows, other_ids.reshape(num_experts, capacity))
    stored = jnp.concatenate(
        [jnp.swapaxes(expert_in, 1, 2), jnp.swapaxes(expert_out, 0, 1)[None]]
    )
    expert_part = jnp.stack(
        [stored[:, :, f * hid_unit : (f + 1) * hid_unit] for f in range(fsdp_count)]
    )
    near_out, far_out = swap(attn_out[0], "fsdp", 1), swap(attn_out[0], "fsdp", 2)
    far_shard, tables, meta, gains, expert_part = lax.optimization_barrier(
        (far_shard, tables, meta, gains, expert_part)
    )
    w_attn_in_one = (shard, near_shard, far_shard, swap(far_shard, "fsdp", 1))
    own_out = attn_out[0]
    far_shard, far_out, attn_in, attn_out, mlp_in, mlp_out = lax.optimization_barrier(
        (far_shard, far_out, attn_in, attn_out, mlp_in, mlp_out)
    )
    w_attn_out_one = (own_out, near_out, far_out, swap(far_out, "fsdp", 1))
    w_mlp_in_one, w_mlp_out_one = gathered(mlp_in[0]), gathered(mlp_out[0])
    w_mlp_in_two, w_mlp_out_two = gathered(mlp_in[1]), gathered(mlp_out[1])

    resid_in = tokens[0].astype(jnp.float32)
    heads_one, kept_one, (grad_sent, attn_in, attn_out) = attend_forward(
        meta, count, resid_in, gains[0], tables, w_attn_in_one, (grad_sent, attn_in, attn_out)
    )
    far_in, far_out = swap(attn_in[1], "fsdp", 2), swap(attn_out[1], "fsdp", 2)
    grad_sent = dispatch(grad_sent)
    heads_one = exchange(heads_one)
    after_one, _, blocks_one, keep_one, send_one, att_keep_one, att_send_one = post(
        meta, resid_in, gains[1], heads_one, w_attn_out_one
    )
    after_one, grad_sent, expert_part = lax.optimization_barrier(
        (after_one, grad_sent, expert_part)
    )
    expert_w = lax.all_to_all(expert_part, "fsdp", 0, 0, tiled=True)
    middle, mixed_one, hid_keep_one, hid_send_one = mlp(
        meta, after_one, blocks_one, w_mlp_in_one, w_mlp_out_one
    )
    middle, far_in, far_out = lax.optimization_barrier((middle, far_in, far_out))
    w_attn_in_two, w_attn_out_two = [
        (own, swap(own, "fsdp", 1), far, swap(far, "fsdp", 1))
        for own, far in ((attn_in[1], far_in), (attn_out[1], far_out))
    ]
    near_one = near(send_one, att_send_one, hid_send_one)
    heads_two, kept_two, grad_sent = attend_forward(
        meta, count, middle, gains[2], tables, w_attn_in_two, grad_sent
    )
    grad_arrived = to_units(grad_sent[:, :capacity].reshape(slot_count, model_width))
    arrived_ids = jnp.concatenate(
        to_units(grad_sent[:, capacity, :capacity].astype(jnp.float32))
    ).reshape(-1, 1)
    heads_two, grad_arrived, arrived_ids = lax.optimization_barrier(
        (heads_two, grad_arrived, arrived_ids)
    )
    heads_two = exchange(heads_two)
    heads_two, w_attn_out_two, expert_w = lax.optimization_barrier(
        (heads_two, w_attn_out_two, expert_w)
    )
    after_two, normed_three, blocks_two, keep_two, send_two, att_keep_two, att_send_two = post(
        meta, middle, gains[3], heads_two, w_attn_out_two
    )

    rows_sent = send_rows(normed_three)
    shared, mixed_two, hid_keep_two, hid_send_two = mlp(
        meta, after_two, blocks_two, w_mlp_in_two, w_mlp_out_two
    )
    grad_mixed_two, grad_shared_in = mlp_back(
        meta, cotangent, mixed_two, w_mlp_in_two, w_mlp_out_two
    )
    grad_mlp_out_two = weight_grad(
        meta, hid_keep_two, *near(hid_send_two), cotangent, *near(cotangent)
    )
    logits = jnp.dot(normed_three, router_full, preferred_element_type=jnp.float32)
    picked = jnp.sum(jnp.where(chosen, logits[:, None, :], 0.0), axis=-1)
    gate_probs = jax.nn.softmax(picked, axis=-1)
    rows_sent, grad_shared_in, grad_mlp_out_two, gate_probs = lax.optimization_barrier(
        (rows_sent, grad_shared_in, grad_mlp_out_two, gate_probs)
    )
    sum_mlp_out_two = add_arrived(grad_mlp_out_two)
    router_wide = jnp.pad(router_full, ((0, 0), (0, 128 - num_experts)))
    own_expert = ((own_ctx * fsdp_count + own_fsdp) // units).reshape(1)
    partial_rows, partial_back, kept_rows = experts(
        own_expert,
        to_units(rows_sent.reshape(slot_count, model_width)),
        grad_arrived,
        router_wide,
        arrived_ids,
        expert_w,
    )
    arrived, grad_rows, hidden_rows, grad_gate, grad_up, dots = kept_rows
    dots = from_units(dots.reshape(units, num_experts, capacity))
    coarse = lax.optimization_barrier(dots.astype(jnp.bfloat16))
    payload = with_notes(
        from_units(partial_back).astype(jnp.bfloat16).reshape(num_experts, capacity, model_width),
        coarse,
        dots - coarse.astype(jnp.float32),
    )
    payload, kept_rows, partial_rows = lax.optimization_barrier((payload, kept_rows, partial_rows))
    arrived, grad_rows, hidden_rows, grad_gate, grad_up, _ = kept_rows
    back = dispatch(payload)
    grad_experts = jnp.stack(
        [
            jnp.einsum("rd,rf->df", left, right, preferred_element_type=jnp.float32)
            .astype(jnp.bfloat16)
            .reshape(fsdp_count, shard_width, hid_unit)
            for left, right in ((arrived, grad_gate), (arrived, grad_up), (grad_rows, hidden_rows))
        ],
        axis=1,
    )
    grad_mlp_in_two = weight_grad(
        meta, keep_two, *near(send_two), grad_mixed_two, *near(grad_mixed_two)
    )
    back, grad_experts, grad_mlp_in_two, sum_mlp_out_two = lax.optimization_barrier(
        (back, grad_experts, grad_mlp_in_two, sum_mlp_out_two)
    )
    grad_out = cotangent[0].astype(jnp.float32)
    stride = back.shape[1]
    notes = back[:, capacity : capacity + 2, :capacity].astype(jnp.float32)
    slot_dots = jnp.sum(notes, axis=1).reshape(1, slot_count)
    grad_gates = jnp.stack(
        [
            jnp.sum(
                jnp.where(slots[None, :] == slot_target[:, k, None], slot_dots, 0.0), axis=-1
            )
            for k in range(TOP)
        ],
        axis=1,
    )
    grad_picked = gate_probs * (
        grad_gates - jnp.sum(gate_probs * grad_gates, axis=-1, keepdims=True)
    )
    grad_logits = jnp.sum(jnp.where(chosen, grad_picked[..., None], 0.0), axis=1)
    grad_router = jnp.einsum(
        "te,td->ed", grad_logits, normed_three.astype(jnp.float32), precision=HIGHEST
    )
    wide = jnp.arange(num_experts * stride, dtype=jnp.int32)[None, :]
    wide_target = slot_target + (stride - capacity) * routes[0]
    spread = (wide == wide_target[:, 0, None]) | (wide == wide_target[:, 1, None])
    grad_normed = (
        grad_shared_in
        + jnp.dot(
            spread.astype(jnp.bfloat16),
            back.reshape(num_experts * stride, model_width),
            preferred_element_type=jnp.float32,
        )
        + jnp.einsum(
            "te,de->td", grad_logits, router_full.astype(jnp.float32), precision=HIGHEST
        )
    )
    grad_heads, grad_resid, branch, gain_three = post_back(
        meta, after_two, gains[3], grad_out, grad_normed, w_attn_out_two
    )
    grad_heads = exchange(grad_heads)
    grad_attn_out_two = weight_grad(
        meta, att_keep_two, *near(att_send_two), branch, *near(branch)
    )
    sum_mlp_in_two = add_arrived(grad_mlp_in_two)
    grad_heads, grad_attn_out_two, grad_experts, sum_mlp_in_two, sum_mlp_out_two = (
        lax.optimization_barrier(
            (grad_heads, grad_attn_out_two, grad_experts, sum_mlp_in_two, sum_mlp_out_two)
        )
    )
    grad_experts = lax.all_to_all(grad_experts, "fsdp", 0, 0, tiled=True)
    grad_q, own, others = attend_back(
        meta, kept_two[2], grad_heads, kept_two[3], kept_two[4], count
    )
    arrived_kv = [swap(values, "ctx", part + 1) for part, values in enumerate(others)]
    sum_attn_out_two = add_arrived(grad_attn_out_two)
    grad_qkv = exchange(merge(meta, grad_q, own, arrived_kv))
    expert_rows = from_units(partial_rows).astype(jnp.bfloat16)
    sums_two = jnp.concatenate(
        [sum_mlp_in_two, sum_mlp_out_two.reshape(shard_width, -1)], axis=1
    ).reshape(ctx_count, shard_width // ctx_count, -1)
    grad_qkv, expert_rows, grad_experts, sums_two, sum_attn_out_two = lax.optimization_barrier(
        (grad_qkv, expert_rows, grad_experts, sums_two, sum_attn_out_two)
    )
    sums_two = lax.all_to_all(sums_two, "ctx", 0, 0, tiled=True)
    grad_mixed, grad_resid, gain_two = pre_back(
        meta, middle, gains[2], tables, grad_resid, grad_qkv, w_attn_in_two
    )
    near_qkv = near(kept_two[1], grad_mixed)
    branch = grad_resid.astype(jnp.bfloat16)[None]
    grad_mixed_one, grad_normed = mlp_back(
        meta, branch, mixed_one, w_mlp_in_one, w_mlp_out_one
    )
    grad_attn_in_two = weight_grad(meta, kept_two[0], near_qkv[0], grad_mixed, near_qkv[1])
    grad_normed, grad_attn_in_two = lax.optimization_barrier((grad_normed, grad_attn_in_two))
    near_mixed = [None] + near(branch, grad_mixed_one)
    grad_heads, grad_resid, att_branch, gain_one = post_back(
        meta, after_one, gains[1], grad_resid, grad_normed, w_attn_out_one
    )
    near_branch = near(att_branch)[0]
    grad_heads = exchange(grad_heads)
    grad_mlp_in_one = weight_grad(meta, keep_one, near_one[0], grad_mixed_one, near_mixed[2])
    first_sent = jnp.concatenate([grad_mlp_in_one[1], grad_attn_in_two[1]], axis=1)
    grad_heads, first_sent, expert_rows, sums_two = lax.optimization_barrier(
        (grad_heads, first_sent, expert_rows, sums_two)
    )
    sums_two = jnp.sum(sums_two.astype(jnp.float32), axis=0).astype(jnp.bfloat16)
    sums_two = lax.all_gather(sums_two, "ctx", axis=0, tiled=True)
    expert_rows = dispatch(expert_rows.reshape(num_experts, capacity, model_width))
    expert_rows = expert_rows.reshape(slot_count, model_width)
    first_arrived = swap(first_sent, "fsdp", 2)
    grad_q, own, others = attend_back(
        meta, kept_one[2], grad_heads, kept_one[3], kept_one[4], count
    )
    arrived_kv = [swap(values, "ctx", part + 1) for part, values in enumerate(others)]
    grad_mlp_out_one = weight_grad(meta, hid_keep_one, near_one[2], branch, near_mixed[1])
    grad_attn_out_one = weight_grad(meta, att_keep_one, near_one[1], att_branch, near_branch)
    second_sent = jnp.concatenate([grad_mlp_out_one[1], grad_attn_out_one[1]], axis=0)
    wide = grad_mlp_in_one[0].shape[1]
    first_sums = (
        grad_attn_in_two[0] + first_arrived[:, wide:],
        grad_mlp_in_one[0] + first_arrived[:, :wide],
    )
    arrived_kv, second_sent, first_sums = lax.optimization_barrier(
        (arrived_kv, second_sent, first_sums)
    )
    grad_qkv = exchange(merge(meta, grad_q, own, arrived_kv))
    second_arrived = swap(second_sent, "fsdp", 2)
    tall = grad_mlp_out_one[0].shape[0]
    sums_one = [
        *first_sums,
        grad_attn_out_one[0] + second_arrived[tall:],
        sum_attn_out_two,
    ]
    grad_qkv, expert_rows, sums_two, *sums_one = lax.optimization_barrier(
        (grad_qkv, expert_rows, sums_two, *sums_one)
    )
    sums_one = total(1, sums_one)
    grad_mixed, grad_resid, gain_zero = pre_back(
        meta, resid_in, gains[0], tables, grad_resid, grad_qkv, w_attn_in_one
    )
    near_qkv = near(kept_one[1], grad_mixed)
    grad_attn_in_one = weight_grad(meta, kept_one[0], near_qkv[0], grad_mixed, near_qkv[1])
    grad_attn_in_one, expert_rows, grad_experts = lax.optimization_barrier(
        (grad_attn_in_one, expert_rows, grad_experts)
    )
    grad_experts = jnp.transpose(grad_experts, (1, 2, 0, 3)).astype(jnp.float32)
    grad_experts = grad_experts.reshape(3, shard_width, hid_unit * fsdp_count)
    back_rows = [jnp.dot(p, expert_rows, preferred_element_type=jnp.float32) for p in of_token]
    output = shared + sum(gate_probs[:, k, None] * back_rows[k] for k in range(TOP))
    small_grads = jnp.concatenate([gain_zero, gain_one, gain_two, gain_three, grad_router])
    wide = sums_one[1].shape[1]
    (attn_in_grad, mlp_out_grad), sums_one, small_grads = reduce_last(
        at_ctx,
        [
            (grad_attn_in_one[0], swap(grad_attn_in_one[1], "fsdp", 2), sums_one[0]),
            (
                grad_mlp_out_one[0],
                second_arrived[:tall],
                sums_two[:, wide:].reshape(tall, model_width),
            ),
        ],
        sums_one,
        small_grads,
    )
    small_grads = lax.dynamic_slice_in_dim(small_grads, own_fsdp * shard_width, shard_width, 1)
    attn_out_grad, mlp_in_grad = [
        jnp.stack(pair).astype(jnp.float32)
        for pair in ((sums_one[2], sums_one[3]), (sums_one[1], sums_two[:, :wide]))
    ]
    return (
        output[None],
        grad_resid[None],
        attn_in_grad,
        attn_out_grad,
        small_grads[:4].reshape(2, 2, shard_width),
        mlp_in_grad,
        mlp_out_grad,
        small_grads[4:].T,
        jnp.swapaxes(grad_experts[:2], 1, 2),
        grad_experts[2].T,
    )


def solution(mesh):
    placed = (
        P("fsdp", "ctx", None),
        P("fsdp", "ctx", None),
        P("fsdp", None),
        P("fsdp", None),
        P("fsdp", "ctx", None),
        P(None, "fsdp", None),
        P(None, "fsdp", None),
        P(None, None, "fsdp"),
        P(None, "fsdp", None),
        P(None, "fsdp", None),
        P("fsdp", None),
        P(None, "ctx", "fsdp"),
        P("ctx", "fsdp"),
    )
    return jax.shard_map(
        per_device,
        mesh=mesh,
        in_specs=placed,
        out_specs=(
            P("fsdp", "ctx", None),
            P("fsdp", "ctx", None),
            P(None, "fsdp", None),
            P(None, "fsdp", None),
            P(None, None, "fsdp"),
            P(None, "fsdp", None),
            P(None, "fsdp", None),
            P("fsdp", None),
            P(None, "ctx", "fsdp"),
            P("ctx", "fsdp"),
        ),
        check_vma=False,
    )
```
